32 devices in a mesh: fsdp: 4 (over y, core), dp: 2 (over x), seq: 4 (over z).
Axes of the slice: x: 2, y: 2, z: 4, core: 2. Of those that a mesh axis runs over, the one named last changes fastest.
Arguments:
- tokens: bfloat16 [8, 2560, 1024], P(('fsdp', 'dp'), 'seq'), may hold values from -6 to 6
- qkv_weight: bfloat16 [1024, 3072], P('fsdp'), may hold values from -0.1875 to 0.1875
- out_weight: bfloat16 [1024, 1024], P('fsdp'), may hold values from -0.1875 to 0.1875
- up_weight: bfloat16 [1024, 4096], P('fsdp'), may hold values from -0.1875 to 0.1875
- down_weight: bfloat16 [4096, 1024], P('fsdp'), may hold values from -0.09375 to 0.09375
- norm_gain: float32 [4, 1024], replicated, may hold values from 0.5 to 1.5
- norm_bias: float32 [4, 1024], replicated, may hold values from -1.75 to 1.75
- caption_len: int32 [8, 2], P(('fsdp', 'dp')), may hold values from 5 to 64, as said below
- item_start: int32 [8, 2], P(('fsdp', 'dp')), may hold values from 0 to 1531, as said below
- grad_out: bfloat16 [8, 2560, 1024], P(('fsdp', 'dp'), 'seq'), may hold values from -6 to 6
Outputs:
- block_out: bfloat16 [8, 2560, 1024], P(('fsdp', 'dp'), 'seq')
- grad_in: bfloat16 [8, 2560, 1024], P(('fsdp', 'dp'), 'seq')
- grad_qkv: float32 [1024, 3072], P('fsdp')
- grad_proj: float32 [1024, 1024], P('fsdp')
- grad_up: float32 [1024, 4096], P('fsdp')
- grad_down: float32 [4096, 1024], P('fsdp')
- grad_gain: float32 [4, 1024], replicated
- grad_bias: float32 [4, 1024], replicated
The draws below stay inside these ranges and needn't reach their ends.
Inputs may be any that keep to these rules, and one draw needn't show every extreme that they name: `caption_len`: caption tokens of each item; item j of a row covers positions item_start[j] to item_start[j] + caption_len[j] + 1023 of that row. `item_start`: item j of a row starts at or after j * 1280 and ends before (j + 1) * 1280; positions outside every item are padding.
All inputs are finite; a program needn't handle non-finite values.
Results may differ from the reference program's by a relative error of at most 0.018.
Values may be sent and summed in bfloat16 or wider, within the bound.
A program may use at most 192 MiB of HBM per device.

```python
import jax
import jax.numpy as jnp
from jax import lax

D = 1024
H = 16
HD = 64
FF = 4096
IMAGE = 1024
CAPMAX = 64
SLOT = 1280
ROW = 2560
ITEMS = 2
ROWS = 8


def item_layout(key):
    number = ROWS * ITEMS
    captions = jax.random.randint(jax.random.fold_in(key, 71), (number,), 5, CAPMAX + 1, dtype=jnp.int32)
    captions = captions.at[0].set(CAPMAX).at[number - 1].set(5)
    headroom = SLOT - IMAGE - captions
    gap_sizes = jax.random.randint(jax.random.fold_in(key, 72), (number,), 0, headroom + 1, dtype=jnp.int32)
    gap_sizes = gap_sizes.at[0].set(0).at[number - 1].set(headroom[number - 1])
    slot_index = jnp.tile(jnp.arange(ITEMS, dtype=jnp.int32), ROWS)
    starts = slot_index * SLOT + gap_sizes
    return (captions.reshape(ROWS, ITEMS), starts.reshape(ROWS, ITEMS))


def draw_caption_len(key, part):
    return item_layout(key)[0]


def draw_item_start(key, part):
    return item_layout(key)[1]


def level_of(rng, extent, shards, smallest, top_value):
    def one(position, blocks):
        steps = jax.random.uniform(jax.random.fold_in(jax.random.fold_in(rng, 6), position), (blocks,), jnp.float32, smallest / len(shards), top_value / len(shards))
        return jnp.repeat(jnp.exp(steps), extent[position] // blocks).reshape((-1,) + (1,) * (len(extent) - position - 1))

    level = one(*shards[0])
    for cut in shards[1:]:
        level = level * one(*cut)
    return level


def bell_draw(stream_key, extent, scale, bound, cuts=(), kind=jnp.bfloat16):
    values = jax.random.normal(stream_key, extent, jnp.float32) * scale
    if len(cuts) > 0:
        values = level_of(stream_key, extent, cuts, -0.22, 0.18) * values
    return jnp.clip(values, min=-bound, max=bound).astype(kind)


def setup_inputs(seed: int = 0) -> dict:
    arg_keys = jax.random.split(jax.random.key(seed), 11)
    tokens = bell_draw(arg_keys[0], (ROWS, ROW, D), 1.0, 6.0, ((0, 8), (1, 4)))
    qkv_weight = bell_draw(arg_keys[1], (D, 3 * D), D ** -0.5, 0.1875, ((0, 4),))
    out_weight = bell_draw(arg_keys[2], (D, D), D ** -0.5, 0.1875, ((0, 4),))
    up_weight = bell_draw(arg_keys[3], (D, FF), D ** -0.5, 0.1875, ((0, 4),))
    down_weight = bell_draw(arg_keys[4], (FF, D), FF ** -0.5, 0.09375, ((0, 4),))
    norm_gain = jnp.clip(1.0 + 0.1 * jax.random.normal(arg_keys[5], (4, D), jnp.float32), 0.5, 1.5)
    norm_bias = bell_draw(arg_keys[6], (4, D), 0.3, 1.75, (), jnp.float32)
    caption_len = draw_caption_len(jax.random.fold_in(arg_keys[10], 71), 0)
    item_start = draw_item_start(jax.random.fold_in(arg_keys[10], 71), 0)
    grad_out = bell_draw(arg_keys[9], (ROWS, ROW, D), 1.0, 6.0, ((0, 8), (1, 4)))
    return dict(tokens=tokens, qkv_weight=qkv_weight, out_weight=out_weight, up_weight=up_weight, down_weight=down_weight, norm_gain=norm_gain, norm_bias=norm_bias, caption_len=caption_len, item_start=item_start, grad_out=grad_out)


@jax.custom_vjp
def low(v):
    return lax.optimization_barrier(v.astype(jnp.bfloat16)).astype(jnp.float32)

@jax.custom_vjp
def low_back(v):
    return v

def low_keep(v):
    return (low(v), None)

def low_pass(kept, grad):
    return (grad,)

def back_keep(v):
    return (v, None)

def back_low(kept, grad):
    return (low(grad),)
low.defvjp(low_keep, low_pass)
low_back.defvjp(back_keep, back_low)

def layer_norm(values, gain_row, bias_row):
    middle = lax.optimization_barrier(jnp.mean(values, axis=-1, keepdims=True))
    centred = values - middle
    spread = lax.optimization_barrier(jnp.mean(centred * centred, axis=-1, keepdims=True))
    return centred * lax.rsqrt(spread + 1e-05) * gain_row + bias_row

def matmul(left, right):
    return jnp.dot(left, right, precision=lax.Precision.HIGHEST, preferred_element_type=jnp.float32)

def segment_ids(positions, captions, starts):
    finish = starts + captions + IMAGE
    inside = (positions[:, None] >= starts[None, :]) & (positions[:, None] < finish[None, :])
    labels = jnp.arange(1, captions.shape[0] + 1, dtype=jnp.int32)
    return lax.optimization_barrier(jnp.sum(jnp.where(inside, labels[None, :], 0), axis=-1))

def split_heads(matrix):
    return matrix.reshape(matrix.shape[0], H, HD).transpose(1, 0, 2)

def join_heads(stacked):
    return stacked.transpose(1, 0, 2).reshape(stacked.shape[1], H * HD)

def row_forward(inputs, qkv_weight, out_weight, up_weight, down_weight, norm_gain, norm_bias, allowed):
    model_width = inputs.shape[1]
    normed_one = low(layer_norm(inputs, norm_gain[0], norm_bias[0]))
    projected = matmul(normed_one, qkv_weight)
    queries = low(low_back(projected[:, :model_width]))
    key_rows = low(low_back(projected[:, model_width:2 * model_width]))
    value_rows = low(low_back(projected[:, 2 * model_width:]))

    def one_head(pieces):
        query_head, key_head, value_head = pieces
        raw_scores = low_back(jnp.dot(query_head / 32.0, key_head.T, precision=lax.Precision.HIGHEST))
        scaled = jnp.where(allowed, raw_scores / 8.0, -1e+30)
        row_max = lax.optimization_barrier(jnp.max(scaled, axis=-1, keepdims=True))
        weights = jnp.exp((scaled - row_max) * 32.0)
        attn_probs = low(weights / lax.optimization_barrier(jnp.sum(weights, axis=-1, keepdims=True)))
        return jnp.dot(attn_probs, value_head, precision=lax.Precision.HIGHEST)
    mixed_heads = lax.map(jax.checkpoint(one_head), (split_heads(queries), split_heads(key_rows), split_heads(value_rows)))
    attended = low(low_back(join_heads(mixed_heads)))
    branch = low_back(matmul(attended, out_weight))
    middle = inputs + layer_norm(branch, norm_gain[1], norm_bias[1])
    normed_two = low(layer_norm(middle, norm_gain[2], norm_bias[2]))
    hidden = low_back(matmul(normed_two, up_weight))
    activated = low(jax.nn.gelu(hidden, approximate=True))
    feed_out = low_back(matmul(activated, down_weight))
    return middle + layer_norm(feed_out, norm_gain[3], norm_bias[3])

def reference(tokens, qkv_weight, out_weight, up_weight, down_weight, norm_gain, norm_bias, caption_len, item_start, grad_out):
    matrices = (qkv_weight.astype(jnp.float32), out_weight.astype(jnp.float32), up_weight.astype(jnp.float32), down_weight.astype(jnp.float32))
    positions = jnp.arange(ROW, dtype=jnp.int32)

    def per_row(totals, row_data):
        row_tokens, row_grad, captions, starts = row_data
        segments = segment_ids(positions, captions, starts)
        allowed = (segments[:, None] == segments[None, :]) & (positions[None, :] <= positions[:, None])

        def forward_fn(inputs, first, second, third, fourth, gains, biases):
            return row_forward(inputs, first, second, third, fourth, gains, biases, allowed)
        row_out, pullback = jax.vjp(forward_fn, row_tokens.astype(jnp.float32), matrices[0], matrices[1], matrices[2], matrices[3], norm_gain, norm_bias)
        gradients = pullback(row_grad.astype(jnp.float32))
        totals = tuple((running + grad_part for running, grad_part in zip(totals, gradients[1:])))
        return (totals, (row_out.astype(jnp.bfloat16), gradients[0].astype(jnp.bfloat16)))
    starting = tuple((jnp.zeros_like(matrix) for matrix in matrices)) + (jnp.zeros_like(norm_gain), jnp.zeros_like(norm_bias))
    totals, (outputs, grad_inputs) = lax.scan(per_row, starting, (tokens, grad_out, caption_len, item_start))
    return (outputs, grad_inputs, totals[0], totals[1], totals[2], totals[3], totals[4], totals[5])
```

```python
import functools

import jax
import jax.numpy as jnp
from jax import lax
from jax.experimental import pallas as pl
from jax.experimental.pallas import tpu as pltpu
from jax.sharding import PartitionSpec as P

HD = 64
IMAGE = 1024
SLOT = 1280
BLK = 256
LOG2E = 1.4426950408889634
SCALE = LOG2E / 8.0
NEG = -1e30
F32 = jnp.float32
BF16 = jnp.bfloat16
VMEM_LIMIT = 60 * 1024 * 1024
GROUPS = 2


def nn(a, b):
    return lax.dot_general(a, b, (((1,), (0,)), ((), ())), preferred_element_type=F32)


def nt(a, b):
    return lax.dot_general(a, b, (((1,), (1,)), ((), ())), preferred_element_type=F32)


def tn(a, b):
    return lax.dot_general(a, b, (((0,), (0,)), ((), ())), preferred_element_type=F32)


def normalise(v):
    mean = jnp.mean(v, axis=-1, keepdims=True)
    centred = v - mean
    var = jnp.mean(centred * centred, axis=-1, keepdims=True)
    rstd = lax.rsqrt(var + 1e-05)
    return centred * rstd, rstd


def norm_back(g, hat, rstd, gain):
    gg = g * gain
    return rstd * (
        gg - jnp.mean(gg, axis=-1, keepdims=True) - hat * jnp.mean(gg * hat, axis=-1, keepdims=True)
    )


def call(body, grid, prefetch, in_specs, out_specs, out_shape, scratch=(), flops=0, moved=0):
    return pl.pallas_call(
        body,
        grid_spec=pltpu.PrefetchScalarGridSpec(
            num_scalar_prefetch=prefetch,
            grid=grid,
            in_specs=in_specs,
            out_specs=out_specs,
            scratch_shapes=list(scratch),
        ),
        out_shape=out_shape,
        compiler_params=pltpu.CompilerParams(vmem_limit_bytes=VMEM_LIMIT),
        cost_estimate=pl.CostEstimate(flops=int(flops), bytes_accessed=int(moved), transcendentals=0),
    )


def full(shape):
    zeros = (0,) * len(shape)
    return pl.BlockSpec(shape, lambda *_: zeros)


def hbm():
    return pl.BlockSpec(memory_space=pl.ANY)


def shape(dims, dtype):
    return jax.ShapeDtypeStruct(dims, dtype)


def project_body(info, pos, own, head, rest, gain, bias, *refs, pieces):
    parts = refs[:pieces]
    q, k, v, n_t, w, sems = refs[pieces:]
    step = pl.program_id(0)
    half = q.shape[1]

    def copies():
        return [
            pltpu.make_async_copy(
                parts[i], w.at[pl.ds(pl.multiple_of(pos[i], 16), parts[i].shape[0])], sems.at[i]
            )
            for i in range(pieces)
        ]

    @pl.when(step == 0)
    def _():
        for c in copies():
            c.start()

    def rows(x):
        hat, _ = normalise(x.astype(F32))
        return (hat * gain[...] + bias[...]).astype(BF16)

    def emit(normed):
        n_t[...] = normed.T
        out = nn(normed, w[...])
        q[...] = out[:, :half].astype(BF16)
        k[...] = out[:, half : 2 * half].astype(BF16)
        v[...] = out[:, 2 * half :].astype(BF16)

    @pl.when(step == 0)
    def _():
        normed = rows(own[...])
        for c in copies():
            c.wait()
        emit(normed)

    @pl.when(step == 1)
    def _():
        emit(rows(jnp.concatenate([head[...], rest[...]], axis=0)))


def project(info, pos, own, head, rest, gain, bias, parts):
    local, d = own.shape
    wide = parts[0].shape[1]
    half = wide // 3
    block = lambda i, info, pos: ((info[1] + i) % 2, 0)
    return call(
        functools.partial(project_body, pieces=len(parts)),
        (2,),
        2,
        [full(own.shape), full(head.shape), full(rest.shape), full((1, d)), full((1, d))]
        + [hbm()] * len(parts),
        [pl.BlockSpec((local, half), block)] * 3
        + [
            pl.BlockSpec((d, local), lambda i, info, pos: (0, (info[1] + i) % 2)),
            full((d, wide)),
        ],
        [shape((2 * local, half), BF16)] * 3 + [shape((d, 2 * local), BF16), shape((d, wide), BF16)],
        [pltpu.SemaphoreType.DMA((len(parts),))],
        flops=4 * local * d * wide,
        moved=16e6,
    )(info, pos, own, head, rest, gain, bias, *parts)


def pad_body(x, gain, bias, w, k, v, n_t):
    hat, _ = normalise(x[...].astype(F32))
    normed = (hat * gain[...] + bias[...]).astype(BF16)
    n_t[...] = normed.T
    half = k.shape[1]
    out = nn(normed, w[:, half:])
    k[...] = out[:, :half].astype(BF16)
    v[...] = out[:, half:].astype(BF16)


def pad_project(x, gain, bias, w):
    rows, d = x.shape
    half = w.shape[1] // 3
    return call(
        pad_body,
        (1,),
        0,
        [full(x.shape), full((1, d)), full((1, d)), full(w.shape)],
        [full((rows, half)), full((rows, half)), full((d, rows))],
        [shape((rows, half), BF16)] * 2 + [shape((d, rows), BF16)],
        flops=4 * rows * d * half,
        moved=5e6,
    )(x, gain, bias, w)


def attend_body(info, q, k, v, kp, vp, o, lse):
    start, stop, pad_a, pad_b = info[2], info[3], info[4], info[5]
    lane = lax.broadcasted_iota(jnp.int32, (1, 2 * HD), 1)
    row = lax.broadcasted_iota(jnp.int32, (BLK, 1), 0)
    col = lax.broadcasted_iota(jnp.int32, (1, BLK), 1)
    causal = col <= row
    pad_col = (col < pad_a) | (col >= pad_b)
    count = SLOT // BLK
    for i in range(count):
        n = (i + 1) * BLK
        qi = q[i * BLK : n, :]
        edge = i in (0, count - 1)
        pos_q = row + i * BLK
        in_q = (pos_q >= start) & (pos_q < stop)
        masks = []
        for j in range(i + 1):
            pos_k = col + j * BLK
            mask = None
            if edge:
                in_k = (pos_k >= start) & (pos_k < stop)
                mask = (in_q & in_k) | (~in_q & ~in_k)
            elif j == 0:
                mask = jnp.broadcast_to(pos_k >= start, (BLK, BLK))
            if j == i:
                mask = causal if mask is None else mask & causal
            masks.append(mask)
        outs = []
        for h in range(2):
            qh = jnp.where(lane // HD == h, qi, jnp.zeros_like(qi))
            blocks = []
            for j in range(i + 1):
                s = nt(qh, k[j * BLK : (j + 1) * BLK, :]) * SCALE
                if masks[j] is not None:
                    s = jnp.where(masks[j], s, NEG)
                blocks.append(s)
            if edge:
                s = nt(qh, kp[...]) * SCALE
                blocks.append(jnp.where(~in_q & pad_col, s, NEG))
            top = functools.reduce(jnp.maximum, blocks)
            top = jnp.max(top, axis=1, keepdims=True)
            probs = [jnp.exp2(s - top) for s in blocks]
            total = jnp.sum(functools.reduce(jnp.add, probs), axis=1, keepdims=True)
            probs = [x.astype(BF16) for x in probs]
            mixed = nn(jnp.concatenate(probs[: i + 1], axis=1), v[0:n, :])
            if edge:
                mixed = mixed + nn(probs[-1], vp[...])
            outs.append(mixed * (1.0 / total))
            level = jnp.broadcast_to(top + jnp.log2(total), (BLK, 128))
            lse[0, h : h + 1, i * BLK : n] = level.T[0:1, :]
        o[i * BLK : n, :] = jnp.where(lane < HD, outs[0], outs[1]).astype(BF16)


def attend(info, q, k, v, kp, vp):
    rows, half = q.shape
    pairs = half // (2 * HD)
    pair = pl.BlockSpec((rows, 2 * HD), lambda i, info: (0, i))
    pad = pl.BlockSpec((kp.shape[0], 2 * HD), lambda i, info: (0, i))
    return call(
        attend_body,
        (pairs,),
        1,
        [pair, pair, pair, pad, pad],
        [pair, pl.BlockSpec((1, 2, rows), lambda i, info: (i, 0, 0))],
        [shape((rows, half), BF16), shape((pairs, 2, rows), F32)],
        flops=pairs * 34 * BLK * BLK * 256 * 4,
        moved=6e6,
    )(info, q, k, v, kp, vp)


def attend_back_body(
    info, q, k, v, kp, vp, o, lse, d_own, d_other, dq, dk, dv, dkp, dvp, do, dk_sum, dv_sum, dkp_sum, dvp_sum
):
    parity, start, stop, pad_a, pad_b = info[1], info[2], info[3], info[4], info[5]
    local = d_own.shape[0]
    do[pl.ds(pl.multiple_of(parity * local, 128), local), :] = d_own[...]
    do[pl.ds(pl.multiple_of((1 - parity) * local, 128), local), :] = d_other[...]
    lane = lax.broadcasted_iota(jnp.int32, (1, 2 * HD), 1)
    pick = (
        lax.broadcasted_iota(jnp.int32, (8, 2 * HD), 1) // HD
        == lax.broadcasted_iota(jnp.int32, (8, 2 * HD), 0)
    ).astype(F32)
    inner = lax.dot_general(
        pick,
        do[...].astype(F32) * o[...].astype(F32),
        (((1,), (1,)), ((), ())),
        precision=lax.Precision.HIGHEST,
        preferred_element_type=F32,
    )
    row = lax.broadcasted_iota(jnp.int32, (BLK, 1), 0)
    col = lax.broadcasted_iota(jnp.int32, (1, 2 * BLK), 1) % BLK
    causal = row <= col
    pad_row = (row < pad_a) | (row >= pad_b)
    dk_sum[...] = jnp.zeros_like(dk_sum)
    dv_sum[...] = jnp.zeros_like(dv_sum)
    dkp_sum[...] = jnp.zeros_like(dkp_sum)
    dvp_sum[...] = jnp.zeros_like(dvp_sum)
    count = SLOT // BLK

    def split(x):
        zero = jnp.zeros_like(x)
        return [jnp.where(lane // HD == h, x, zero) for h in range(2)]

    for i in range(count):
        rows = slice(i * BLK, (i + 1) * BLK)
        qs = jnp.concatenate(split(q[rows, :]), axis=0)
        ds = jnp.concatenate(split(do[rows, :]), axis=0)
        level = jnp.concatenate([lse[0, 0:1, rows], lse[0, 1:2, rows]], axis=1)
        inner_i = jnp.concatenate([inner[0:1, rows], inner[1:2, rows]], axis=1)
        edge = i in (0, count - 1)
        pos_q = col + i * BLK
        in_q = (pos_q >= start) & (pos_q < stop)
        dq_sum = jnp.zeros((BLK, 2 * HD), F32)

        def block(kj, vj, mask):
            s = nt(kj, qs) * SCALE - level
            if mask is not None:
                s = jnp.where(mask, s, NEG)
            p = jnp.exp2(s)
            g = p * (nt(vj, ds) - inner_i)
            p, g = p.astype(BF16), g.astype(BF16)
            halves = split(kj)
            part = tn(g[:, :BLK], halves[0]) + tn(g[:, BLK:], halves[1])
            return nn(g, qs), nn(p, ds), part

        for j in range(i + 1):
            keys = slice(j * BLK, (j + 1) * BLK)
            pos_k = row + j * BLK
            mask = None
            if edge:
                in_k = (pos_k >= start) & (pos_k < stop)
                mask = (in_q & in_k) | (~in_q & ~in_k)
            elif j == 0:
                mask = jnp.broadcast_to(pos_k >= start, (BLK, 2 * BLK))
            if j == i:
                mask = causal if mask is None else mask & causal
            gk, gv, part = block(k[keys, :], v[keys, :], mask)
            dk_sum[keys, :] += gk
            dv_sum[keys, :] += gv
            dq_sum = dq_sum + part
        if edge:
            gk, gv, part = block(kp[...], vp[...], ~in_q & pad_row)
            dkp_sum[...] += gk
            dvp_sum[...] += gv
            dq_sum = dq_sum + part
        dq[rows, :] = (dq_sum * 0.125).astype(BF16)
    dk[...] = (dk_sum[...] * 0.125).astype(BF16)
    dv[...] = dv_sum[...].astype(BF16)
    dkp[...] = (dkp_sum[...] * 0.125).astype(BF16)
    dvp[...] = dvp_sum[...].astype(BF16)


def attend_back(info, q, k, v, kp, vp, o, lse, d_own, d_other):
    rows, half = q.shape
    pads = kp.shape[0]
    pairs = half // (2 * HD)
    pick = lambda n: pl.BlockSpec((n, 2 * HD), lambda i, info: (0, i))
    pair, pad, part = pick(rows), pick(pads), pick(d_own.shape[0])
    return call(
        attend_back_body,
        (pairs,),
        1,
        [pair, pair, pair, pad, pad, pair, pl.BlockSpec((1, 2, rows), lambda i, info: (i, 0, 0)), part, part],
        [pair, pair, pair, pad, pad],
        [shape((rows, half), BF16)] * 3 + [shape((pads, half), BF16)] * 2,
        [
            pltpu.VMEM((rows, 2 * HD), BF16),
            pltpu.VMEM((rows, 2 * HD), F32),
            pltpu.VMEM((rows, 2 * HD), F32),
            pltpu.VMEM((pads, 2 * HD), F32),
            pltpu.VMEM((pads, 2 * HD), F32),
        ],
        flops=pairs * 34 * BLK * BLK * 256 * 10,
        moved=14e6,
    )(info, q, k, v, kp, vp, o, lse, d_own, d_other)


def forward_body(info, pos, own, other, x, up, gains, biases, *refs, counts):
    total = sum(counts)
    parts = refs[:total]
    (out, g_feed, act_t, slope, n_t, branch, middle, edges, wo_out, wu_out, wd_out) = refs[total : total + 11]
    wo, wu, wd, normed, feed, sems, out_sems = refs[total + 11 :]
    parity = info[1]
    step, last = pl.program_id(0), pl.num_programs(0) - 1
    local = x.shape[0]
    half = own.shape[1]
    tile = slope.shape[1]
    blocks = local // 128

    def copies(which):
        first = sum(counts[:which])
        target = (wo, wu, wd)[which]
        return [
            pltpu.make_async_copy(
                parts[i],
                target.at[pl.ds(pl.multiple_of(pos[i], 16), parts[i].shape[0])],
                sems.at[i],
            )
            for i in range(first, first + counts[which])
        ]

    def store(which):
        return pltpu.make_async_copy(
            (wo, wu, wd)[which], (wo_out, wu_out, wd_out)[which], out_sems.at[which]
        )

    @pl.when(step == 0)
    def _():
        for which in range(3):
            for c in copies(which):
                c.start()
        for c in copies(0):
            c.wait()
        store(0).start()
        w_own = wo[pl.ds(pl.multiple_of(parity * half, 128), half), :]
        w_other = wo[pl.ds(pl.multiple_of((1 - parity) * half, 128), half), :]
        branch[...] = nn(own[...], w_own) + nn(other[...], w_other)

        def rows(i, carry):
            at = pl.ds(pl.multiple_of(i * 128, 128), 128)
            hat, _ = normalise(branch[at, :])
            mid = x[at, :].astype(F32) + hat * gains[1:2, :] + biases[1:2, :]
            middle[at, :] = mid
            hat, _ = normalise(mid)
            two = (hat * gains[2:3, :] + biases[2:3, :]).astype(BF16)
            normed[at, :] = two
            n_t[:, at] = two.T
            return carry

        lax.fori_loop(0, blocks, rows, 0)
        feed[...] = jnp.zeros_like(feed)
        for which in (1, 2):
            for c in copies(which):
                c.wait()
            store(which).start()

    cols = pl.ds(pl.multiple_of(step * tile, 128), tile)
    u = nn(normed[...], wu[:, cols])
    th = jnp.tanh(0.7978845608 * (u + 0.044715 * (u * u * u)))
    act = (0.5 * u * (1.0 + th)).astype(BF16)
    slope[...] = (
        0.5 * (1.0 + th) + 0.5 * u * (1.0 - th * th) * (0.7978845608 + (3 * 0.044715 * 0.7978845608) * (u * u))
    ).astype(BF16)
    act_t[...] = act.T
    feed[...] += nn(act, wd[cols, :])

    @pl.when(step == last)
    def _():
        def rows(i, carry):
            at = pl.ds(pl.multiple_of(i * 128, 128), 128)
            g = up[at, :].astype(F32)
            hat, rstd = normalise(feed[at, :])
            gain = gains[3:4, :]
            out[at, :] = (middle[at, :] + hat * gain + biases[3:4, :]).astype(BF16)
            g_feed[at, :] = norm_back(g, hat, rstd, gain).astype(BF16)
            return (
                carry[0] + jnp.sum(g * hat, axis=0, keepdims=True),
                carry[1] + jnp.sum(g, axis=0, keepdims=True),
            )

        zero = jnp.zeros((1, x.shape[1]), F32)
        a, b = lax.fori_loop(0, blocks, rows, (zero, zero))
        edges[0:1, :] = a
        edges[1:2, :] = b
        for which in range(3):
            store(which).wait()


def forward(info, pos, own, other, x, up, gains, biases, parts, counts, ff):
    attn, half, parity = own
    local, d = x.shape
    tile = 512
    once = lambda s: pl.BlockSpec(s, lambda *_: (0,) * len(s), pipeline_mode=pl.Buffered(1))
    return call(
        functools.partial(forward_body, counts=counts),
        (ff // tile,),
        2,
        [
            pl.BlockSpec((local, half), lambda i, info, pos: (info[1], 0), pipeline_mode=pl.Buffered(1)),
            once(other.shape),
            once(x.shape),
            once(up.shape),
            once(gains.shape),
            once(biases.shape),
        ]
        + [hbm()] * len(parts),
        [
            full((local, d)),
            full((local, d)),
            pl.BlockSpec((tile, local), lambda i, info, pos: (i, 0)),
            pl.BlockSpec((local, tile), lambda i, info, pos: (0, i)),
            full((d, local)),
            full((local, d)),
            full((local, d)),
            full((2, d)),
            hbm(),
            hbm(),
            hbm(),
        ],
        [
            shape((local, d), BF16),
            shape((local, d), BF16),
            shape((ff, local), BF16),
            shape((local, ff), BF16),
            shape((d, local), BF16),
            shape((local, d), F32),
            shape((local, d), F32),
            shape((2, d), F32),
            shape((d, d), BF16),
            shape((d, ff), BF16),
            shape((ff, d), BF16),
        ],
        [
            pltpu.VMEM((d, d), BF16),
            pltpu.VMEM((d, ff), BF16),
            pltpu.VMEM((ff, d), BF16),
            pltpu.VMEM((local, d), BF16),
            pltpu.VMEM((local, d), F32),
            pltpu.SemaphoreType.DMA((len(parts),)),
            pltpu.SemaphoreType.DMA((3,)),
        ],
        flops=2 * local * d * (d + 2 * ff),
        moved=60e6,
    )(info, pos, attn, other, x, up, gains, biases, *parts)


def back_body(info, g_feed, n_t, act_t, slope, wd, wu, keep, send, g_two, *, fsdp):
    r = pl.program_id(0)
    f = info[0]
    tile = wd.shape[0]
    rows = n_t.shape[0] // fsdp
    width = keep.shape[2]
    piece = width // fsdp
    here = r ^ f
    g = g_feed[...]
    hid = (nt(g, wd[...]) * slope[...].astype(F32)).astype(BF16)
    down = nn(act_t[...], g).astype(BF16)
    even = r % 2 == 0

    @pl.when(even)
    def _():
        keep[r // 2, 0:tile, :] = down

    @pl.when(~even)
    def _():
        send[r // 2, 0:tile, :] = down

    lanes = pl.ds(pl.multiple_of(here * piece, 128), piece)
    for other in range(fsdp):
        shard = other ^ f
        up = nn(n_t[pl.ds(pl.multiple_of(shard * rows, 128), rows), :], hid).astype(BF16)
        target = (keep, send)[other % 2]
        for c in range(tile // piece):
            target[other // 2, tile + c * rows : tile + (c + 1) * rows, lanes] = up[:, c * piece : (c + 1) * piece]
    part = nt(hid, wu[...])

    @pl.when(r == 0)
    def _():
        g_two[...] = part

    @pl.when(r != 0)
    def _():
        g_two[...] += part


def back_group(info, g, g_feed, n_t, act_t, slope, wd, wu, fsdp):
    local, d = g_feed.shape
    ff = wd.shape[0]
    tile = ff // fsdp // GROUPS
    extra = (d // fsdp) * (fsdp * tile // d)
    block = lambda i, info: (i ^ info[0]) * GROUPS + g
    grads = shape((fsdp // 2, tile + extra, d), BF16)
    return call(
        functools.partial(back_body, fsdp=fsdp),
        (fsdp,),
        1,
        [
            full((local, d)),
            full((d, local)),
            pl.BlockSpec((tile, local), lambda i, info: (block(i, info), 0)),
            pl.BlockSpec((local, tile), lambda i, info: (0, block(i, info))),
            pl.BlockSpec((tile, d), lambda i, info: (block(i, info), 0)),
            pl.BlockSpec((d, tile), lambda i, info: (0, block(i, info))),
        ],
        [full(grads.shape), full(grads.shape), full((local, d))],
        [grads, grads, shape((local, d), F32)],
        flops=8 * local * d * tile * fsdp,
        moved=40e6,
    )(info, g_feed, n_t, act_t, slope, wd, wu)


def middle_body(
    info, ga, gb, middle, branch, up, gains, wo, own, other, g_mid, d_own, d_send, keep, send, edges, att, gbr, *, fsdp
):
    f, parity = info[0], info[1]
    step, last = pl.program_id(0), pl.num_programs(0) - 1
    half = own.shape[1]

    @pl.when(step == 0)
    def _():
        edges[...] = jnp.zeros_like(edges)
        att[:, pl.ds(pl.multiple_of(parity * half, 128), half)] = own[...]
        att[:, pl.ds(pl.multiple_of((1 - parity) * half, 128), half)] = other[...]

    g = ga[...] + gb[...]
    hat, rstd = normalise(middle[...])
    edges[2:3, :] += jnp.sum(g * hat, axis=0, keepdims=True)
    edges[3:4, :] += jnp.sum(g, axis=0, keepdims=True)
    gm = up[...].astype(F32) + norm_back(g, hat, rstd, gains[2:3, :])
    g_mid[...] = gm
    hat, rstd = normalise(branch[...])
    edges[0:1, :] += jnp.sum(gm * hat, axis=0, keepdims=True)
    edges[1:2, :] += jnp.sum(gm, axis=0, keepdims=True)
    gr = norm_back(gm, hat, rstd, gains[1:2, :]).astype(BF16)
    gbr[pl.ds(pl.multiple_of(step * gr.shape[0], 16), gr.shape[0]), :] = gr

    @pl.when(step == last)
    def _():
        grad = gbr[...]
        d_send[...] = nt(grad, wo[pl.ds(pl.multiple_of((1 - parity) * half, 128), half), :]).astype(BF16)
        d_own[...] = nt(grad, wo[pl.ds(pl.multiple_of(parity * half, 128), half), :]).astype(BF16)
        rows = keep.shape[1]
        for r in range(fsdp):
            cols = pl.ds(pl.multiple_of((r ^ f) * rows, 128), rows)
            (keep, send)[r % 2][r // 2] = tn(att[:, cols], grad).astype(BF16)


def middle_back(info, ga, gb, middle, branch, up, gains, wo, attn, half, other, fsdp):
    local, d = ga.shape
    rows = 128
    block = pl.BlockSpec((rows, d), lambda i, info: (i, 0))
    grads = shape((fsdp // 2, d // fsdp, d), BF16)
    return call(
        functools.partial(middle_body, fsdp=fsdp),
        (local // rows,),
        1,
        [block, block, block, block, block, full(gains.shape), full(wo.shape)]
        + [pl.BlockSpec((local, half), lambda i, info: (info[1], 0)), full(other.shape)],
        [block, full((local, half)), full((local, half)), full(grads.shape), full(grads.shape), full((4, d))],
        [shape((local, d), F32), shape((local, half), BF16), shape((local, half), BF16), grads, grads, shape((4, d), F32)],
        [pltpu.VMEM((local, d), BF16), pltpu.VMEM((local, d), BF16)],
        flops=4 * local * d * d,
        moved=22e6,
    )(info, ga, gb, middle, branch, up, gains, wo, attn, other)


def project_back_body(
    info, own, head, rest, padx, gains, dq, dk, dv, dkp, dvp, w, n_t, np_t, g_own, g_send, g_pad, keep, send, edges, *, fsdp
):
    f, parity = info[0], info[1]
    step = pl.program_id(0)
    local = own.shape[0]
    half = dq.shape[1]
    gain = gains[0:1, :]

    def through(at):
        return (
            nt(dq[at, :], w[:, 0:half])
            + nt(dk[at, :], w[:, half : 2 * half])
            + nt(dv[at, :], w[:, 2 * half :])
        )

    @pl.when(step == 0)
    def _():
        g = nt(dkp[...], w[:, half : 2 * half]) + nt(dvp[...], w[:, 2 * half :])
        g_pad[...] = g.astype(BF16)
        hat, _ = normalise(padx[...].astype(F32))
        edges[0:1, :] = jnp.sum(g * hat, axis=0, keepdims=True)
        edges[1:2, :] = jnp.sum(g, axis=0, keepdims=True)
        g = through(pl.ds(pl.multiple_of((1 - parity) * local, 128), local))
        g_send[...] = g.astype(BF16)
        hat, _ = normalise(jnp.concatenate([head[...], rest[...]], axis=0).astype(F32))
        edges[0:1, :] += jnp.sum(g * hat, axis=0, keepdims=True)
        edges[1:2, :] += jnp.sum(g, axis=0, keepdims=True)

    @pl.when(step == 1)
    def _():
        g = through(pl.ds(pl.multiple_of(parity * local, 128), local))
        g_own[...] = g
        hat, _ = normalise(own[...].astype(F32))
        edges[0:1, :] += jnp.sum(g * hat, axis=0, keepdims=True)
        edges[1:2, :] += jnp.sum(g, axis=0, keepdims=True)
        rows = keep.shape[1]
        for r in range(fsdp):
            at = pl.ds(pl.multiple_of((r ^ f) * rows, 128), rows)
            target = (keep, send)[r % 2]
            left, pads = n_t[at, :], np_t[at, :]
            target[r // 2, :, 0:half] = nn(left, dq[...]).astype(BF16)
            target[r // 2, :, half : 2 * half] = (nn(left, dk[...]) + nn(pads, dkp[...])).astype(BF16)
            target[r // 2, :, 2 * half :] = (nn(left, dv[...]) + nn(pads, dvp[...])).astype(BF16)


def project_back(info, own, head, rest, padx, gains, dq, dk, dv, dkp, dvp, w, n_t, np_t, fsdp):
    local, d = own.shape
    wide = w.shape[1]
    pads = padx.shape[0]
    grads = shape((fsdp // 2, d // fsdp, wide), BF16)
    arrays = (own, head, rest, padx, gains, dq, dk, dv, dkp, dvp, w, n_t, np_t)
    return call(
        functools.partial(project_back_body, fsdp=fsdp),
        (2,),
        1,
        [pl.BlockSpec(a.shape, lambda *_: (0, 0), pipeline_mode=pl.Buffered(1)) for a in arrays],
        [full((local, d)), full((local, d)), full((pads, d)), full(grads.shape), full(grads.shape), full((2, d))],
        [shape((local, d), F32), shape((local, d), BF16), shape((pads, d), BF16), grads, grads, shape((2, d), F32)],
        flops=8 * local * d * wide,
        moved=24e6,
    )(info, *arrays)


def finish_body(info, x, g_own, g_other, pad_a, pad_b, g_mid, gains, out, total):
    s, start, cut = info[6], info[7], info[8]
    row = lax.broadcasted_iota(jnp.int32, (pad_a.shape[0], 1), 0)
    mine = ((s == 0) & (row < start)) | ((s == 1) & (row >= cut))
    extra = jnp.where(mine, pad_a[...].astype(F32) + pad_b[...].astype(F32), 0.0)
    total[...] = g_own[...] + g_other[...].astype(F32)
    at = pl.ds(pl.multiple_of(jnp.where(s == 0, 0, total.shape[0] - pad_a.shape[0]), 128), pad_a.shape[0])
    total[at, :] += extra

    def rows(i, carry):
        at = pl.ds(pl.multiple_of(i * 128, 128), 128)
        hat, rstd = normalise(x[at, :].astype(F32))
        out[at, :] = (g_mid[at, :] + norm_back(total[at, :], hat, rstd, gains[0:1, :])).astype(BF16)
        return carry

    lax.fori_loop(0, x.shape[0] // 128, rows, 0)


def finish(info, x, g_own, g_other, pad_a, pad_b, g_mid, gains):
    arrays = (x, g_own, g_other, pad_a, pad_b, g_mid, gains)
    return call(
        finish_body,
        (1,),
        1,
        [full(a.shape) for a in arrays],
        full(x.shape),
        shape(x.shape, BF16),
        [pltpu.VMEM(x.shape, F32)],
        flops=1e7,
        moved=12e6,
    )(info, *arrays)


def hop(value, axis, mask):
    return lax.ppermute(value, axis, [(i, i ^ mask) for i in range(lax.axis_size(axis))])


def arrange(pieces, index):
    count = len(pieces)
    if count == 1:
        return list(pieces)
    half = count // 2
    low, high = arrange(pieces[:half], index), arrange(pieces[half:], index)
    bit = (index & half) != 0
    return [jnp.where(bit, b, a) for a, b in zip(low, high)] + [jnp.where(bit, a, b) for a, b in zip(low, high)]


def part_of(value, count, index):
    rows = value.shape[0] // count
    return lax.dynamic_slice_in_dim(value, index * rows, rows, 0)


def gather_weight(w, f, x):
    fsdp, dp = lax.axis_size("fsdp"), lax.axis_size("dp")
    rows = w.shape[0]
    sub = rows // dp
    pieces, places = [w, hop(w, "fsdp", 1)], [f * rows, (f ^ 1) * rows]
    mine = part_of(w, dp, x)
    for ry in range(1, fsdp // 2):
        first = hop(mine, "fsdp", 2 * ry)
        for rx in range(dp):
            got = first if rx == 0 else hop(first, "dp", rx)
            pieces += [got, hop(got, "fsdp", 1)]
            place = (x ^ rx) * sub
            places += [(f ^ (2 * ry)) * rows + place, (f ^ (2 * ry + 1)) * rows + place]
    return pieces, places


def gather_half(w, f):
    fsdp = lax.axis_size("fsdp")
    rows = w.shape[0]
    pieces, places = [], []
    for ry in range(fsdp // 2):
        got = w if ry == 0 else hop(w, "fsdp", 2 * ry)
        pieces += [got, hop(got, "fsdp", 1)]
        places += [(f ^ (2 * ry)) * rows, (f ^ (2 * ry + 1)) * rows]
    return pieces, places


def add_hop(total, value, axis, mask):
    return total + hop(value.astype(BF16), axis, mask).astype(F32)


def split_sum(value, count, axis, unit, index):
    total = part_of(value, count, index)
    for m in range(1, count):
        total = add_hop(total, part_of(value, count, index ^ m), axis, m * unit)
    return total


def join(value, count, axis, unit, index):
    pieces = [value] + [hop(value, axis, m * unit) for m in range(1, count)]
    return jnp.concatenate(arrange(pieces, index), axis=0)


def reduce_shard(keep, send, x, s, pair_done):
    got = hop(send, "fsdp", 1)
    total = keep[0].astype(F32) + got[0].astype(F32)
    for ry in range(1, keep.shape[0]):
        total = add_hop(total, keep[ry].astype(F32) + got[ry].astype(F32), "fsdp", 2 * ry)
    dp = lax.axis_size("dp")
    part = split_sum(total, dp, "dp", 1, x)
    count, unit, index = (2, 2, s // 2) if pair_done else (lax.axis_size("seq"), 1, s)
    part = split_sum(part, count, "seq", unit, index)
    part = join(part.astype(BF16), count, "seq", unit, index)
    return join(part, dp, "dp", 1, x)


def sum_all(value):
    for axis in ("fsdp", "dp", "seq"):
        m = 1
        while m < lax.axis_size(axis):
            value = value + hop(value, axis, m)
            m *= 2
    return value


def local(
    tokens, qkv_weight, out_weight, up_weight, down_weight, norm_gain, norm_bias, caption_len, item_start, grad_out
):
    x_tok, up = tokens[0], grad_out[0]
    local_rows, d = x_tok.shape
    fsdp = lax.axis_size("fsdp")
    ff = up_weight.shape[1]
    half = d // 2
    f, x, s = lax.axis_index("fsdp"), lax.axis_index("dp"), lax.axis_index("seq")
    parity, slot = s % 2, s // 2
    caps, starts = caption_len[0], item_start[0]
    start = jnp.where(slot == 0, starts[0], starts[1] - SLOT)
    stop = start + jnp.where(slot == 0, caps[0], caps[1]) + IMAGE
    pad_a = jnp.where(slot == 0, 0, starts[0])
    pad_b = jnp.where(slot == 0, BLK, starts[0] + caps[0])
    info = jnp.stack(
        [f, parity, start, stop, pad_a, pad_b, s, starts[0], starts[0] + caps[0]]
    ).astype(jnp.int32)

    head = hop(x_tok[:BLK], "seq", 1)
    rest = hop(x_tok[BLK:], "seq", 1)
    index = lax.broadcasted_iota(jnp.int32, (BLK, 1), 0)
    pads = jnp.where(index < starts[0], head, x_tok[local_rows - BLK :])
    pads = lax.ppermute(pads, "seq", [(1, 2)])
    pads = jnp.where(s == 3, lax.ppermute(pads, "seq", [(2, 3)]), pads)

    w_half = jnp.concatenate(
        [lax.dynamic_slice_in_dim(qkv_weight, c * d + parity * half, half, 1) for c in range(3)], axis=1
    )
    parts, places = gather_half(w_half, f)
    gain0, bias0 = norm_gain[0:1], norm_bias[0:1]
    q, k, v, n_t, w_qkv = project(
        info, jnp.stack(places).astype(jnp.int32), x_tok, head, rest, gain0, bias0, parts
    )
    kp, vp, np_t = pad_project(pads, gain0, bias0, w_qkv)
    mixed, lse = attend(info, q, k, v, kp, vp)
    to_send = lax.dynamic_slice_in_dim(mixed, (1 - parity) * local_rows, local_rows, 0)
    other = hop(to_send, "seq", 1)

    parts, places, counts = [], [], []
    for w in (out_weight, up_weight, down_weight):
        got, at = gather_weight(w, f, x)
        parts += got
        places += at
        counts.append(len(got))
    (out, g_feed, act_t, slope, two_t, branch, middle, edges3, wo, wu, wd) = forward(
        info,
        jnp.stack(places).astype(jnp.int32),
        (mixed, half, parity),
        other,
        x_tok,
        up,
        norm_gain,
        norm_bias,
        parts,
        tuple(counts),
        ff,
    )
    keeps, g_twos = [], []
    for g in range(GROUPS):
        keep, send, g_two = back_group(info, g, g_feed, two_t, act_t, slope, wd, wu, fsdp)
        keeps.append((keep, send))
        g_twos.append(g_two)
    g_mid, d_own, d_send, keep_o, send_o, edges12 = middle_back(
        info, g_twos[0], g_twos[1], middle, branch, up, norm_gain, wo, mixed, half, other, fsdp
    )
    d_other = hop(d_send, "seq", 1)
    dq, dk, dv, dkp, dvp = attend_back(info, q, k, v, kp, vp, mixed, lse, d_own, d_other)
    g_own, g_send, g_pad, keep_q, send_q, edges0 = project_back(
        info, x_tok, head, rest, pads, norm_gain, dq, dk, dv, dkp, dvp, w_qkv, n_t, np_t, fsdp
    )
    g_other = hop(g_send, "seq", 1)
    back_a = lax.ppermute(g_pad, "seq", [(2, 0), (3, 1)])
    back_b = lax.ppermute(g_pad, "seq", [(2, 1), (3, 0)])
    grad_in = finish(info, x_tok, g_own, g_other, back_a, back_b, g_mid, norm_gain)

    sums = sum_all(
        jnp.stack(
            [edges0[0], edges12[0], edges12[2], edges3[0], edges0[1], edges12[1], edges12[3], edges3[1]]
        )
    )

    reduced = [reduce_shard(a, b, x, s, False) for a, b in keeps]
    grad_proj = reduce_shard(keep_o, send_o, x, s, False).astype(F32)
    half_q = reduce_shard(keep_q, send_q, x, s, True)
    both = arrange([half_q, hop(half_q, "seq", 1)], parity)
    grad_qkv = jnp.concatenate(
        [both[h][:, c * half : (c + 1) * half] for c in range(3) for h in range(2)], axis=1
    ).astype(F32)
    tile = ff // fsdp // GROUPS
    rows = d // fsdp
    grad_down = jnp.concatenate([r[:tile] for r in reduced], axis=0).astype(F32)
    piece = d // fsdp
    blocks = []
    for h in range(fsdp):
        for r in reduced:
            for c in range(tile // piece):
                blocks.append(r[tile + c * rows : tile + (c + 1) * rows, h * piece : (h + 1) * piece])
    grad_up = jnp.concatenate(blocks, axis=1).astype(F32)
    return (out[None], grad_in[None], grad_qkv, grad_proj, grad_up, grad_down, sums[0:4], sums[4:8])


def solution(mesh):
    rows = P(("fsdp", "dp"), "seq", None)
    shard = P("fsdp", None)
    items = P(("fsdp", "dp"), None)
    return jax.shard_map(
        local,
        mesh=mesh,
        in_specs=(rows, shard, shard, shard, shard, P(), P(), items, items, rows),
        out_specs=(rows, rows, shard, shard, shard, shard, P(), P()),
        check_vma=False,
    )
```

```python
import functools

import jax
import jax.numpy as jnp
from jax import lax
from jax.experimental import pallas as pl
from jax.experimental.pallas import tpu as pltpu
from jax.sharding import PartitionSpec as P

HD = 64
IMAGE = 1024
SLOT = 1280
BLK = 256
LOG2E = 1.4426950408889634
SCALE = LOG2E / 8.0
NEG = -1e30
F32 = jnp.float32
BF16 = jnp.bfloat16
VMEM_LIMIT = 60 * 1024 * 1024
GROUPS = 2


def nn(a, b):
    return lax.dot_general(a, b, (((1,), (0,)), ((), ())), preferred_element_type=F32)


def nt(a, b):
    return lax.dot_general(a, b, (((1,), (1,)), ((), ())), preferred_element_type=F32)


def tn(a, b):
    return lax.dot_general(a, b, (((0,), (0,)), ((), ())), preferred_element_type=F32)


def normalise(v):
    mean = jnp.mean(v, axis=-1, keepdims=True)
    centred = v - mean
    var = jnp.mean(centred * centred, axis=-1, keepdims=True)
    rstd = lax.rsqrt(var + 1e-05)
    return centred * rstd, rstd


def norm_back(g, hat, rstd, gain):
    gg = g * gain
    return rstd * (
        gg - jnp.mean(gg, axis=-1, keepdims=True) - hat * jnp.mean(gg * hat, axis=-1, keepdims=True)
    )


def call(body, grid, prefetch, in_specs, out_specs, out_shape, scratch=(), flops=0, moved=0):
    return pl.pallas_call(
        body,
        grid_spec=pltpu.PrefetchScalarGridSpec(
            num_scalar_prefetch=prefetch,
            grid=grid,
            in_specs=in_specs,
            out_specs=out_specs,
            scratch_shapes=list(scratch),
        ),
        out_shape=out_shape,
        compiler_params=pltpu.CompilerParams(vmem_limit_bytes=VMEM_LIMIT),
        cost_estimate=pl.CostEstimate(flops=int(flops), bytes_accessed=int(moved), transcendentals=0),
    )


def full(shape):
    zeros = (0,) * len(shape)
    return pl.BlockSpec(shape, lambda *_: zeros)


def hbm():
    return pl.BlockSpec(memory_space=pl.ANY)


def shape(dims, dtype):
    return jax.ShapeDtypeStruct(dims, dtype)


def project_body(info, pos, own, head, rest, gain, bias, *refs, pieces):
    parts = refs[:pieces]
    q, k, v, n_t, w, sems = refs[pieces:]
    step = pl.program_id(0)
    half = q.shape[1]

    def copies():
        return [
            pltpu.make_async_copy(
                parts[i], w.at[pl.ds(pl.multiple_of(pos[i], 16), parts[i].shape[0])], sems.at[i]
            )
            for i in range(pieces)
        ]

    @pl.when(step == 0)
    def _():
        for c in copies():
            c.start()

    def rows(x):
        hat, _ = normalise(x.astype(F32))
        return (hat * gain[...] + bias[...]).astype(BF16)

    def emit(normed):
        n_t[...] = normed.T
        out = nn(normed, w[...])
        q[...] = out[:, :half].astype(BF16)
        k[...] = out[:, half : 2 * half].astype(BF16)
        v[...] = out[:, 2 * half :].astype(BF16)

    @pl.when(step == 0)
    def _():
        normed = rows(own[...])
        for c in copies():
            c.wait()
        emit(normed)

    @pl.when(step == 1)
    def _():
        emit(rows(jnp.concatenate([head[...], rest[...]], axis=0)))


def project(info, pos, own, head, rest, gain, bias, parts):
    local, d = own.shape
    wide = parts[0].shape[1]
    half = wide // 3
    block = lambda i, info, pos: ((info[1] + i) % 2, 0)
    return call(
        functools.partial(project_body, pieces=len(parts)),
        (2,),
        2,
        [full(own.shape), full(head.shape), full(rest.shape), full((1, d)), full((1, d))]
        + [hbm()] * len(parts),
        [pl.BlockSpec((local, half), block)] * 3
        + [
            pl.BlockSpec((d, local), lambda i, info, pos: (0, (info[1] + i) % 2)),
            full((d, wide)),
        ],
        [shape((2 * local, half), BF16)] * 3 + [shape((d, 2 * local), BF16), shape((d, wide), BF16)],
        [pltpu.SemaphoreType.DMA((len(parts),))],
        flops=4 * local * d * wide,
        moved=16e6,
    )(info, pos, own, head, rest, gain, bias, *parts)


def pad_body(x, gain, bias, w, k, v, n_t):
    hat, _ = normalise(x[...].astype(F32))
    normed = (hat * gain[...] + bias[...]).astype(BF16)
    n_t[...] = normed.T
    half = k.shape[1]
    out = nn(normed, w[:, half:])
    k[...] = out[:, :half].astype(BF16)
    v[...] = out[:, half:].astype(BF16)


def pad_project(x, gain, bias, w):
    rows, d = x.shape
    half = w.shape[1] // 3
    return call(
        pad_body,
        (1,),
        0,
        [full(x.shape), full((1, d)), full((1, d)), full(w.shape)],
        [full((rows, half)), full((rows, half)), full((d, rows))],
        [shape((rows, half), BF16)] * 2 + [shape((d, rows), BF16)],
        flops=4 * rows * d * half,
        moved=5e6,
    )(x, gain, bias, w)


def attend_body(info, q, k, v, kp, vp, o, lse):
    start, stop, pad_a, pad_b = info[2], info[3], info[4], info[5]
    lane = lax.broadcasted_iota(jnp.int32, (1, 2 * HD), 1)
    row = lax.broadcasted_iota(jnp.int32, (BLK, 1), 0)
    col = lax.broadcasted_iota(jnp.int32, (1, BLK), 1)
    causal = col <= row
    pad_col = (col < pad_a) | (col >= pad_b)
    count = SLOT // BLK
    for i in range(count):
        n = (i + 1) * BLK
        qi = q[i * BLK : n, :]
        edge = i in (0, count - 1)
        pos_q = row + i * BLK
        in_q = (pos_q >= start) & (pos_q < stop)
        masks = []
        for j in range(i + 1):
            pos_k = col + j * BLK
            mask = None
            if edge:
                in_k = (pos_k >= start) & (pos_k < stop)
                mask = (in_q & in_k) | (~in_q & ~in_k)
            elif j == 0:
                mask = jnp.broadcast_to(pos_k >= start, (BLK, BLK))
            if j == i:
                mask = causal if mask is None else mask & causal
            masks.append(mask)
        outs = []
        for h in range(2):
            qh = jnp.where(lane // HD == h, qi, jnp.zeros_like(qi))
            blocks = []
            for j in range(i + 1):
                s = nt(qh, k[j * BLK : (j + 1) * BLK, :]) * SCALE
                if masks[j] is not None:
                    s = jnp.where(masks[j], s, NEG)
                blocks.append(s)
            if edge:
                s = nt(qh, kp[...]) * SCALE
                blocks.append(jnp.where(~in_q & pad_col, s, NEG))
            top = functools.reduce(jnp.maximum, blocks)
            top = jnp.max(top, axis=1, keepdims=True)
            probs = [jnp.exp2(s - top) for s in blocks]
            total = jnp.sum(functools.reduce(jnp.add, probs), axis=1, keepdims=True)
            probs = [x.astype(BF16) for x in probs]
            mixed = nn(jnp.concatenate(probs[: i + 1], axis=1), v[0:n, :])
            if edge:
                mixed = mixed + nn(probs[-1], vp[...])
            outs.append(mixed * (1.0 / total))
            level = jnp.broadcast_to(top + jnp.log2(total), (BLK, 128))
            lse[0, h : h + 1, i * BLK : n] = level.T[0:1, :]
        o[i * BLK : n, :] = jnp.where(lane < HD, outs[0], outs[1]).astype(BF16)


def attend(info, q, k, v, kp, vp):
    rows, half = q.shape
    pairs = half // (2 * HD)
    pair = pl.BlockSpec((rows, 2 * HD), lambda i, info: (0, i))
    pad = pl.BlockSpec((kp.shape[0], 2 * HD), lambda i, info: (0, i))
    return call(
        attend_body,
        (pairs,),
        1,
        [pair, pair, pair, pad, pad],
        [pair, pl.BlockSpec((1, 2, rows), lambda i, info: (i, 0, 0))],
        [shape((rows, half), BF16), shape((pairs, 2, rows), F32)],
        flops=pairs * 34 * BLK * BLK * 256 * 4,
        moved=6e6,
    )(info, q, k, v, kp, vp)


def attend_back_body(
    info, q, k, v, kp, vp, o, lse, d_own, d_other, dq, dk, dv, dkp, dvp, do, dk_sum, dv_sum, dkp_sum, dvp_sum
):
    parity, start, stop, pad_a, pad_b = info[1], info[2], info[3], info[4], info[5]
    local = d_own.shape[0]
    do[pl.ds(pl.multiple_of(parity * local, 128), local), :] = d_own[...]
    do[pl.ds(pl.multiple_of((1 - parity) * local, 128), local), :] = d_other[...]
    lane = lax.broadcasted_iota(jnp.int32, (1, 2 * HD), 1)
    pick = (
        lax.broadcasted_iota(jnp.int32, (8, 2 * HD), 1) // HD
        == lax.broadcasted_iota(jnp.int32, (8, 2 * HD), 0)
    ).astype(F32)
    inner = lax.dot_general(
        pick,
        do[...].astype(F32) * o[...].astype(F32),
        (((1,), (1,)), ((), ())),
        precision=lax.Precision.HIGHEST,
        preferred_element_type=F32,
    )
    row = lax.broadcasted_iota(jnp.int32, (BLK, 1), 0)
    col = lax.broadcasted_iota(jnp.int32, (1, 2 * BLK), 1) % BLK
    causal = row <= col
    pad_row = (row < pad_a) | (row >= pad_b)
    dk_sum[...] = jnp.zeros_like(dk_sum)
    dv_sum[...] = jnp.zeros_like(dv_sum)
    dkp_sum[...] = jnp.zeros_like(dkp_sum)
    dvp_sum[...] = jnp.zeros_like(dvp_sum)
    count = SLOT // BLK

    def split(x):
        zero = jnp.zeros_like(x)
        return [jnp.where(lane // HD == h, x, zero) for h in range(2)]

    for i in range(count):
        rows = slice(i * BLK, (i + 1) * BLK)
        qs = jnp.concatenate(split(q[rows, :]), axis=0)
        ds = jnp.concatenate(split(do[rows, :]), axis=0)
        level = jnp.concatenate([lse[0, 0:1, rows], lse[0, 1:2, rows]], axis=1)
        inner_i = jnp.concatenate([inner[0:1, rows], inner[1:2, rows]], axis=1)
        edge = i in (0, count - 1)
        pos_q = col + i * BLK
        in_q = (pos_q >= start) & (pos_q < stop)
        dq_sum = jnp.zeros((BLK, 2 * HD), F32)

        def block(kj, vj, mask):
            s = nt(kj, qs) * SCALE - level
            if mask is not None:
                s = jnp.where(mask, s, NEG)
            p = jnp.exp2(s)
            g = p * (nt(vj, ds) - inner_i)
            p, g = p.astype(BF16), g.astype(BF16)
            halves = split(kj)
            part = tn(g[:, :BLK], halves[0]) + tn(g[:, BLK:], halves[1])
            return nn(g, qs), nn(p, ds), part

        for j in range(i + 1):
            keys = slice(j * BLK, (j + 1) * BLK)
            pos_k = row + j * BLK
            mask = None
            if edge:
                in_k = (pos_k >= start) & (pos_k < stop)
                mask = (in_q & in_k) | (~in_q & ~in_k)
            elif j == 0:
                mask = jnp.broadcast_to(pos_k >= start, (BLK, 2 * BLK))
            if j == i:
                mask = causal if mask is None else mask & causal
            gk, gv, part = block(k[keys, :], v[keys, :], mask)
            dk_sum[keys, :] += gk
            dv_sum[keys, :] += gv
            dq_sum = dq_sum + part
        if edge:
            gk, gv, part = block(kp[...], vp[...], ~in_q & pad_row)
            dkp_sum[...] += gk
            dvp_sum[...] += gv
            dq_sum = dq_sum + part
        dq[rows, :] = (dq_sum * 0.125).astype(BF16)
    dk[...] = (dk_sum[...] * 0.125).astype(BF16)
    dv[...] = dv_sum[...].astype(BF16)
    dkp[...] = (dkp_sum[...] * 0.125).astype(BF16)
    dvp[...] = dvp_sum[...].astype(BF16)


def attend_back(info, q, k, v, kp, vp, o, lse, d_own, d_other):
    rows, half = q.shape
    pads = kp.shape[0]
    pairs = half // (2 * HD)
    pick = lambda n: pl.BlockSpec((n, 2 * HD), lambda i, info: (0, i))
    pair, pad, part = pick(rows), pick(pads), pick(d_own.shape[0])
    return call(
        attend_back_body,
        (pairs,),
        1,
        [pair, pair, pair, pad, pad, pair, pl.BlockSpec((1, 2, rows), lambda i, info: (i, 0, 0)), part, part],
        [pair, pair, pair, pad, pad],
        [shape((rows, half), BF16)] * 3 + [shape((pads, half), BF16)] * 2,
        [
            pltpu.VMEM((rows, 2 * HD), BF16),
            pltpu.VMEM((rows, 2 * HD), F32),
            pltpu.VMEM((rows, 2 * HD), F32),
            pltpu.VMEM((pads, 2 * HD), F32),
            pltpu.VMEM((pads, 2 * HD), F32),
        ],
        flops=pairs * 34 * BLK * BLK * 256 * 10,
        moved=14e6,
    )(info, q, k, v, kp, vp, o, lse, d_own, d_other)


def forward_body(info, pos, own, other, x, up, gains, biases, *refs, counts):
    total = sum(counts)
    parts = refs[:total]
    (out, g_feed, act_t, slope, n_t, branch, middle, edges, wo_out, wu_out, wd_out) = refs[total : total + 11]
    wo, wu, wd, normed, feed, sems, out_sems = refs[total + 11 :]
    parity = info[1]
    step, last = pl.program_id(0), pl.num_programs(0) - 1
    local = x.shape[0]
    half = own.shape[1]
    tile = slope.shape[1]
    blocks = local // 128

    def copies(which):
        first = sum(counts[:which])
        target = (wo, wu, wd)[which]
        return [
            pltpu.make_async_copy(
                parts[i],
                target.at[pl.ds(pl.multiple_of(pos[i], 16), parts[i].shape[0])],
                sems.at[i],
            )
            for i in range(first, first + counts[which])
        ]

    def store(which):
        return pltpu.make_async_copy(
            (wo, wu, wd)[which], (wo_out, wu_out, wd_out)[which], out_sems.at[which]
        )

    @pl.when(step == 0)
    def _():
        for which in range(3):
            for c in copies(which):
                c.start()
        for c in copies(0):
            c.wait()
        store(0).start()
        w_own = wo[pl.ds(pl.multiple_of(parity * half, 128), half), :]
        w_other = wo[pl.ds(pl.multiple_of((1 - parity) * half, 128), half), :]
        branch[...] = nn(own[...], w_own) + nn(other[...], w_other)

        def rows(i, carry):
            at = pl.ds(pl.multiple_of(i * 128, 128), 128)
            hat, _ = normalise(branch[at, :])
            mid = x[at, :].astype(F32) + hat * gains[1:2, :] + biases[1:2, :]
            middle[at, :] = mid
            hat, _ = normalise(mid)
            two = (hat * gains[2:3, :] + biases[2:3, :]).astype(BF16)
            normed[at, :] = two
            n_t[:, at] = two.T
            return carry

        lax.fori_loop(0, blocks, rows, 0)
        feed[...] = jnp.zeros_like(feed)
        for which in (1, 2):
            for c in copies(which):
                c.wait()
            store(which).start()

    cols = pl.ds(pl.multiple_of(step * tile, 128), tile)
    u = nn(normed[...], wu[:, cols])
    th = jnp.tanh(0.7978845608 * (u + 0.044715 * (u * u * u)))
    act = (0.5 * u * (1.0 + th)).astype(BF16)
    slope[...] = (
        0.5 * (1.0 + th) + 0.5 * u * (1.0 - th * th) * (0.7978845608 + (3 * 0.044715 * 0.7978845608) * (u * u))
    ).astype(BF16)
    act_t[...] = act.T
    feed[...] += nn(act, wd[cols, :])

    @pl.when(step == last)
    def _():
        def rows(i, carry):
            at = pl.ds(pl.multiple_of(i * 128, 128), 128)
            g = up[at, :].astype(F32)
            hat, rstd = normalise(feed[at, :])
            gain = gains[3:4, :]
            out[at, :] = (middle[at, :] + hat * gain + biases[3:4, :]).astype(BF16)
            g_feed[at, :] = norm_back(g, hat, rstd, gain).astype(BF16)
            return (
                carry[0] + jnp.sum(g * hat, axis=0, keepdims=True),
                carry[1] + jnp.sum(g, axis=0, keepdims=True),
            )

        zero = jnp.zeros((1, x.shape[1]), F32)
        a, b = lax.fori_loop(0, blocks, rows, (zero, zero))
        edges[0:1, :] = a
        edges[1:2, :] = b
        for which in range(3):
            store(which).wait()


def forward(info, pos, own, other, x, up, gains, biases, parts, counts, ff):
    attn, half, parity = own
    local, d = x.shape
    tile = 512
    once = lambda s: pl.BlockSpec(s, lambda *_: (0,) * len(s), pipeline_mode=pl.Buffered(1))
    return call(
        functools.partial(forward_body, counts=counts),
        (ff // tile,),
        2,
        [
            pl.BlockSpec((local, half), lambda i, info, pos: (info[1], 0), pipeline_mode=pl.Buffered(1)),
            once(other.shape),
            once(x.shape),
            once(up.shape),
            once(gains.shape),
            once(biases.shape),
        ]
        + [hbm()] * len(parts),
        [
            full((local, d)),
            full((local, d)),
            pl.BlockSpec((tile, local), lambda i, info, pos: (i, 0)),
            pl.BlockSpec((local, tile), lambda i, info, pos: (0, i)),
            full((d, local)),
            full((local, d)),
            full((local, d)),
            full((2, d)),
            hbm(),
            hbm(),
            hbm(),
        ],
        [
            shape((local, d), BF16),
            shape((local, d), BF16),
            shape((ff, local), BF16),
            shape((local, ff), BF16),
            shape((d, local), BF16),
            shape((local, d), F32),
            shape((local, d), F32),
            shape((2, d), F32),
            shape((d, d), BF16),
            shape((d, ff), BF16),
            shape((ff, d), BF16),
        ],
        [
            pltpu.VMEM((d, d), BF16),
            pltpu.VMEM((d, ff), BF16),
            pltpu.VMEM((ff, d), BF16),
            pltpu.VMEM((local, d), BF16),
            pltpu.VMEM((local, d), F32),
            pltpu.SemaphoreType.DMA((len(parts),)),
            pltpu.SemaphoreType.DMA((3,)),
        ],
        flops=2 * local * d * (d + 2 * ff),
        moved=60e6,
    )(info, pos, attn, other, x, up, gains, biases, *parts)


def back_body(info, g_feed, n_t, act_t, slope, wd, wu, keep, send, g_two, *, fsdp):
    r = pl.program_id(0)
    f = info[0]
    tile = wd.shape[0]
    rows = n_t.shape[0] // fsdp
    width = keep.shape[2]
    piece = width // fsdp
    here = r ^ f
    g = g_feed[...]
    hid = (nt(g, wd[...]) * slope[...].astype(F32)).astype(BF16)
    down = nn(act_t[...], g).astype(BF16)
    even = r % 2 == 0

    @pl.when(even)
    def _():
        keep[r // 2, 0:tile, :] = down

    @pl.when(~even)
    def _():
        send[r // 2, 0:tile, :] = down

    lanes = pl.ds(pl.multiple_of(here * piece, 128), piece)
    for other in range(fsdp):
        shard = other ^ f
        up = nn(n_t[pl.ds(pl.multiple_of(shard * rows, 128), rows), :], hid).astype(BF16)
        target = (keep, send)[other % 2]
        for c in range(tile // piece):
            target[other // 2, tile + c * rows : tile + (c + 1) * rows, lanes] = up[:, c * piece : (c + 1) * piece]
    part = nt(hid, wu[...])

    @pl.when(r == 0)
    def _():
        g_two[...] = part

    @pl.when(r != 0)
    def _():
        g_two[...] += part


def back_group(info, g, g_feed, n_t, act_t, slope, wd, wu, fsdp):
    local, d = g_feed.shape
    ff = wd.shape[0]
    tile = ff // fsdp // GROUPS
    extra = (d // fsdp) * (fsdp * tile // d)
    block = lambda i, info: (i ^ info[0]) * GROUPS + g
    grads = shape((fsdp // 2, tile + extra, d), BF16)
    return call(
        functools.partial(back_body, fsdp=fsdp),
        (fsdp,),
        1,
        [
            full((local, d)),
            full((d, local)),
            pl.BlockSpec((tile, local), lambda i, info: (block(i, info), 0)),
            pl.BlockSpec((local, tile), lambda i, info: (0, block(i, info))),
            pl.BlockSpec((tile, d), lambda i, info: (block(i, info), 0)),
            pl.BlockSpec((d, tile), lambda i, info: (0, block(i, info))),
        ],
        [full(grads.shape), full(grads.shape), full((local, d))],
        [grads, grads, shape((local, d), F32)],
        flops=8 * local * d * tile * fsdp,
        moved=40e6,
    )(info, g_feed, n_t, act_t, slope, wd, wu)


def middle_body(
    info, ga, gb, middle, branch, up, gains, wo, own, other, g_mid, d_own, d_send, keep, send, edges, att, gbr, *, fsdp
):
    f, parity = info[0], info[1]
    step, last = pl.program_id(0), pl.num_programs(0) - 1
    half = own.shape[1]

    @pl.when(step == 0)
    def _():
        edges[...] = jnp.zeros_like(edges)
        att[:, pl.ds(pl.multiple_of(parity * half, 128), half)] = own[...]
        att[:, pl.ds(pl.multiple_of((1 - parity) * half, 128), half)] = other[...]

    g = ga[...] + gb[...]
    hat, rstd = normalise(middle[...])
    edges[2:3, :] += jnp.sum(g * hat, axis=0, keepdims=True)
    edges[3:4, :] += jnp.sum(g, axis=0, keepdims=True)
    gm = up[...].astype(F32) + norm_back(g, hat, rstd, gains[2:3, :])
    g_mid[...] = gm
    hat, rstd = normalise(branch[...])
    edges[0:1, :] += jnp.sum(gm * hat, axis=0, keepdims=True)
    edges[1:2, :] += jnp.sum(gm, axis=0, keepdims=True)
    gr = norm_back(gm, hat, rstd, gains[1:2, :]).astype(BF16)
    gbr[pl.ds(pl.multiple_of(step * gr.shape[0], 16), gr.shape[0]), :] = gr

    @pl.when(step == last)
    def _():
        grad = gbr[...]
        d_send[...] = nt(grad, wo[pl.ds(pl.multiple_of((1 - parity) * half, 128), half), :]).astype(BF16)
        d_own[...] = nt(grad, wo[pl.ds(pl.multiple_of(parity * half, 128), half), :]).astype(BF16)
        rows = keep.shape[1]
        for r in range(fsdp):
            cols = pl.ds(pl.multiple_of((r ^ f) * rows, 128), rows)
            (keep, send)[r % 2][r // 2] = tn(att[:, cols], grad).astype(BF16)


def middle_back(info, ga, gb, middle, branch, up, gains, wo, attn, half, other, fsdp):
    local, d = ga.shape
    rows = 128
    block = pl.BlockSpec((rows, d), lambda i, info: (i, 0))
    grads = shape((fsdp // 2, d // fsdp, d), BF16)
    return call(
        functools.partial(middle_body, fsdp=fsdp),
        (local // rows,),
        1,
        [block, block, block, block, block, full(gains.shape), full(wo.shape)]
        + [pl.BlockSpec((local, half), lambda i, info: (info[1], 0)), full(other.shape)],
        [block, full((local, half)), full((local, half)), full(grads.shape), full(grads.shape), full((4, d))],
        [shape((local, d), F32), shape((local, half), BF16), shape((local, half), BF16), grads, grads, shape((4, d), F32)],
        [pltpu.VMEM((local, d), BF16), pltpu.VMEM((local, d), BF16)],
        flops=4 * local * d * d,
        moved=22e6,
    )(info, ga, gb, middle, branch, up, gains, wo, attn, other)


def project_back_body(
    info, own, head, rest, padx, gains, dq, dk, dv, dkp, dvp, w, n_t, np_t, g_own, g_send, g_pad, keep, send, edges, *, fsdp
):
    f, parity = info[0], info[1]
    step = pl.program_id(0)
    local = own.shape[0]
    half = dq.shape[1]
    gain = gains[0:1, :]

    def through(at):
        return (
            nt(dq[at, :], w[:, 0:half])
            + nt(dk[at, :], w[:, half : 2 * half])
            + nt(dv[at, :], w[:, 2 * half :])
        )

    @pl.when(step == 0)
    def _():
        g = nt(dkp[...], w[:, half : 2 * half]) + nt(dvp[...], w[:, 2 * half :])
        g_pad[...] = g.astype(BF16)
        hat, _ = normalise(padx[...].astype(F32))
        edges[0:1, :] = jnp.sum(g * hat, axis=0, keepdims=True)
        edges[1:2, :] = jnp.sum(g, axis=0, keepdims=True)
        g = through(pl.ds(pl.multiple_of((1 - parity) * local, 128), local))
        g_send[...] = g.astype(BF16)
        hat, _ = normalise(jnp.concatenate([head[...], rest[...]], axis=0).astype(F32))
        edges[0:1, :] += jnp.sum(g * hat, axis=0, keepdims=True)
        edges[1:2, :] += jnp.sum(g, axis=0, keepdims=True)

    @pl.when(step == 1)
    def _():
        g = through(pl.ds(pl.multiple_of(parity * local, 128), local))
        g_own[...] = g
        hat, _ = normalise(own[...].astype(F32))
        edges[0:1, :] += jnp.sum(g * hat, axis=0, keepdims=True)
        edges[1:2, :] += jnp.sum(g, axis=0, keepdims=True)
        rows = keep.shape[1]
        for r in range(fsdp):
            at = pl.ds(pl.multiple_of((r ^ f) * rows, 128), rows)
            target = (keep, send)[r % 2]
            left, pads = n_t[at, :], np_t[at, :]
            target[r // 2, :, 0:half] = nn(left, dq[...]).astype(BF16)
            target[r // 2, :, half : 2 * half] = (nn(left, dk[...]) + nn(pads, dkp[...])).astype(BF16)
            target[r // 2, :, 2 * half :] = (nn(left, dv[...]) + nn(pads, dvp[...])).astype(BF16)


def project_back(info, own, head, rest, padx, gains, dq, dk, dv, dkp, dvp, w, n_t, np_t, fsdp):
    local, d = own.shape
    wide = w.shape[1]
    pads = padx.shape[0]
    grads = shape((fsdp // 2, d // fsdp, wide), BF16)
    arrays = (own, head, rest, padx, gains, dq, dk, dv, dkp, dvp, w, n_t, np_t)
    return call(
        functools.partial(project_back_body, fsdp=fsdp),
        (2,),
        1,
        [pl.BlockSpec(a.shape, lambda *_: (0, 0), pipeline_mode=pl.Buffered(1)) for a in arrays],
        [full((local, d)), full((local, d)), full((pads, d)), full(grads.shape), full(grads.shape), full((2, d))],
        [shape((local, d), F32), shape((local, d), BF16), shape((pads, d), BF16), grads, grads, shape((2, d), F32)],
        flops=8 * local * d * wide,
        moved=24e6,
    )(info, *arrays)


def finish_body(info, x, g_own, g_other, pad_a, pad_b, g_mid, gains, out, total):
    s, start, cut = info[6], info[7], info[8]
    row = lax.broadcasted_iota(jnp.int32, (pad_a.shape[0], 1), 0)
    mine = ((s == 0) & (row < start)) | ((s == 1) & (row >= cut))
    extra = jnp.where(mine, pad_a[...].astype(F32) + pad_b[...].astype(F32), 0.0)
    total[...] = g_own[...] + g_other[...].astype(F32)
    at = pl.ds(pl.multiple_of(jnp.where(s == 0, 0, total.shape[0] - pad_a.shape[0]), 128), pad_a.shape[0])
    total[at, :] += extra

    def rows(i, carry):
        at = pl.ds(pl.multiple_of(i * 128, 128), 128)
        hat, rstd = normalise(x[at, :].astype(F32))
        out[at, :] = (g_mid[at, :] + norm_back(total[at, :], hat, rstd, gains[0:1, :])).astype(BF16)
        return carry

    lax.fori_loop(0, x.shape[0] // 128, rows, 0)


def finish(info, x, g_own, g_other, pad_a, pad_b, g_mid, gains):
    arrays = (x, g_own, g_other, pad_a, pad_b, g_mid, gains)
    return call(
        finish_body,
        (1,),
        1,
        [full(a.shape) for a in arrays],
        full(x.shape),
        shape(x.shape, BF16),
        [pltpu.VMEM(x.shape, F32)],
        flops=1e7,
        moved=12e6,
    )(info, *arrays)


def peer(axis, mask):
    return {axis: lax.axis_index(axis) ^ mask}


def greet(partners):
    barrier = pltpu.get_barrier_semaphore()
    for p in partners:
        pl.semaphore_signal(barrier, inc=1, device_id=p, device_id_type=pl.DeviceIdType.MESH)
    pl.semaphore_wait(barrier, len(partners))


def remote(src, dst, send, recv, to):
    return pltpu.make_async_remote_copy(
        src_ref=src, dst_ref=dst, send_sem=send, recv_sem=recv, device_id=to, device_id_type=pl.DeviceIdType.MESH
    )


class Lane:
    names = ("core_s", "core_r", "y_s", "y_r", "x_s", "x_r", "z_s", "z_r", "zz_s", "zz_r", "xx_s", "xx_r", "own")

    @staticmethod
    def scratch(count, rows, cols, fsdp, dp, masks):
        y, parts = fsdp // 2, len(masks) + 1
        dma = pltpu.SemaphoreType.DMA
        sems = [(count,), (count,)]
        sems += [(count, max(y - 1, 1))] * 2 + [(count, max(dp - 1, 1))] * 2
        sems += [(count, len(masks))] * 4 + [(count, max(dp - 1, 1))] * 2 + [(count,)]
        return [
            pltpu.VMEM((count, y, rows, cols), BF16),
            pltpu.VMEM((count, max(y - 1, 1), rows, cols), BF16),
            pltpu.VMEM((count, max(dp - 1, 1), rows // dp, cols), BF16),
            pltpu.VMEM((count, len(masks), rows // dp, cols // parts), BF16),
        ] + [dma(s) for s in sems]

    size = 4 + 13

    def __init__(self, refs, final, fsdp, dp, masks, unit):
        self.acc, self.y_in, self.x_in, self.z_in = refs[:4]
        self.sems = dict(zip(self.names, refs[4:]))
        self.final = final
        self.ys, self.dp, self.masks = fsdp // 2, dp, masks
        self.count, _, self.rows, self.cols = self.acc.shape
        self.x = lax.axis_index("dp")
        self.part = self.cols // (len(masks) + 1)
        self.unit = unit

    def place(self, mask=0):
        at = (lax.axis_index("seq") ^ mask) // self.unit % (len(self.masks) + 1)
        return pl.ds(pl.multiple_of(at * self.part, 128), self.part)

    def band(self, mask=0):
        n = self.rows // self.dp
        return pl.ds(pl.multiple_of((self.x ^ mask) * n, 16), n)

    def core(self, u, src):
        return remote(src, self.acc.at[u], self.sems["core_s"].at[u], self.sems["core_r"].at[u], peer("fsdp", 1))

    def over_y(self, u, ry):
        s = self.sems
        return remote(
            self.acc.at[u, ry], self.y_in.at[u, ry - 1], s["y_s"].at[u, ry - 1], s["y_r"].at[u, ry - 1], peer("fsdp", 2 * ry)
        )

    def over_x(self, u, rx):
        s = self.sems
        return remote(
            self.acc.at[u, 0, self.band(rx)],
            self.x_in.at[u, rx - 1],
            s["x_s"].at[u, rx - 1],
            s["x_r"].at[u, rx - 1],
            peer("dp", rx),
        )

    def over_z(self, u, i):
        s, m = self.sems, self.masks[i]
        return remote(
            self.acc.at[u, 0, self.band(), self.place(m)],
            self.z_in.at[u, i],
            s["z_s"].at[u, i],
            s["z_r"].at[u, i],
            peer("seq", m),
        )

    def back_z(self, u, i):
        s, m = self.sems, self.masks[i]
        return remote(
            self.acc.at[u, 0, self.band(), self.place()],
            self.final.at[u, self.band(), self.place()],
            s["zz_s"].at[u, i],
            s["zz_r"].at[u, i],
            peer("seq", m),
        )

    def back_x(self, u, rx):
        s = self.sems
        at = self.final.at[u, self.band()]
        return remote(at, at, s["xx_s"].at[u, rx - 1], s["xx_r"].at[u, rx - 1], peer("dp", rx))

    def keep(self, u):
        return pltpu.make_async_copy(
            self.acc.at[u, 0, self.band(), self.place()],
            self.final.at[u, self.band(), self.place()],
            self.sems["own"].at[u],
        )

    def add(self, target, sources):
        rows = target.shape[0]
        step = 64 if rows % 64 == 0 else 16

        def body(i, carry):
            at = pl.ds(pl.multiple_of(i * step, 16), step)
            total = target[at, :].astype(F32)
            for src in sources:
                total = total + src[at, :].astype(F32)
            target[at, :] = total.astype(BF16)
            return carry

        lax.fori_loop(0, rows // step, body, 0)

    def one(self, u, keep):
        self.core(u, keep).wait_recv()
        for ry in range(self.ys):
            self.add(self.acc.at[u, ry], [keep.at[ry]])
        for ry in range(1, self.ys):
            self.over_y(u, ry).start()

    def two(self, u):
        for ry in range(1, self.ys):
            self.over_y(u, ry).wait_recv()
        self.add(self.acc.at[u, 0], [self.y_in.at[u, ry - 1] for ry in range(1, self.ys)])
        for rx in range(1, self.dp):
            self.over_x(u, rx).start()

    def three(self, u):
        for rx in range(1, self.dp):
            self.over_x(u, rx).wait_recv()
        self.add(self.acc.at[u, 0, self.band()], [self.x_in.at[u, rx - 1] for rx in range(1, self.dp)])
        for i in range(len(self.masks)):
            self.over_z(u, i).start()

    def four(self, u):
        for i in range(len(self.masks)):
            self.over_z(u, i).wait_recv()
        self.add(
            self.acc.at[u, 0, self.band(), self.place()], [self.z_in.at[u, i] for i in range(len(self.masks))]
        )
        self.keep(u).start()
        for i in range(len(self.masks)):
            self.back_z(u, i).start()

    def five(self, u):
        self.keep(u).wait()
        for i in range(len(self.masks)):
            self.back_z(u, i).wait_recv()
        for rx in range(1, self.dp):
            self.back_x(u, rx).start()

    def six(self, u):
        for rx in range(1, self.dp):
            self.back_x(u, rx).wait_recv()

    def drain(self, u, src):
        self.core(u, src).wait_send()
        for ry in range(1, self.ys):
            self.over_y(u, ry).wait_send()
        for rx in range(1, self.dp):
            self.over_x(u, rx).wait_send()
            self.back_x(u, rx).wait_send()
        for i in range(len(self.masks)):
            self.over_z(u, i).wait_send()
            self.back_z(u, i).wait_send()


def partners(fsdp, dp):
    return (
        [peer("fsdp", 1)]
        + [peer("fsdp", 2 * ry) for ry in range(1, fsdp // 2)]
        + [peer("dp", rx) for rx in range(1, dp)]
        + [peer("seq", m) for m in (1, 2, 3)]
    )


def reduce_body(*refs, fsdp, dp, layout):
    n_in = len(layout)
    keeps, sends = refs[:n_in], refs[n_in : 2 * n_in]
    final_a, final_b = refs[2 * n_in : 2 * n_in + 2]
    rest = refs[2 * n_in + 2 :]
    held_a, held_b, load_a, load_b = rest[:4]
    a = Lane(rest[4 : 4 + Lane.size], final_a, fsdp, dp, (1, 2, 3), 1)
    b = Lane(rest[4 + Lane.size :], final_b, fsdp, dp, (2,), 2)
    greet(partners(fsdp, dp))

    def views(lane, held, load):
        u = 0
        for i, (kind, cuts) in enumerate(layout):
            if kind != (lane is b):
                continue
            for cut in range(cuts):
                if kind:
                    at = (slice(None), slice(None), pl.ds(cut * lane.cols, lane.cols))
                else:
                    at = (slice(None), pl.ds(cut * lane.rows, lane.rows))
                yield u, sends[i].at[at], functools.partial(
                    pltpu.make_async_copy, keeps[i].at[at], held.at[u], load.at[u]
                )
                u += 1

    lanes = ((a, held_a, load_a), (b, held_b, load_b))
    for lane, held, load in lanes:
        for u, src, copy in views(lane, held, load):
            lane.core(u, src).start()
            copy().start()
    for lane, held, load in lanes:
        for u, src, copy in views(lane, held, load):
            copy().wait()
    total = a.count + b.count

    def tick(t, carry):
        for offset, name in ((0, "one"), (2, "two"), (3, "three"), (4, "four"), (5, "five"), (6, "six")):
            for lane, held, first in ((a, held_a, 0), (b, held_b, a.count)):
                u = t - offset - first

                @pl.when((u >= 0) & (u < lane.count))
                def _():
                    if name == "one":
                        lane.one(u, held.at[u])
                    else:
                        getattr(lane, name)(u)

        return carry

    lax.fori_loop(0, total + 6, tick, 0)
    for lane, held, load in lanes:
        for u, src, copy in views(lane, held, load):
            lane.drain(u, src)


def reduce_all(pairs, fsdp, dp):
    d = pairs[0][0].shape[2]
    rows = d // fsdp
    layout = tuple((False, k.shape[1] // rows) for k, _ in pairs[:-1]) + ((True, 3),)
    n_a = sum(c for kind, c in layout if not kind)
    wide = pairs[-1][0].shape[2] // 3
    y = fsdp // 2
    return pl.pallas_call(
        functools.partial(reduce_body, fsdp=fsdp, dp=dp, layout=layout),
        in_specs=[hbm()] * (2 * len(pairs)),
        out_specs=[hbm(), hbm()],
        out_shape=[shape((n_a, rows, d), BF16), shape((3, rows, wide), BF16)],
        scratch_shapes=[
            pltpu.VMEM((n_a, y, rows, d), BF16),
            pltpu.VMEM((3, y, rows, wide), BF16),
            pltpu.SemaphoreType.DMA((n_a,)),
            pltpu.SemaphoreType.DMA((3,)),
        ]
        + Lane.scratch(n_a, rows, d, fsdp, dp, (1, 2, 3))
        + Lane.scratch(3, rows, wide, fsdp, dp, (2,)),
        compiler_params=pltpu.CompilerParams(vmem_limit_bytes=VMEM_LIMIT, collective_id=0, has_side_effects=True),
        cost_estimate=pl.CostEstimate(flops=10**8, bytes_accessed=5 * 10**8, transcendentals=0),
    )(*[k for k, _ in pairs], *[s for _, s in pairs])


def hop(value, axis, mask):
    return lax.ppermute(value, axis, [(i, i ^ mask) for i in range(lax.axis_size(axis))])


def arrange(pieces, index):
    count = len(pieces)
    if count == 1:
        return list(pieces)
    half = count // 2
    low, high = arrange(pieces[:half], index), arrange(pieces[half:], index)
    bit = (index & half) != 0
    return [jnp.where(bit, b, a) for a, b in zip(low, high)] + [jnp.where(bit, a, b) for a, b in zip(low, high)]


def part_of(value, count, index):
    rows = value.shape[0] // count
    return lax.dynamic_slice_in_dim(value, index * rows, rows, 0)


def gather_weight(w, f, x):
    fsdp, dp = lax.axis_size("fsdp"), lax.axis_size("dp")
    rows = w.shape[0]
    sub = rows // dp
    pieces, places = [w, hop(w, "fsdp", 1)], [f * rows, (f ^ 1) * rows]
    mine = part_of(w, dp, x)
    for ry in range(1, fsdp // 2):
        first = hop(mine, "fsdp", 2 * ry)
        for rx in range(dp):
            got = first if rx == 0 else hop(first, "dp", rx)
            pieces += [got, hop(got, "fsdp", 1)]
            place = (x ^ rx) * sub
            places += [(f ^ (2 * ry)) * rows + place, (f ^ (2 * ry + 1)) * rows + place]
    return pieces, places


def gather_half(w, f):
    fsdp = lax.axis_size("fsdp")
    rows = w.shape[0]
    pieces, places = [], []
    for ry in range(fsdp // 2):
        got = w if ry == 0 else hop(w, "fsdp", 2 * ry)
        pieces += [got, hop(got, "fsdp", 1)]
        places += [(f ^ (2 * ry)) * rows, (f ^ (2 * ry + 1)) * rows]
    return pieces, places


def sum_all(value):
    for axis in ("fsdp", "dp", "seq"):
        m = 1
        while m < lax.axis_size(axis):
            value = value + hop(value, axis, m)
            m *= 2
    return value


def local(
    tokens, qkv_weight, out_weight, up_weight, down_weight, norm_gain, norm_bias, caption_len, item_start, grad_out
):
    x_tok, up = tokens[0], grad_out[0]
    local_rows, d = x_tok.shape
    fsdp = lax.axis_size("fsdp")
    ff = up_weight.shape[1]
    half = d // 2
    f, x, s = lax.axis_index("fsdp"), lax.axis_index("dp"), lax.axis_index("seq")
    parity, slot = s % 2, s // 2
    caps, starts = caption_len[0], item_start[0]
    start = jnp.where(slot == 0, starts[0], starts[1] - SLOT)
    stop = start + jnp.where(slot == 0, caps[0], caps[1]) + IMAGE
    pad_a = jnp.where(slot == 0, 0, starts[0])
    pad_b = jnp.where(slot == 0, BLK, starts[0] + caps[0])
    info = jnp.stack(
        [f, parity, start, stop, pad_a, pad_b, s, starts[0], starts[0] + caps[0]]
    ).astype(jnp.int32)

    head = hop(x_tok[:BLK], "seq", 1)
    rest = hop(x_tok[BLK:], "seq", 1)
    index = lax.broadcasted_iota(jnp.int32, (BLK, 1), 0)
    pads = jnp.where(index < starts[0], head, x_tok[local_rows - BLK :])
    pads = lax.ppermute(pads, "seq", [(1, 2)])
    pads = jnp.where(s == 3, lax.ppermute(pads, "seq", [(2, 3)]), pads)

    w_half = jnp.concatenate(
        [lax.dynamic_slice_in_dim(qkv_weight, c * d + parity * half, half, 1) for c in range(3)], axis=1
    )
    parts, places = gather_half(w_half, f)
    gain0, bias0 = norm_gain[0:1], norm_bias[0:1]
    q, k, v, n_t, w_qkv = project(
        info, jnp.stack(places).astype(jnp.int32), x_tok, head, rest, gain0, bias0, parts
    )
    kp, vp, np_t = pad_project(pads, gain0, bias0, w_qkv)
    mixed, lse = attend(info, q, k, v, kp, vp)
    to_send = lax.dynamic_slice_in_dim(mixed, (1 - parity) * local_rows, local_rows, 0)
    other = hop(to_send, "seq", 1)

    parts, places, counts = [], [], []
    for w in (out_weight, up_weight, down_weight):
        got, at = gather_weight(w, f, x)
        parts += got
        places += at
        counts.append(len(got))
    (out, g_feed, act_t, slope, two_t, branch, middle, edges3, wo, wu, wd) = forward(
        info,
        jnp.stack(places).astype(jnp.int32),
        (mixed, half, parity),
        other,
        x_tok,
        up,
        norm_gain,
        norm_bias,
        parts,
        tuple(counts),
        ff,
    )
    keeps, g_twos = [], []
    for g in range(GROUPS):
        keep, send, g_two = back_group(info, g, g_feed, two_t, act_t, slope, wd, wu, fsdp)
        keeps.append((keep, send))
        g_twos.append(g_two)
    g_mid, d_own, d_send, keep_o, send_o, edges12 = middle_back(
        info, g_twos[0], g_twos[1], middle, branch, up, norm_gain, wo, mixed, half, other, fsdp
    )
    d_other = hop(d_send, "seq", 1)
    dq, dk, dv, dkp, dvp = attend_back(info, q, k, v, kp, vp, mixed, lse, d_own, d_other)
    g_own, g_send, g_pad, keep_q, send_q, edges0 = project_back(
        info, x_tok, head, rest, pads, norm_gain, dq, dk, dv, dkp, dvp, w_qkv, n_t, np_t, fsdp
    )
    g_other = hop(g_send, "seq", 1)
    back_a = lax.ppermute(g_pad, "seq", [(2, 0), (3, 1)])
    back_b = lax.ppermute(g_pad, "seq", [(2, 1), (3, 0)])
    grad_in = finish(info, x_tok, g_own, g_other, back_a, back_b, g_mid, norm_gain)

    sums = sum_all(
        jnp.stack(
            [edges0[0], edges12[0], edges12[2], edges3[0], edges0[1], edges12[1], edges12[3], edges3[1]]
        )
    )

    dp = lax.axis_size("dp")
    done, done_q = reduce_all(keeps + [(keep_o, send_o), (keep_q, send_q)], fsdp, dp)
    rows = d // fsdp
    per = (done.shape[0] - 1) // GROUPS
    reduced = [done[g * per : (g + 1) * per].reshape(per * rows, d) for g in range(GROUPS)]
    grad_proj = done[-1].astype(F32)
    half_q = jnp.concatenate([done_q[0], done_q[1], done_q[2]], axis=1)
    both = arrange([half_q, hop(half_q, "seq", 1)], parity)
    grad_qkv = jnp.concatenate(
        [both[h][:, c * half : (c + 1) * half] for c in range(3) for h in range(2)], axis=1
    ).astype(F32)
    tile = ff // fsdp // GROUPS
    grad_down = jnp.concatenate([r[:tile] for r in reduced], axis=0).astype(F32)
    piece = d // fsdp
    blocks = []
    for h in range(fsdp):
        for r in reduced:
            for c in range(tile // piece):
                blocks.append(r[tile + c * rows : tile + (c + 1) * rows, h * piece : (h + 1) * piece])
    grad_up = jnp.concatenate(blocks, axis=1).astype(F32)
    return (out[None], grad_in[None], grad_qkv, grad_proj, grad_up, grad_down, sums[0:4], sums[4:8])


def solution(mesh):
    rows = P(("fsdp", "dp"), "seq", None)
    shard = P("fsdp", None)
    items = P(("fsdp", "dp"), None)
    return jax.shard_map(
        local,
        mesh=mesh,
        in_specs=(rows, shard, shard, shard, shard, P(), P(), items, items, rows),
        out_specs=(rows, rows, shard, shard, shard, shard, P(), P()),
        check_vma=False,
    )
```

```python
import functools

import jax
import jax.numpy as jnp
from jax import lax
from jax.experimental import pallas as pl
from jax.experimental.pallas import tpu as pltpu
from jax.sharding import PartitionSpec as P

HD = 64
IMAGE = 1024
SLOT = 1280
BLK = 256
LOG2E = 1.4426950408889634
SCALE = LOG2E / 8.0
NEG = -1e30
F32 = jnp.float32
BF16 = jnp.bfloat16
VMEM_LIMIT = 60 * 1024 * 1024
GROUPS = 2


def nn(a, b):
    return lax.dot_general(a, b, (((1,), (0,)), ((), ())), preferred_element_type=F32)


def nt(a, b):
    return lax.dot_general(a, b, (((1,), (1,)), ((), ())), preferred_element_type=F32)


def tn(a, b):
    return lax.dot_general(a, b, (((0,), (0,)), ((), ())), preferred_element_type=F32)


def normalise(v):
    mean = jnp.mean(v, axis=-1, keepdims=True)
    centred = v - mean
    var = jnp.mean(centred * centred, axis=-1, keepdims=True)
    rstd = lax.rsqrt(var + 1e-05)
    return centred * rstd, rstd


def norm_back(g, hat, rstd, gain):
    gg = g * gain
    return rstd * (
        gg - jnp.mean(gg, axis=-1, keepdims=True) - hat * jnp.mean(gg * hat, axis=-1, keepdims=True)
    )


def call(body, grid, prefetch, in_specs, out_specs, out_shape, scratch=(), flops=0, moved=0):
    return pl.pallas_call(
        body,
        grid_spec=pltpu.PrefetchScalarGridSpec(
            num_scalar_prefetch=prefetch,
            grid=grid,
            in_specs=in_specs,
            out_specs=out_specs,
            scratch_shapes=list(scratch),
        ),
        out_shape=out_shape,
        compiler_params=pltpu.CompilerParams(vmem_limit_bytes=VMEM_LIMIT),
        cost_estimate=pl.CostEstimate(flops=int(flops), bytes_accessed=int(moved), transcendentals=0),
    )


def full(shape):
    zeros = (0,) * len(shape)
    return pl.BlockSpec(shape, lambda *_: zeros)


def hbm():
    return pl.BlockSpec(memory_space=pl.ANY)


def shape(dims, dtype):
    return jax.ShapeDtypeStruct(dims, dtype)


def attend_pair(bounds, q, k, v, kp, vp, o, lse):
    start, stop, pad_a, pad_b = bounds
    lane = lax.broadcasted_iota(jnp.int32, (1, 2 * HD), 1)
    row = lax.broadcasted_iota(jnp.int32, (BLK, 1), 0)
    col = lax.broadcasted_iota(jnp.int32, (1, BLK), 1)
    causal = col <= row
    pad_col = (col < pad_a) | (col >= pad_b)
    count = SLOT // BLK
    for i in range(count):
        n = (i + 1) * BLK
        qi = q(slice(i * BLK, n))
        edge = i in (0, count - 1)
        pos_q = row + i * BLK
        in_q = (pos_q >= start) & (pos_q < stop)
        masks = []
        for j in range(i + 1):
            pos_k = col + j * BLK
            mask = None
            if edge:
                in_k = (pos_k >= start) & (pos_k < stop)
                mask = (in_q & in_k) | (~in_q & ~in_k)
            elif j == 0:
                mask = jnp.broadcast_to(pos_k >= start, (BLK, BLK))
            if j == i:
                mask = causal if mask is None else mask & causal
            masks.append(mask)
        outs = []
        for h in range(2):
            qh = jnp.where(lane // HD == h, qi, jnp.zeros_like(qi))
            blocks = []
            for j in range(i + 1):
                s = nt(qh, k(slice(j * BLK, (j + 1) * BLK))) * SCALE
                if masks[j] is not None:
                    s = jnp.where(masks[j], s, NEG)
                blocks.append(s)
            if edge:
                s = nt(qh, kp(slice(None))) * SCALE
                blocks.append(jnp.where(~in_q & pad_col, s, NEG))
            top = functools.reduce(jnp.maximum, blocks)
            top = jnp.max(top, axis=1, keepdims=True)
            probs = [jnp.exp2(s - top) for s in blocks]
            total = jnp.sum(functools.reduce(jnp.add, probs), axis=1, keepdims=True)
            probs = [x.astype(BF16) for x in probs]
            mixed = nn(jnp.concatenate(probs[: i + 1], axis=1), v(slice(0, n)))
            if edge:
                mixed = mixed + nn(probs[-1], vp(slice(None)))
            outs.append(mixed * (1.0 / total))
            level = jnp.broadcast_to(top + jnp.log2(total), (BLK, 128))
            lse(h, slice(i * BLK, n), level.T[0:1, :])
        o(slice(i * BLK, n), jnp.where(lane < HD, outs[0], outs[1]).astype(BF16))


def attend_back_body(
    info, q, k, v, kp, vp, o, lse, d_own, d_other, dq, dk, dv, dkp, dvp, do, dk_sum, dv_sum, dkp_sum, dvp_sum
):
    parity, start, stop, pad_a, pad_b = info[1], info[2], info[3], info[4], info[5]
    local = d_own.shape[0]
    do[pl.ds(pl.multiple_of(parity * local, 128), local), :] = d_own[...]
    do[pl.ds(pl.multiple_of((1 - parity) * local, 128), local), :] = d_other[...]
    lane = lax.broadcasted_iota(jnp.int32, (1, 2 * HD), 1)
    pick = (
        lax.broadcasted_iota(jnp.int32, (8, 2 * HD), 1) // HD
        == lax.broadcasted_iota(jnp.int32, (8, 2 * HD), 0)
    ).astype(F32)
    inner = lax.dot_general(
        pick,
        do[...].astype(F32) * o[...].astype(F32),
        (((1,), (1,)), ((), ())),
        precision=lax.Precision.HIGHEST,
        preferred_element_type=F32,
    )
    row = lax.broadcasted_iota(jnp.int32, (BLK, 1), 0)
    col = lax.broadcasted_iota(jnp.int32, (1, 2 * BLK), 1) % BLK
    causal = row <= col
    pad_row = (row < pad_a) | (row >= pad_b)
    dk_sum[...] = jnp.zeros_like(dk_sum)
    dv_sum[...] = jnp.zeros_like(dv_sum)
    dkp_sum[...] = jnp.zeros_like(dkp_sum)
    dvp_sum[...] = jnp.zeros_like(dvp_sum)
    count = SLOT // BLK

    def split(x):
        zero = jnp.zeros_like(x)
        return [jnp.where(lane // HD == h, x, zero) for h in range(2)]

    for i in range(count):
        rows = slice(i * BLK, (i + 1) * BLK)
        qs = jnp.concatenate(split(q[rows, :]), axis=0)
        ds = jnp.concatenate(split(do[rows, :]), axis=0)
        level = jnp.concatenate([lse[0, 0:1, rows], lse[0, 1:2, rows]], axis=1)
        inner_i = jnp.concatenate([inner[0:1, rows], inner[1:2, rows]], axis=1)
        edge = i in (0, count - 1)
        pos_q = col + i * BLK
        in_q = (pos_q >= start) & (pos_q < stop)
        dq_sum = jnp.zeros((BLK, 2 * HD), F32)

        def block(kj, vj, mask):
            s = nt(kj, qs) * SCALE - level
            if mask is not None:
                s = jnp.where(mask, s, NEG)
            p = jnp.exp2(s)
            g = p * (nt(vj, ds) - inner_i)
            p, g = p.astype(BF16), g.astype(BF16)
            halves = split(kj)
            part = tn(g[:, :BLK], halves[0]) + tn(g[:, BLK:], halves[1])
            return nn(g, qs), nn(p, ds), part

        for j in range(i + 1):
            keys = slice(j * BLK, (j + 1) * BLK)
            pos_k = row + j * BLK
            mask = None
            if edge:
                in_k = (pos_k >= start) & (pos_k < stop)
                mask = (in_q & in_k) | (~in_q & ~in_k)
            elif j == 0:
                mask = jnp.broadcast_to(pos_k >= start, (BLK, 2 * BLK))
            if j == i:
                mask = causal if mask is None else mask & causal
            gk, gv, part = block(k[keys, :], v[keys, :], mask)
            dk_sum[keys, :] += gk
            dv_sum[keys, :] += gv
            dq_sum = dq_sum + part
        if edge:
            gk, gv, part = block(kp[...], vp[...], ~in_q & pad_row)
            dkp_sum[...] += gk
            dvp_sum[...] += gv
            dq_sum = dq_sum + part
        dq[rows, :] = (dq_sum * 0.125).astype(BF16)
    dk[...] = (dk_sum[...] * 0.125).astype(BF16)
    dv[...] = dv_sum[...].astype(BF16)
    dkp[...] = (dkp_sum[...] * 0.125).astype(BF16)
    dvp[...] = dvp_sum[...].astype(BF16)


def attend_back(info, q, k, v, kp, vp, o, lse, d_own, d_other):
    rows, half = q.shape
    pads = kp.shape[0]
    pairs = half // (2 * HD)
    pick = lambda n: pl.BlockSpec((n, 2 * HD), lambda i, info: (0, i))
    pair, pad, part = pick(rows), pick(pads), pick(d_own.shape[0])
    return call(
        attend_back_body,
        (pairs,),
        1,
        [pair, pair, pair, pad, pad, pair, pl.BlockSpec((1, 2, rows), lambda i, info: (i, 0, 0)), part, part],
        [pair, pair, pair, pad, pad],
        [shape((rows, half), BF16)] * 3 + [shape((pads, half), BF16)] * 2,
        [
            pltpu.VMEM((rows, 2 * HD), BF16),
            pltpu.VMEM((rows, 2 * HD), F32),
            pltpu.VMEM((rows, 2 * HD), F32),
            pltpu.VMEM((pads, 2 * HD), F32),
            pltpu.VMEM((pads, 2 * HD), F32),
        ],
        flops=pairs * 34 * BLK * BLK * 256 * 10,
        moved=14e6,
    )(info, q, k, v, kp, vp, o, lse, d_own, d_other)


def peer(axis, mask):
    return {axis: lax.axis_index(axis) ^ mask}


def greet(partners):
    barrier = pltpu.get_barrier_semaphore()
    for p in partners:
        pl.semaphore_signal(barrier, inc=1, device_id=p, device_id_type=pl.DeviceIdType.MESH)
    pl.semaphore_wait(barrier, len(partners))


def remote(src, dst, send, recv, to):
    return pltpu.make_async_remote_copy(
        src_ref=src, dst_ref=dst, send_sem=send, recv_sem=recv, device_id=to, device_id_type=pl.DeviceIdType.MESH
    )


def front_body(
    info, tokens, wqkv, wo, wu, wd, gain, bias,
    q_out, k_out, v_out, n_out, np_out, kp_out, vp_out, w_out, mix_out, lse_out, other, tok_out, pad_out, wo_all, wu_all, wd_all,
    mine, theirs, pads, made, w, normed, n_t, np_t, q, k, v, kp, vp, mixed, held_o, held_u, held_d, lse,
    tok_l, tok_s, tok_r, pad_s, pad_r, q_l, q_cs, q_cr, q_ys, q_yr, q_fs, q_fr,
    h_l, s_l, s_cs, s_cr, y_s, y_r, x_s, x_r, fy_s, fy_r, fx_s, fx_r, o_s, o_r, out_l,
    *, fsdp, dp
):
    f, x, s = lax.axis_index("fsdp"), lax.axis_index("dp"), lax.axis_index("seq")
    parity = s % 2
    local, d = tokens.shape
    half = d // 2
    ys = fsdp // 2
    bounds = tuple(info[i] for i in range(2, 6))
    core, mate = peer("fsdp", 1), peer("seq", 1)
    greet(
        [core]
        + [peer("fsdp", 2 * r) for r in range(1, ys)]
        + [peer("dp", r) for r in range(1, dp)]
        + [mate, peer("seq", 3)]
    )

    cuts = ((0, BLK), (BLK, local - BLK))

    def token(i):
        at = pl.ds(*cuts[i])
        return remote(tokens.at[at], theirs.at[at], tok_s.at[i], tok_r.at[i], mate)

    load = pltpu.make_async_copy(tokens, mine, tok_l.at[0])
    load.start()
    token(0).start()
    token(1).start()

    rows = wqkv.shape[0]

    def band(r):
        return pl.ds(pl.multiple_of((f ^ r) * rows, 16), rows)

    def source(c):
        return wqkv.at[:, pl.ds(pl.multiple_of(c * d + parity * half, 128), half)]

    def cols(c):
        return pl.ds(c * half, half)

    def q_local(c):
        return pltpu.make_async_copy(source(c), w.at[band(0), cols(c)], q_l.at[c])

    def q_core(c):
        return remote(source(c), w.at[band(0), cols(c)], q_cs.at[c], q_cr.at[c], core)

    def q_y(c, r):
        at = (c, r - 1)
        return remote(source(c), w.at[band(0), cols(c)], q_ys.at[at], q_yr.at[at], peer("fsdp", 2 * r))

    def q_far(c, r):
        at = (c, r - 1)
        here = w.at[band(2 * r), cols(c)]
        return remote(here, here, q_fs.at[at], q_fr.at[at], core)

    for c in range(3):
        for r in range(1, ys):
            q_y(c, r).start()
        q_core(c).start()
        q_local(c).start()

    shards, wholes = (held_o, held_u, held_d), (wo_all, wu_all, wd_all)

    def hold(i):
        return pltpu.make_async_copy((wo, wu, wd)[i], shards[i], h_l.at[i])

    def whole_shard(i):
        n = shards[i].shape[0]
        return wholes[i].at[pl.ds(pl.multiple_of(f * n, 16), n)]

    def s_local(i):
        return pltpu.make_async_copy(shards[i], whole_shard(i), s_l.at[i])

    def s_core(i):
        return remote(shards[i], whole_shard(i), s_cs.at[i], s_cr.at[i], core)

    units = [(0, 0)] + [(1, j) for j in range(4)] + [(2, j) for j in range(4)]

    def piece(u, owner, part, shard=False):
        which, j = units[u]
        n = shards[which].shape[0]
        sub = n // dp
        base = part * sub if shard else owner * n + part * sub
        ref = shards[which] if shard else wholes[which]
        if which == 0:
            return ref.at[pl.ds(pl.multiple_of(base, 16), sub)]
        if which == 1:
            wide = ref.shape[1] // 4
            return ref.at[pl.ds(pl.multiple_of(base, 16), sub), pl.ds(j * wide, wide)]
        return ref.at[pl.ds(pl.multiple_of(base + j * (sub // 4), 16), sub // 4)]

    def w_y(u, r):
        at = (u, r - 1)
        return remote(piece(u, f, x, True), piece(u, f, x), y_s.at[at], y_r.at[at], peer("fsdp", 2 * r))

    def w_x(u, r, t):
        at = (u, r - 1, t - 1)
        here = piece(u, f ^ (2 * r), x)
        return remote(here, here, x_s.at[at], x_r.at[at], peer("dp", t))

    def w_fy(u, r):
        at = (u, r - 1)
        here = piece(u, f ^ (2 * r), x)
        return remote(here, here, fy_s.at[at], fy_r.at[at], core)

    def w_fx(u, r, t):
        at = (u, r - 1, t - 1)
        here = piece(u, f ^ (2 * r), x ^ t)
        return remote(here, here, fx_s.at[at], fx_r.at[at], core)

    def issue(u):
        if u < len(units):
            for r in range(1, ys):
                w_y(u, r).start()

    def came_y(u):
        for r in range(1, ys):
            w_y(u, r).wait_recv()
        issue(u + 3)
        for r in range(1, ys):
            for t in range(1, dp):
                w_x(u, r, t).start()
            w_fy(u, r).start()

    def came_x(u):
        for r in range(1, ys):
            for t in range(1, dp):
                w_x(u, r, t).wait_recv()
                w_fx(u, r, t).start()

    def normalise_rows(src, at, count):
        def body(i, carry):
            here = pl.ds(pl.multiple_of(i * 128, 128), 128)
            there = pl.ds(pl.multiple_of(at + i * 128, 128), 128)
            hat, _ = normalise(src[here, :].astype(F32))
            value = (hat * gain[...] + bias[...]).astype(BF16)
            normed[there, :] = value
            n_t[:, there] = value.T
            return carry

        lax.fori_loop(count[0], count[1], body, 0)

    def project(at, c):
        here = pl.ds(pl.multiple_of(at, 128), local)
        (q, k, v)[c][here, :] = nn(normed[here, :], w[:, c * half : (c + 1) * half]).astype(BF16)

    for i in range(3):
        hold(i).start()
    load.wait()
    normalise_rows(mine, parity * local, (0, local // 128))
    for c in range(3):
        q_local(c).wait()
        q_core(c).wait_recv()
        for r in range(1, ys):
            q_y(c, r).wait_recv()
            q_far(c, r).start()
        if c == 0:
            for i in range(3):
                hold(i).wait()
            issue(0)
            for i in range(3):
                s_local(i).start()
                s_core(i).start()
        elif c == 1:
            issue(1)
        else:
            issue(2)
        for r in range(1, ys):
            q_far(c, r).wait_recv()
        if c == 0:
            token(0).wait_recv()
            index = lax.broadcasted_iota(jnp.int32, (BLK, 1), 0)
            made[...] = jnp.where(
                index < info[7], theirs[0:BLK, :].astype(F32), mine[local - BLK : local, :].astype(F32)
            ).astype(BF16)

            @pl.when(s < 2)
            def _():
                pads[...] = made[...]

        project(parity * local, c)
        if c == 0:

            @pl.when(s == 1)
            def _():
                remote(made, pads, pad_s.at[0], pad_r.at[0], peer("seq", 3)).start()

    w_store = pltpu.make_async_copy(w, w_out, out_l.at[0])
    w_store.start()
    forward_pads = remote(pads, pads, pad_s.at[1], pad_r.at[1], mate)

    @pl.when(s == 2)
    def _():
        remote(made, pads, pad_s.at[0], pad_r.at[0], peer("seq", 3)).wait_recv()
        forward_pads.start()

    away = (1 - parity) * local
    normalise_rows(theirs, away, (0, BLK // 128))
    came_y(0)
    token(1).wait_recv()
    normalise_rows(theirs, away, (BLK // 128, local // 128))
    for c in range(3):
        project(away, c)
    stores = [
        pltpu.make_async_copy(a, b, out_l.at[1 + i])
        for i, (a, b) in enumerate(((q, q_out), (k, k_out), (v, v_out), (n_t, n_out), (theirs, tok_out)))
    ]
    for copy in stores:
        copy.start()
    came_y(1)
    came_x(0)

    @pl.when(s == 3)
    def _():
        forward_pads.wait_recv()

    hat, _ = normalise(pads[...].astype(F32))
    value = (hat * gain[...] + bias[...]).astype(BF16)
    np_t[...] = value.T
    kp[...] = nn(value, w[:, half : 2 * half]).astype(BF16)
    vp[...] = nn(value, w[:, 2 * half :]).astype(BF16)
    late = [
        pltpu.make_async_copy(a, b, out_l.at[6 + i])
        for i, (a, b) in enumerate(((np_t, np_out), (kp, kp_out), (vp, vp_out), (pads, pad_out)))
    ]
    for copy in late:
        copy.start()
    came_y(2)
    came_x(1)

    def give(i):
        lanes = pl.ds(pl.multiple_of(i * 2 * HD, 128), 2 * HD)
        return remote(
            mixed.at[pl.ds(pl.multiple_of(away, 16), local), lanes], other.at[:, lanes], o_s.at[i], o_r.at[i], mate
        )

    pairs = half // (2 * HD)
    done_y, done_x = 3, 2
    for i in range(pairs):
        lanes = slice(i * 2 * HD, (i + 1) * 2 * HD)

        def put(at, value):
            mixed[at, lanes] = value

        def put_lse(h, at, value):
            lse[i, h : h + 1, at] = value

        attend_pair(
            bounds,
            lambda at: q[at, lanes],
            lambda at: k[at, lanes],
            lambda at: v[at, lanes],
            lambda at: kp[at, lanes],
            lambda at: vp[at, lanes],
            put,
            put_lse,
        )
        give(i).start()
        came_y(done_y)
        came_x(done_x)
        done_y, done_x = done_y + 1, done_x + 1
    last = [
        pltpu.make_async_copy(mixed, mix_out, out_l.at[10]),
        pltpu.make_async_copy(lse, lse_out, out_l.at[11]),
    ]
    for copy in last:
        copy.start()
    for u in range(done_y, len(units)):
        came_y(u)
        came_x(u - 1)
    came_x(len(units) - 1)

    for i in range(pairs):
        give(i).wait()
    for i in range(3):
        s_local(i).wait()
        s_core(i).wait()
    for u in range(len(units)):
        for r in range(1, ys):
            w_y(u, r).wait_send()
            w_fy(u, r).wait()
            for t in range(1, dp):
                w_x(u, r, t).wait_send()
                w_fx(u, r, t).wait()
    for c in range(3):
        q_core(c).wait_send()
        for r in range(1, ys):
            q_y(c, r).wait_send()
            q_far(c, r).wait_send()
    token(0).wait_send()
    token(1).wait_send()

    @pl.when(s == 1)
    def _():
        remote(made, pads, pad_s.at[0], pad_r.at[0], peer("seq", 3)).wait_send()

    @pl.when(s == 2)
    def _():
        forward_pads.wait_send()

    for copy in [w_store] + stores + late + last:
        copy.wait()


def front(info, tokens, wqkv, wo, wu, wd, gain, bias, fsdp, dp):
    local, d = tokens.shape
    half, ff = d // 2, wu.shape[1]
    pairs = half // (2 * HD)
    y, px, n = max(fsdp // 2 - 1, 1), max(dp - 1, 1), 9
    dma = pltpu.SemaphoreType.DMA
    outs = [((2 * local, half), BF16)] * 3 + [
        ((d, 2 * local), BF16),
        ((d, BLK), BF16),
        ((BLK, half), BF16),
        ((BLK, half), BF16),
        ((d, 3 * half), BF16),
        ((2 * local, half), BF16),
        ((pairs, 2, 2 * local), F32),
        ((local, half), BF16),
        ((local, d), BF16),
        ((BLK, d), BF16),
        ((d, d), BF16),
        ((d, ff), BF16),
        ((ff, d), BF16),
    ]
    buffers = [
        (local, d), (local, d), (BLK, d), (BLK, d), (d, 3 * half), (2 * local, d), (d, 2 * local), (d, BLK),
        (2 * local, half), (2 * local, half), (2 * local, half), (BLK, half), (BLK, half), (2 * local, half),
        wo.shape, wu.shape, wd.shape,
    ]
    sems = [(1,), (2,), (2,), (2,), (2,), (3,), (3,), (3,), (3, y), (3, y), (3, y), (3, y)]
    sems += [(3,)] * 4 + [(n, y)] * 2 + [(n, y, px)] * 2 + [(n, y)] * 2 + [(n, y, px)] * 2 + [(pairs,)] * 2 + [(12,)]
    return pl.pallas_call(
        functools.partial(front_body, fsdp=fsdp, dp=dp),
        in_specs=[pl.BlockSpec(memory_space=pltpu.SMEM)] + [hbm()] * 5 + [pl.BlockSpec(memory_space=pltpu.VMEM)] * 2,
        out_specs=[hbm()] * len(outs),
        out_shape=[shape(*o) for o in outs],
        scratch_shapes=[pltpu.VMEM(b, BF16) for b in buffers]
        + [pltpu.VMEM((pairs, 2, 2 * local), F32)]
        + [dma(s) for s in sems],
        compiler_params=pltpu.CompilerParams(vmem_limit_bytes=VMEM_LIMIT, collective_id=1, has_side_effects=True),
        cost_estimate=pl.CostEstimate(flops=10**10, bytes_accessed=10**8, transcendentals=0),
    )(info, tokens, wqkv, wo, wu, wd, gain, bias)


def forward_body(
    info, own, other, x, up, gains, biases, wo, wu, wd, out, g_feed, act_t, slope, n_t, branch, middle, edges, normed, feed
):
    parity = info[1]
    step, last = pl.program_id(0), pl.num_programs(0) - 1
    half = own.shape[1]
    blocks = x.shape[0] // 128

    @pl.when(step == 0)
    def _():
        w_own = wo[pl.ds(pl.multiple_of(parity * half, 128), half), :]
        w_other = wo[pl.ds(pl.multiple_of((1 - parity) * half, 128), half), :]
        branch[...] = nn(own[...], w_own) + nn(other[...], w_other)

        def rows(i, carry):
            at = pl.ds(pl.multiple_of(i * 128, 128), 128)
            hat, _ = normalise(branch[at, :])
            mid = x[at, :].astype(F32) + hat * gains[1:2, :] + biases[1:2, :]
            middle[at, :] = mid
            hat, _ = normalise(mid)
            two = (hat * gains[2:3, :] + biases[2:3, :]).astype(BF16)
            normed[at, :] = two
            n_t[:, at] = two.T
            return carry

        lax.fori_loop(0, blocks, rows, 0)
        feed[...] = jnp.zeros_like(feed)

    u = nn(normed[...], wu[...])
    th = jnp.tanh(0.7978845608 * (u + 0.044715 * (u * u * u)))
    act = (0.5 * u * (1.0 + th)).astype(BF16)
    slope[...] = (
        0.5 * (1.0 + th) + 0.5 * u * (1.0 - th * th) * (0.7978845608 + (3 * 0.044715 * 0.7978845608) * (u * u))
    ).astype(BF16)
    act_t[...] = act.T
    feed[...] += nn(act, wd[...])

    @pl.when(step == last)
    def _():
        def rows(i, carry):
            at = pl.ds(pl.multiple_of(i * 128, 128), 128)
            g = up[at, :].astype(F32)
            hat, rstd = normalise(feed[at, :])
            gain = gains[3:4, :]
            out[at, :] = (middle[at, :] + hat * gain + biases[3:4, :]).astype(BF16)
            g_feed[at, :] = norm_back(g, hat, rstd, gain).astype(BF16)
            return (
                carry[0] + jnp.sum(g * hat, axis=0, keepdims=True),
                carry[1] + jnp.sum(g, axis=0, keepdims=True),
            )

        zero = jnp.zeros((1, x.shape[1]), F32)
        a, b = lax.fori_loop(0, blocks, rows, (zero, zero))
        edges[0:1, :] = a
        edges[1:2, :] = b


def forward(info, mixed, other, x, up, gains, biases, wo, wu, wd):
    local, d = x.shape
    half, ff = mixed.shape[1], wu.shape[1]
    tile = 512
    once = lambda s: pl.BlockSpec(s, lambda *_: (0,) * len(s), pipeline_mode=pl.Buffered(1))
    return call(
        forward_body,
        (ff // tile,),
        1,
        [
            pl.BlockSpec((local, half), lambda i, info: (info[1], 0), pipeline_mode=pl.Buffered(1)),
            once(other.shape),
            once(x.shape),
            once(up.shape),
            once(gains.shape),
            once(biases.shape),
            once(wo.shape),
            pl.BlockSpec((d, tile), lambda i, info: (0, i)),
            pl.BlockSpec((tile, d), lambda i, info: (i, 0)),
        ],
        [
            full((local, d)),
            full((local, d)),
            pl.BlockSpec((tile, local), lambda i, info: (i, 0)),
            pl.BlockSpec((local, tile), lambda i, info: (0, i)),
            full((d, local)),
            full((local, d)),
            full((local, d)),
            full((2, d)),
        ],
        [
            shape((local, d), BF16),
            shape((local, d), BF16),
            shape((ff, local), BF16),
            shape((local, ff), BF16),
            shape((d, local), BF16),
            shape((local, d), F32),
            shape((local, d), F32),
            shape((2, d), F32),
        ],
        [pltpu.VMEM((local, d), BF16), pltpu.VMEM((local, d), F32)],
        flops=2 * local * d * (d + 2 * ff),
        moved=40e6,
    )(info, mixed, other, x, up, gains, biases, wo, wu, wd)


def back_body(info, g_feed, n_t, act_t, slope, wd, wu, keep, send, g_two, *, fsdp):
    r = pl.program_id(0)
    f = info[0]
    tile = wd.shape[0]
    rows = n_t.shape[0] // fsdp
    width = keep.shape[2]
    piece = width // fsdp
    here = r ^ f
    g = g_feed[...]
    hid = (nt(g, wd[...]) * slope[...].astype(F32)).astype(BF16)
    down = nn(act_t[...], g).astype(BF16)
    even = r % 2 == 0

    @pl.when(even)
    def _():
        keep[r // 2, 0:tile, :] = down

    @pl.when(~even)
    def _():
        send[r // 2, 0:tile, :] = down

    lanes = pl.ds(pl.multiple_of(here * piece, 128), piece)
    for other in range(fsdp):
        shard = other ^ f
        up = nn(n_t[pl.ds(pl.multiple_of(shard * rows, 128), rows), :], hid).astype(BF16)
        target = (keep, send)[other % 2]
        for c in range(tile // piece):
            target[other // 2, tile + c * rows : tile + (c + 1) * rows, lanes] = up[:, c * piece : (c + 1) * piece]
    part = nt(hid, wu[...])

    @pl.when(r == 0)
    def _():
        g_two[...] = part

    @pl.when(r != 0)
    def _():
        g_two[...] += part


def back_group(info, g, g_feed, n_t, act_t, slope, wd, wu, fsdp):
    local, d = g_feed.shape
    ff = wd.shape[0]
    tile = ff // fsdp // GROUPS
    extra = (d // fsdp) * (fsdp * tile // d)
    block = lambda i, info: (i ^ info[0]) * GROUPS + g
    grads = shape((fsdp // 2, tile + extra, d), BF16)
    return call(
        functools.partial(back_body, fsdp=fsdp),
        (fsdp,),
        1,
        [
            full((local, d)),
            full((d, local)),
            pl.BlockSpec((tile, local), lambda i, info: (block(i, info), 0)),
            pl.BlockSpec((local, tile), lambda i, info: (0, block(i, info))),
            pl.BlockSpec((tile, d), lambda i, info: (block(i, info), 0)),
            pl.BlockSpec((d, tile), lambda i, info: (0, block(i, info))),
        ],
        [full(grads.shape), full(grads.shape), full((local, d))],
        [grads, grads, shape((local, d), F32)],
        flops=8 * local * d * tile * fsdp,
        moved=40e6,
    )(info, g_feed, n_t, act_t, slope, wd, wu)


def middle_body(
    info, ga, gb, middle, branch, up, gains, wo, own, other, g_mid, d_own, d_send, keep, send, edges, att, gbr, *, fsdp
):
    f, parity = info[0], info[1]
    step, last = pl.program_id(0), pl.num_programs(0) - 1
    half = own.shape[1]

    @pl.when(step == 0)
    def _():
        edges[...] = jnp.zeros_like(edges)
        att[:, pl.ds(pl.multiple_of(parity * half, 128), half)] = own[...]
        att[:, pl.ds(pl.multiple_of((1 - parity) * half, 128), half)] = other[...]

    g = ga[...] + gb[...]
    hat, rstd = normalise(middle[...])
    edges[2:3, :] += jnp.sum(g * hat, axis=0, keepdims=True)
    edges[3:4, :] += jnp.sum(g, axis=0, keepdims=True)
    gm = up[...].astype(F32) + norm_back(g, hat, rstd, gains[2:3, :])
    g_mid[...] = gm
    hat, rstd = normalise(branch[...])
    edges[0:1, :] += jnp.sum(gm * hat, axis=0, keepdims=True)
    edges[1:2, :] += jnp.sum(gm, axis=0, keepdims=True)
    gr = norm_back(gm, hat, rstd, gains[1:2, :]).astype(BF16)
    gbr[pl.ds(pl.multiple_of(step * gr.shape[0], 16), gr.shape[0]), :] = gr

    @pl.when(step == last)
    def _():
        grad = gbr[...]
        d_send[...] = nt(grad, wo[pl.ds(pl.multiple_of((1 - parity) * half, 128), half), :]).astype(BF16)
        d_own[...] = nt(grad, wo[pl.ds(pl.multiple_of(parity * half, 128), half), :]).astype(BF16)
        rows = keep.shape[1]
        for r in range(fsdp):
            cols = pl.ds(pl.multiple_of((r ^ f) * rows, 128), rows)
            (keep, send)[r % 2][r // 2] = tn(att[:, cols], grad).astype(BF16)


def middle_back(info, ga, gb, middle, branch, up, gains, wo, attn, half, other, fsdp):
    local, d = ga.shape
    rows = 128
    block = pl.BlockSpec((rows, d), lambda i, info: (i, 0))
    grads = shape((fsdp // 2, d // fsdp, d), BF16)
    return call(
        functools.partial(middle_body, fsdp=fsdp),
        (local // rows,),
        1,
        [block, block, block, block, block, full(gains.shape), full(wo.shape)]
        + [pl.BlockSpec((local, half), lambda i, info: (info[1], 0)), full(other.shape)],
        [block, full((local, half)), full((local, half)), full(grads.shape), full(grads.shape), full((4, d))],
        [shape((local, d), F32), shape((local, half), BF16), shape((local, half), BF16), grads, grads, shape((4, d), F32)],
        [pltpu.VMEM((local, d), BF16), pltpu.VMEM((local, d), BF16)],
        flops=4 * local * d * d,
        moved=22e6,
    )(info, ga, gb, middle, branch, up, gains, wo, attn, other)


def project_back_body(
    info, own, theirs, padx, gains, dq, dk, dv, dkp, dvp, w, n_t, np_t, g_own, g_send, g_pad, keep, send, edges, *, fsdp
):
    f, parity = info[0], info[1]
    step = pl.program_id(0)
    local = own.shape[0]
    half = dq.shape[1]
    gain = gains[0:1, :]

    def through(at):
        return (
            nt(dq[at, :], w[:, 0:half])
            + nt(dk[at, :], w[:, half : 2 * half])
            + nt(dv[at, :], w[:, 2 * half :])
        )

    @pl.when(step == 0)
    def _():
        g = nt(dkp[...], w[:, half : 2 * half]) + nt(dvp[...], w[:, 2 * half :])
        g_pad[...] = g.astype(BF16)
        hat, _ = normalise(padx[...].astype(F32))
        edges[0:1, :] = jnp.sum(g * hat, axis=0, keepdims=True)
        edges[1:2, :] = jnp.sum(g, axis=0, keepdims=True)
        g = through(pl.ds(pl.multiple_of((1 - parity) * local, 128), local))
        g_send[...] = g.astype(BF16)
        hat, _ = normalise(theirs[...].astype(F32))
        edges[0:1, :] += jnp.sum(g * hat, axis=0, keepdims=True)
        edges[1:2, :] += jnp.sum(g, axis=0, keepdims=True)

    @pl.when(step == 1)
    def _():
        g = through(pl.ds(pl.multiple_of(parity * local, 128), local))
        g_own[...] = g
        hat, _ = normalise(own[...].astype(F32))
        edges[0:1, :] += jnp.sum(g * hat, axis=0, keepdims=True)
        edges[1:2, :] += jnp.sum(g, axis=0, keepdims=True)
        rows = keep.shape[1]
        for r in range(fsdp):
            at = pl.ds(pl.multiple_of((r ^ f) * rows, 128), rows)
            target = (keep, send)[r % 2]
            left, pads = n_t[at, :], np_t[at, :]
            target[r // 2, :, 0:half] = nn(left, dq[...]).astype(BF16)
            target[r // 2, :, half : 2 * half] = (nn(left, dk[...]) + nn(pads, dkp[...])).astype(BF16)
            target[r // 2, :, 2 * half :] = (nn(left, dv[...]) + nn(pads, dvp[...])).astype(BF16)


def project_back(info, own, theirs, padx, gains, dq, dk, dv, dkp, dvp, w, n_t, np_t, fsdp):
    local, d = own.shape
    wide = w.shape[1]
    pads = padx.shape[0]
    grads = shape((fsdp // 2, d // fsdp, wide), BF16)
    arrays = (own, theirs, padx, gains, dq, dk, dv, dkp, dvp, w, n_t, np_t)
    return call(
        functools.partial(project_back_body, fsdp=fsdp),
        (2,),
        1,
        [pl.BlockSpec(a.shape, lambda *_: (0, 0), pipeline_mode=pl.Buffered(1)) for a in arrays],
        [full((local, d)), full((local, d)), full((pads, d)), full(grads.shape), full(grads.shape), full((2, d))],
        [shape((local, d), F32), shape((local, d), BF16), shape((pads, d), BF16), grads, grads, shape((2, d), F32)],
        flops=8 * local * d * wide,
        moved=24e6,
    )(info, *arrays)


def finish_body(info, x, g_own, g_other, pad_a, pad_b, g_mid, gains, out, total):
    s, start, cut = info[6], info[7], info[8]
    row = lax.broadcasted_iota(jnp.int32, (pad_a.shape[0], 1), 0)
    mine = ((s == 0) & (row < start)) | ((s == 1) & (row >= cut))
    extra = jnp.where(mine, pad_a[...].astype(F32) + pad_b[...].astype(F32), 0.0)
    total[...] = g_own[...] + g_other[...].astype(F32)
    at = pl.ds(pl.multiple_of(jnp.where(s == 0, 0, total.shape[0] - pad_a.shape[0]), 128), pad_a.shape[0])
    total[at, :] += extra

    def rows(i, carry):
        at = pl.ds(pl.multiple_of(i * 128, 128), 128)
        hat, rstd = normalise(x[at, :].astype(F32))
        out[at, :] = (g_mid[at, :] + norm_back(total[at, :], hat, rstd, gains[0:1, :])).astype(BF16)
        return carry

    lax.fori_loop(0, x.shape[0] // 128, rows, 0)


def finish(info, x, g_own, g_other, pad_a, pad_b, g_mid, gains):
    arrays = (x, g_own, g_other, pad_a, pad_b, g_mid, gains)
    return call(
        finish_body,
        (1,),
        1,
        [full(a.shape) for a in arrays],
        full(x.shape),
        shape(x.shape, BF16),
        [pltpu.VMEM(x.shape, F32)],
        flops=1e7,
        moved=12e6,
    )(info, *arrays)


class Lane:
    names = ("core_s", "core_r", "y_s", "y_r", "x_s", "x_r", "z_s", "z_r", "zz_s", "zz_r", "xx_s", "xx_r", "own")

    @staticmethod
    def scratch(count, rows, cols, fsdp, dp, masks):
        y, parts = fsdp // 2, len(masks) + 1
        dma = pltpu.SemaphoreType.DMA
        sems = [(count,), (count,)]
        sems += [(count, max(y - 1, 1))] * 2 + [(count, max(dp - 1, 1))] * 2
        sems += [(count, len(masks))] * 4 + [(count, max(dp - 1, 1))] * 2 + [(count,)]
        return [
            pltpu.VMEM((count, y, rows, cols), BF16),
            pltpu.VMEM((count, max(y - 1, 1), rows, cols), BF16),
            pltpu.VMEM((count, max(dp - 1, 1), rows // dp, cols), BF16),
            pltpu.VMEM((count, len(masks), rows // dp, cols // parts), BF16),
        ] + [dma(s) for s in sems]

    size = 4 + 13

    def __init__(self, refs, final, fsdp, dp, masks, unit):
        self.acc, self.y_in, self.x_in, self.z_in = refs[:4]
        self.sems = dict(zip(self.names, refs[4:]))
        self.final = final
        self.ys, self.dp, self.masks = fsdp // 2, dp, masks
        self.count, _, self.rows, self.cols = self.acc.shape
        self.x = lax.axis_index("dp")
        self.part = self.cols // (len(masks) + 1)
        self.unit = unit

    def place(self, mask=0):
        at = (lax.axis_index("seq") ^ mask) // self.unit % (len(self.masks) + 1)
        return pl.ds(pl.multiple_of(at * self.part, 128), self.part)

    def band(self, mask=0):
        n = self.rows // self.dp
        return pl.ds(pl.multiple_of((self.x ^ mask) * n, 16), n)

    def core(self, u, src):
        return remote(src, self.acc.at[u], self.sems["core_s"].at[u], self.sems["core_r"].at[u], peer("fsdp", 1))

    def over_y(self, u, ry):
        s = self.sems
        return remote(
            self.acc.at[u, ry], self.y_in.at[u, ry - 1], s["y_s"].at[u, ry - 1], s["y_r"].at[u, ry - 1], peer("fsdp", 2 * ry)
        )

    def over_x(self, u, rx):
        s = self.sems
        return remote(
            self.acc.at[u, 0, self.band(rx)],
            self.x_in.at[u, rx - 1],
            s["x_s"].at[u, rx - 1],
            s["x_r"].at[u, rx - 1],
            peer("dp", rx),
        )

    def over_z(self, u, i):
        s, m = self.sems, self.masks[i]
        return remote(
            self.acc.at[u, 0, self.band(), self.place(m)],
            self.z_in.at[u, i],
            s["z_s"].at[u, i],
            s["z_r"].at[u, i],
            peer("seq", m),
        )

    def back_z(self, u, i):
        s, m = self.sems, self.masks[i]
        return remote(
            self.acc.at[u, 0, self.band(), self.place()],
            self.final.at[u, self.band(), self.place()],
            s["zz_s"].at[u, i],
            s["zz_r"].at[u, i],
            peer("seq", m),
        )

    def back_x(self, u, rx):
        s = self.sems
        at = self.final.at[u, self.band()]
        return remote(at, at, s["xx_s"].at[u, rx - 1], s["xx_r"].at[u, rx - 1], peer("dp", rx))

    def keep(self, u):
        return pltpu.make_async_copy(
            self.acc.at[u, 0, self.band(), self.place()],
            self.final.at[u, self.band(), self.place()],
            self.sems["own"].at[u],
        )

    def add(self, target, sources):
        rows = target.shape[0]
        step = 64 if rows % 64 == 0 else 16

        def body(i, carry):
            at = pl.ds(pl.multiple_of(i * step, 16), step)
            total = target[at, :].astype(F32)
            for src in sources:
                total = total + src[at, :].astype(F32)
            target[at, :] = total.astype(BF16)
            return carry

        lax.fori_loop(0, rows // step, body, 0)

    def one(self, u, keep):
        self.core(u, keep).wait_recv()
        for ry in range(self.ys):
            self.add(self.acc.at[u, ry], [keep.at[ry]])
        for ry in range(1, self.ys):
            self.over_y(u, ry).start()

    def two(self, u):
        for ry in range(1, self.ys):
            self.over_y(u, ry).wait_recv()
        self.add(self.acc.at[u, 0], [self.y_in.at[u, ry - 1] for ry in range(1, self.ys)])
        for rx in range(1, self.dp):
            self.over_x(u, rx).start()

    def three(self, u):
        for rx in range(1, self.dp):
            self.over_x(u, rx).wait_recv()
        self.add(self.acc.at[u, 0, self.band()], [self.x_in.at[u, rx - 1] for rx in range(1, self.dp)])
        for i in range(len(self.masks)):
            self.over_z(u, i).start()

    def four(self, u):
        for i in range(len(self.masks)):
            self.over_z(u, i).wait_recv()
        self.add(
            self.acc.at[u, 0, self.band(), self.place()], [self.z_in.at[u, i] for i in range(len(self.masks))]
        )
        self.keep(u).start()
        for i in range(len(self.masks)):
            self.back_z(u, i).start()

    def five(self, u):
        self.keep(u).wait()
        for i in range(len(self.masks)):
            self.back_z(u, i).wait_recv()
        for rx in range(1, self.dp):
            self.back_x(u, rx).start()

    def six(self, u):
        for rx in range(1, self.dp):
            self.back_x(u, rx).wait_recv()

    def drain(self, u, src):
        self.core(u, src).wait_send()
        for ry in range(1, self.ys):
            self.over_y(u, ry).wait_send()
        for rx in range(1, self.dp):
            self.over_x(u, rx).wait_send()
            self.back_x(u, rx).wait_send()
        for i in range(len(self.masks)):
            self.over_z(u, i).wait_send()
            self.back_z(u, i).wait_send()


def partners(fsdp, dp):
    return (
        [peer("fsdp", 1)]
        + [peer("fsdp", 2 * ry) for ry in range(1, fsdp // 2)]
        + [peer("dp", rx) for rx in range(1, dp)]
        + [peer("seq", m) for m in (1, 2, 3)]
    )


def reduce_body(*refs, fsdp, dp, layout):
    n_in = len(layout)
    keeps, sends = refs[:n_in], refs[n_in : 2 * n_in]
    final_a, final_b = refs[2 * n_in : 2 * n_in + 2]
    rest = refs[2 * n_in + 2 :]
    held_a, held_b, load_a, load_b = rest[:4]
    a = Lane(rest[4 : 4 + Lane.size], final_a, fsdp, dp, (1, 2, 3), 1)
    b = Lane(rest[4 + Lane.size :], final_b, fsdp, dp, (2,), 2)
    greet(partners(fsdp, dp))

    def views(lane, held, load):
        u = 0
        for i, (kind, cuts) in enumerate(layout):
            if kind != (lane is b):
                continue
            for cut in range(cuts):
                if kind:
                    at = (slice(None), slice(None), pl.ds(cut * lane.cols, lane.cols))
                else:
                    at = (slice(None), pl.ds(cut * lane.rows, lane.rows))
                yield u, sends[i].at[at], functools.partial(
                    pltpu.make_async_copy, keeps[i].at[at], held.at[u], load.at[u]
                )
                u += 1

    lanes = ((a, held_a, load_a), (b, held_b, load_b))
    for lane, held, load in lanes:
        for u, src, copy in views(lane, held, load):
            lane.core(u, src).start()
            copy().start()
    for lane, held, load in lanes:
        for u, src, copy in views(lane, held, load):
            copy().wait()
    total = a.count + b.count

    def tick(t, carry):
        for offset, name in ((0, "one"), (2, "two"), (3, "three"), (4, "four"), (5, "five"), (6, "six")):
            for lane, held, first in ((a, held_a, 0), (b, held_b, a.count)):
                u = t - offset - first

                @pl.when((u >= 0) & (u < lane.count))
                def _():
                    if name == "one":
                        lane.one(u, held.at[u])
                    else:
                        getattr(lane, name)(u)

        return carry

    lax.fori_loop(0, total + 6, tick, 0)
    for lane, held, load in lanes:
        for u, src, copy in views(lane, held, load):
            lane.drain(u, src)


def reduce_all(pairs, fsdp, dp):
    d = pairs[0][0].shape[2]
    rows = d // fsdp
    layout = tuple((False, k.shape[1] // rows) for k, _ in pairs[:-1]) + ((True, 3),)
    n_a = sum(c for kind, c in layout if not kind)
    wide = pairs[-1][0].shape[2] // 3
    y = fsdp // 2
    return pl.pallas_call(
        functools.partial(reduce_body, fsdp=fsdp, dp=dp, layout=layout),
        in_specs=[hbm()] * (2 * len(pairs)),
        out_specs=[hbm(), hbm()],
        out_shape=[shape((n_a, rows, d), BF16), shape((3, rows, wide), BF16)],
        scratch_shapes=[
            pltpu.VMEM((n_a, y, rows, d), BF16),
            pltpu.VMEM((3, y, rows, wide), BF16),
            pltpu.SemaphoreType.DMA((n_a,)),
            pltpu.SemaphoreType.DMA((3,)),
        ]
        + Lane.scratch(n_a, rows, d, fsdp, dp, (1, 2, 3))
        + Lane.scratch(3, rows, wide, fsdp, dp, (2,)),
        compiler_params=pltpu.CompilerParams(vmem_limit_bytes=VMEM_LIMIT, collective_id=0, has_side_effects=True),
        cost_estimate=pl.CostEstimate(flops=10**8, bytes_accessed=5 * 10**8, transcendentals=0),
    )(*[k for k, _ in pairs], *[s for _, s in pairs])


def hop(value, axis, mask):
    return lax.ppermute(value, axis, [(i, i ^ mask) for i in range(lax.axis_size(axis))])


def arrange(pieces, index):
    count = len(pieces)
    if count == 1:
        return list(pieces)
    half = count // 2
    low, high = arrange(pieces[:half], index), arrange(pieces[half:], index)
    bit = (index & half) != 0
    return [jnp.where(bit, b, a) for a, b in zip(low, high)] + [jnp.where(bit, a, b) for a, b in zip(low, high)]


def sum_all(value):
    for axis in ("fsdp", "dp", "seq"):
        m = 1
        while m < lax.axis_size(axis):
            value = value + hop(value, axis, m)
            m *= 2
    return value


def local(
    tokens, qkv_weight, out_weight, up_weight, down_weight, norm_gain, norm_bias, caption_len, item_start, grad_out
):
    x_tok, up = tokens[0], grad_out[0]
    local_rows, d = x_tok.shape
    fsdp = lax.axis_size("fsdp")
    ff = up_weight.shape[1]
    half = d // 2
    f, s = lax.axis_index("fsdp"), lax.axis_index("seq")
    parity, slot = s % 2, s // 2
    caps, starts = caption_len[0], item_start[0]
    start = jnp.where(slot == 0, starts[0], starts[1] - SLOT)
    stop = start + jnp.where(slot == 0, caps[0], caps[1]) + IMAGE
    pad_a = jnp.where(slot == 0, 0, starts[0])
    pad_b = jnp.where(slot == 0, BLK, starts[0] + caps[0])
    info = jnp.stack(
        [f, parity, start, stop, pad_a, pad_b, s, starts[0], starts[0] + caps[0]]
    ).astype(jnp.int32)

    dp = lax.axis_size("dp")
    (q, k, v, n_t, np_t, kp, vp, w_qkv, mixed, lse, other, theirs, pads, wo, wu, wd) = front(
        info, x_tok, qkv_weight, out_weight, up_weight, down_weight, norm_gain[0:1], norm_bias[0:1], fsdp, dp
    )
    (out, g_feed, act_t, slope, two_t, branch, middle, edges3) = forward(
        info, mixed, other, x_tok, up, norm_gain, norm_bias, wo, wu, wd
    )
    keeps, g_twos = [], []
    for g in range(GROUPS):
        keep, send, g_two = back_group(info, g, g_feed, two_t, act_t, slope, wd, wu, fsdp)
        keeps.append((keep, send))
        g_twos.append(g_two)
    g_mid, d_own, d_send, keep_o, send_o, edges12 = middle_back(
        info, g_twos[0], g_twos[1], middle, branch, up, norm_gain, wo, mixed, half, other, fsdp
    )
    d_other = hop(d_send, "seq", 1)
    dq, dk, dv, dkp, dvp = attend_back(info, q, k, v, kp, vp, mixed, lse, d_own, d_other)
    g_own, g_send, g_pad, keep_q, send_q, edges0 = project_back(
        info, x_tok, theirs, pads, norm_gain, dq, dk, dv, dkp, dvp, w_qkv, n_t, np_t, fsdp
    )
    g_other = hop(g_send, "seq", 1)
    back_a = lax.ppermute(g_pad, "seq", [(2, 0), (3, 1)])
    back_b = lax.ppermute(g_pad, "seq", [(2, 1), (3, 0)])
    grad_in = finish(info, x_tok, g_own, g_other, back_a, back_b, g_mid, norm_gain)

    sums = sum_all(
        jnp.stack(
            [edges0[0], edges12[0], edges12[2], edges3[0], edges0[1], edges12[1], edges12[3], edges3[1]]
        )
    )

    done, done_q = reduce_all(keeps + [(keep_o, send_o), (keep_q, send_q)], fsdp, dp)
    rows = d // fsdp
    per = (done.shape[0] - 1) // GROUPS
    reduced = [done[g * per : (g + 1) * per].reshape(per * rows, d) for g in range(GROUPS)]
    grad_proj = done[-1].astype(F32)
    half_q = jnp.concatenate([done_q[0], done_q[1], done_q[2]], axis=1)
    both = arrange([half_q, hop(half_q, "seq", 1)], parity)
    grad_qkv = jnp.concatenate(
        [both[h][:, c * half : (c + 1) * half] for c in range(3) for h in range(2)], axis=1
    ).astype(F32)
    tile = ff // fsdp // GROUPS
    grad_down = jnp.concatenate([r[:tile] for r in reduced], axis=0).astype(F32)
    piece = d // fsdp
    blocks = []
    for h in range(fsdp):
        for r in reduced:
            for c in range(tile // piece):
                blocks.append(r[tile + c * rows : tile + (c + 1) * rows, h * piece : (h + 1) * piece])
    grad_up = jnp.concatenate(blocks, axis=1).astype(F32)
    return (out[None], grad_in[None], grad_qkv, grad_proj, grad_up, grad_down, sums[0:4], sums[4:8])


def solution(mesh):
    rows = P(("fsdp", "dp"), "seq", None)
    shard = P("fsdp", None)
    items = P(("fsdp", "dp"), None)
    return jax.shard_map(
        local,
        mesh=mesh,
        in_specs=(rows, shard, shard, shard, shard, P(), P(), items, items, rows),
        out_specs=(rows, rows, shard, shard, shard, shard, P(), P()),
        check_vma=False,
    )
```

```python
import functools

import jax
import jax.numpy as jnp
from jax import lax
from jax.experimental import pallas as pl
from jax.experimental.pallas import tpu as pltpu
from jax.sharding import PartitionSpec as P

HD = 64
IMAGE = 1024
SLOT = 1280
BLK = 256
LOG2E = 1.4426950408889634
SCALE = LOG2E / 8.0
NEG = -1e30
F32 = jnp.float32
BF16 = jnp.bfloat16
VMEM_LIMIT = 60 * 1024 * 1024
PIECES = 4


def nn(a, b):
    return lax.dot_general(a, b, (((1,), (0,)), ((), ())), preferred_element_type=F32)


def nt(a, b):
    return lax.dot_general(a, b, (((1,), (1,)), ((), ())), preferred_element_type=F32)


def tn(a, b):
    return lax.dot_general(a, b, (((0,), (0,)), ((), ())), preferred_element_type=F32)


def normalise(v):
    mean = jnp.mean(v, axis=-1, keepdims=True)
    centred = v - mean
    var = jnp.mean(centred * centred, axis=-1, keepdims=True)
    rstd = lax.rsqrt(var + 1e-05)
    return centred * rstd, rstd


def norm_back(g, hat, rstd, gain):
    gg = g * gain
    return rstd * (
        gg - jnp.mean(gg, axis=-1, keepdims=True) - hat * jnp.mean(gg * hat, axis=-1, keepdims=True)
    )


def call(body, grid, prefetch, in_specs, out_specs, out_shape, scratch=(), flops=0, moved=0):
    return pl.pallas_call(
        body,
        grid_spec=pltpu.PrefetchScalarGridSpec(
            num_scalar_prefetch=prefetch,
            grid=grid,
            in_specs=in_specs,
            out_specs=out_specs,
            scratch_shapes=list(scratch),
        ),
        out_shape=out_shape,
        compiler_params=pltpu.CompilerParams(vmem_limit_bytes=VMEM_LIMIT),
        cost_estimate=pl.CostEstimate(flops=int(flops), bytes_accessed=int(moved), transcendentals=0),
    )


def full(shape):
    zeros = (0,) * len(shape)
    return pl.BlockSpec(shape, lambda *_: zeros)


def hbm():
    return pl.BlockSpec(memory_space=pl.ANY)


def shape(dims, dtype):
    return jax.ShapeDtypeStruct(dims, dtype)


def attend_pair(bounds, q, k, v, kp, vp, o, lse):
    start, stop, pad_a, pad_b = bounds
    lane = lax.broadcasted_iota(jnp.int32, (1, 2 * HD), 1)
    row = lax.broadcasted_iota(jnp.int32, (BLK, 1), 0)
    col = lax.broadcasted_iota(jnp.int32, (1, BLK), 1)
    causal = col <= row
    pad_col = (col < pad_a) | (col >= pad_b)
    count = SLOT // BLK
    for i in range(count):
        n = (i + 1) * BLK
        qi = q(slice(i * BLK, n))
        edge = i in (0, count - 1)
        pos_q = row + i * BLK
        in_q = (pos_q >= start) & (pos_q < stop)
        masks = []
        for j in range(i + 1):
            pos_k = col + j * BLK
            mask = None
            if edge:
                in_k = (pos_k >= start) & (pos_k < stop)
                mask = (in_q & in_k) | (~in_q & ~in_k)
            elif j == 0:
                mask = jnp.broadcast_to(pos_k >= start, (BLK, BLK))
            if j == i:
                mask = causal if mask is None else mask & causal
            masks.append(mask)
        outs = []
        for h in range(2):
            qh = jnp.where(lane // HD == h, qi, jnp.zeros_like(qi))
            blocks = []
            for j in range(i + 1):
                s = nt(qh, k(slice(j * BLK, (j + 1) * BLK))) * SCALE
                if masks[j] is not None:
                    s = jnp.where(masks[j], s, NEG)
                blocks.append(s)
            if edge:
                s = nt(qh, kp(slice(None))) * SCALE
                blocks.append(jnp.where(~in_q & pad_col, s, NEG))
            top = functools.reduce(jnp.maximum, blocks)
            top = jnp.max(top, axis=1, keepdims=True)
            probs = [jnp.exp2(s - top) for s in blocks]
            total = jnp.sum(functools.reduce(jnp.add, probs), axis=1, keepdims=True)
            probs = [x.astype(BF16) for x in probs]
            mixed = nn(jnp.concatenate(probs[: i + 1], axis=1), v(slice(0, n)))
            if edge:
                mixed = mixed + nn(probs[-1], vp(slice(None)))
            outs.append(mixed * (1.0 / total))
            level = jnp.broadcast_to(top + jnp.log2(total), (BLK, 128))
            lse(h, slice(i * BLK, n), level.T[0:1, :])
        o(slice(i * BLK, n), jnp.where(lane < HD, outs[0], outs[1]).astype(BF16))


def attend_back_pair(bounds, q, k, v, kp, vp, o, lse, do, dq, dk_sum, dv_sum, dkp_sum, dvp_sum):
    start, stop, pad_a, pad_b = bounds
    lane = lax.broadcasted_iota(jnp.int32, (1, 2 * HD), 1)
    pick = (
        lax.broadcasted_iota(jnp.int32, (8, 2 * HD), 1) // HD
        == lax.broadcasted_iota(jnp.int32, (8, 2 * HD), 0)
    ).astype(F32)
    row = lax.broadcasted_iota(jnp.int32, (BLK, 1), 0)
    col = lax.broadcasted_iota(jnp.int32, (1, 2 * BLK), 1) % BLK
    causal = row <= col
    pad_row = (row < pad_a) | (row >= pad_b)
    dk_sum[...] = jnp.zeros_like(dk_sum)
    dv_sum[...] = jnp.zeros_like(dv_sum)
    dkp_sum[...] = jnp.zeros_like(dkp_sum)
    dvp_sum[...] = jnp.zeros_like(dvp_sum)
    count = SLOT // BLK

    def split(x):
        zero = jnp.zeros_like(x)
        return [jnp.where(lane // HD == h, x, zero) for h in range(2)]

    for i in range(count):
        rows = slice(i * BLK, (i + 1) * BLK)
        do_i = do(rows)
        qs = jnp.concatenate(split(q(rows)), axis=0)
        ds = jnp.concatenate(split(do_i), axis=0)
        level = jnp.concatenate([lse(0, rows), lse(1, rows)], axis=1)
        inner = lax.dot_general(
            pick,
            do_i.astype(F32) * o(rows).astype(F32),
            (((1,), (1,)), ((), ())),
            precision=lax.Precision.HIGHEST,
            preferred_element_type=F32,
        )
        inner = jnp.concatenate([inner[0:1, :], inner[1:2, :]], axis=1)
        edge = i in (0, count - 1)
        pos_q = col + i * BLK
        in_q = (pos_q >= start) & (pos_q < stop)
        dq_sum = jnp.zeros((BLK, 2 * HD), F32)

        def block(kj, vj, mask):
            s = nt(kj, qs) * SCALE - level
            if mask is not None:
                s = jnp.where(mask, s, NEG)
            p = jnp.exp2(s)
            g = p * (nt(vj, ds) - inner)
            p, g = p.astype(BF16), g.astype(BF16)
            halves = split(kj)
            part = tn(g[:, :BLK], halves[0]) + tn(g[:, BLK:], halves[1])
            return nn(g, qs), nn(p, ds), part

        for j in range(i + 1):
            keys = slice(j * BLK, (j + 1) * BLK)
            pos_k = row + j * BLK
            mask = None
            if edge:
                in_k = (pos_k >= start) & (pos_k < stop)
                mask = (in_q & in_k) | (~in_q & ~in_k)
            elif j == 0:
                mask = jnp.broadcast_to(pos_k >= start, (BLK, 2 * BLK))
            if j == i:
                mask = causal if mask is None else mask & causal
            gk, gv, part = block(k(keys), v(keys), mask)
            dk_sum[keys, :] += gk
            dv_sum[keys, :] += gv
            dq_sum = dq_sum + part
        if edge:
            gk, gv, part = block(kp(slice(None)), vp(slice(None)), ~in_q & pad_row)
            dkp_sum[...] += gk
            dvp_sum[...] += gv
            dq_sum = dq_sum + part
        dq(rows, (dq_sum * 0.125).astype(BF16))


def peer(axis, mask):
    return {axis: lax.axis_index(axis) ^ mask}


def greet(partners):
    barrier = pltpu.get_barrier_semaphore()
    for p in partners:
        pl.semaphore_signal(barrier, inc=1, device_id=p, device_id_type=pl.DeviceIdType.MESH)
    pl.semaphore_wait(barrier, len(partners))


def remote(src, dst, send, recv, to):
    return pltpu.make_async_remote_copy(
        src_ref=src, dst_ref=dst, send_sem=send, recv_sem=recv, device_id=to, device_id_type=pl.DeviceIdType.MESH
    )


def front_body(
    info, tokens, wqkv, wo, wu, wd, gain, bias,
    q_out, k_out, v_out, n_out, np_out, kp_out, vp_out, w_out, mix_out, lse_out, other, tok_out, pad_out, wo_all, wu_all, wd_all,
    mine, theirs, pads, made, w, normed, n_t, np_t, q, k, v, kp, vp, mixed, held_o, held_u, held_d, lse,
    tok_l, tok_s, tok_r, pad_s, pad_r, q_l, q_cs, q_cr, q_ys, q_yr, q_fs, q_fr,
    h_l, s_l, s_cs, s_cr, y_s, y_r, x_s, x_r, fy_s, fy_r, fx_s, fx_r, o_s, o_r, out_l,
    *, fsdp, dp
):
    f, x, s = lax.axis_index("fsdp"), lax.axis_index("dp"), lax.axis_index("seq")
    parity = s % 2
    local, d = tokens.shape
    half = d // 2
    ys = fsdp // 2
    bounds = tuple(info[i] for i in range(2, 6))
    core, mate = peer("fsdp", 1), peer("seq", 1)
    greet(
        [core]
        + [peer("fsdp", 2 * r) for r in range(1, ys)]
        + [peer("dp", r) for r in range(1, dp)]
        + [mate, peer("seq", 3)]
    )

    cuts = ((0, BLK), (BLK, local - BLK))

    def token(i):
        at = pl.ds(*cuts[i])
        return remote(tokens.at[at], theirs.at[at], tok_s.at[i], tok_r.at[i], mate)

    load = pltpu.make_async_copy(tokens, mine, tok_l.at[0])
    load.start()
    token(0).start()
    token(1).start()

    rows = wqkv.shape[0]

    def band(r):
        return pl.ds(pl.multiple_of((f ^ r) * rows, 16), rows)

    def source(c):
        return wqkv.at[:, pl.ds(pl.multiple_of(c * d + parity * half, 128), half)]

    def cols(c):
        return pl.ds(c * half, half)

    def q_local(c):
        return pltpu.make_async_copy(source(c), w.at[band(0), cols(c)], q_l.at[c])

    def q_core(c):
        return remote(source(c), w.at[band(0), cols(c)], q_cs.at[c], q_cr.at[c], core)

    def q_y(c, r):
        at = (c, r - 1)
        return remote(source(c), w.at[band(0), cols(c)], q_ys.at[at], q_yr.at[at], peer("fsdp", 2 * r))

    def q_far(c, r):
        at = (c, r - 1)
        here = w.at[band(2 * r), cols(c)]
        return remote(here, here, q_fs.at[at], q_fr.at[at], core)

    for c in range(3):
        for r in range(1, ys):
            q_y(c, r).start()
        q_core(c).start()
        q_local(c).start()

    shards, wholes = (held_o, held_u, held_d), (wo_all, wu_all, wd_all)

    def hold(i):
        return pltpu.make_async_copy((wo, wu, wd)[i], shards[i], h_l.at[i])

    def whole_shard(i):
        n = shards[i].shape[0]
        return wholes[i].at[pl.ds(pl.multiple_of(f * n, 16), n)]

    def s_local(i):
        return pltpu.make_async_copy(shards[i], whole_shard(i), s_l.at[i])

    def s_core(i):
        return remote(shards[i], whole_shard(i), s_cs.at[i], s_cr.at[i], core)

    units = [(0, 0)] + [(1, j) for j in range(4)] + [(2, j) for j in range(4)]

    def piece(u, owner, part, shard=False):
        which, j = units[u]
        n = shards[which].shape[0]
        sub = n // dp
        base = part * sub if shard else owner * n + part * sub
        ref = shards[which] if shard else wholes[which]
        if which == 0:
            return ref.at[pl.ds(pl.multiple_of(base, 16), sub)]
        if which == 1:
            wide = ref.shape[1] // 4
            return ref.at[pl.ds(pl.multiple_of(base, 16), sub), pl.ds(j * wide, wide)]
        return ref.at[pl.ds(pl.multiple_of(base + j * (sub // 4), 16), sub // 4)]

    def w_y(u, r):
        at = (u, r - 1)
        return remote(piece(u, f, x, True), piece(u, f, x), y_s.at[at], y_r.at[at], peer("fsdp", 2 * r))

    def w_x(u, r, t):
        at = (u, r - 1, t - 1)
        here = piece(u, f ^ (2 * r), x)
        return remote(here, here, x_s.at[at], x_r.at[at], peer("dp", t))

    def w_fy(u, r):
        at = (u, r - 1)
        here = piece(u, f ^ (2 * r), x)
        return remote(here, here, fy_s.at[at], fy_r.at[at], core)

    def w_fx(u, r, t):
        at = (u, r - 1, t - 1)
        here = piece(u, f ^ (2 * r), x ^ t)
        return remote(here, here, fx_s.at[at], fx_r.at[at], core)

    def issue(u):
        if u < len(units):
            for r in range(1, ys):
                w_y(u, r).start()

    def came_y(u):
        for r in range(1, ys):
            w_y(u, r).wait_recv()
        issue(u + 3)
        for r in range(1, ys):
            for t in range(1, dp):
                w_x(u, r, t).start()
            w_fy(u, r).start()

    def came_x(u):
        for r in range(1, ys):
            for t in range(1, dp):
                w_x(u, r, t).wait_recv()
                w_fx(u, r, t).start()

    def normalise_rows(src, at, count):
        def body(i, carry):
            here = pl.ds(pl.multiple_of(i * 128, 128), 128)
            there = pl.ds(pl.multiple_of(at + i * 128, 128), 128)
            hat, _ = normalise(src[here, :].astype(F32))
            value = (hat * gain[...] + bias[...]).astype(BF16)
            normed[there, :] = value
            n_t[:, there] = value.T
            return carry

        lax.fori_loop(count[0], count[1], body, 0)

    def project(at, c):
        here = pl.ds(pl.multiple_of(at, 128), local)
        (q, k, v)[c][here, :] = nn(normed[here, :], w[:, c * half : (c + 1) * half]).astype(BF16)

    for i in range(3):
        hold(i).start()
    load.wait()
    normalise_rows(mine, parity * local, (0, local // 128))
    for c in range(3):
        q_local(c).wait()
        q_core(c).wait_recv()
        for r in range(1, ys):
            q_y(c, r).wait_recv()
            q_far(c, r).start()
        if c == 0:
            for i in range(3):
                hold(i).wait()
            issue(0)
            for i in range(3):
                s_local(i).start()
                s_core(i).start()
        elif c == 1:
            issue(1)
        else:
            issue(2)
        for r in range(1, ys):
            q_far(c, r).wait_recv()
        if c == 0:
            token(0).wait_recv()
            index = lax.broadcasted_iota(jnp.int32, (BLK, 1), 0)
            made[...] = jnp.where(
                index < info[7], theirs[0:BLK, :].astype(F32), mine[local - BLK : local, :].astype(F32)
            ).astype(BF16)

            @pl.when(s < 2)
            def _():
                pads[...] = made[...]

        project(parity * local, c)
        if c == 0:

            @pl.when(s == 1)
            def _():
                remote(made, pads, pad_s.at[0], pad_r.at[0], peer("seq", 3)).start()

    w_store = pltpu.make_async_copy(w, w_out, out_l.at[0])
    w_store.start()
    forward_pads = remote(pads, pads, pad_s.at[1], pad_r.at[1], mate)

    @pl.when(s == 2)
    def _():
        remote(made, pads, pad_s.at[0], pad_r.at[0], peer("seq", 3)).wait_recv()
        forward_pads.start()

    away = (1 - parity) * local
    normalise_rows(theirs, away, (0, BLK // 128))
    came_y(0)
    token(1).wait_recv()
    normalise_rows(theirs, away, (BLK // 128, local // 128))
    for c in range(3):
        project(away, c)
    stores = [
        pltpu.make_async_copy(a, b, out_l.at[1 + i])
        for i, (a, b) in enumerate(((q, q_out), (k, k_out), (v, v_out), (n_t, n_out), (theirs, tok_out)))
    ]
    for copy in stores:
        copy.start()
    came_y(1)
    came_x(0)

    @pl.when(s == 3)
    def _():
        forward_pads.wait_recv()

    hat, _ = normalise(pads[...].astype(F32))
    value = (hat * gain[...] + bias[...]).astype(BF16)
    np_t[...] = value.T
    kp[...] = nn(value, w[:, half : 2 * half]).astype(BF16)
    vp[...] = nn(value, w[:, 2 * half :]).astype(BF16)
    late = [
        pltpu.make_async_copy(a, b, out_l.at[6 + i])
        for i, (a, b) in enumerate(((np_t, np_out), (kp, kp_out), (vp, vp_out), (pads, pad_out)))
    ]
    for copy in late:
        copy.start()
    came_y(2)
    came_x(1)

    def give(i):
        lanes = pl.ds(pl.multiple_of(i * 2 * HD, 128), 2 * HD)
        return remote(
            mixed.at[pl.ds(pl.multiple_of(away, 16), local), lanes], other.at[:, lanes], o_s.at[i], o_r.at[i], mate
        )

    pairs = half // (2 * HD)
    done_y, done_x = 3, 2
    for i in range(pairs):
        lanes = slice(i * 2 * HD, (i + 1) * 2 * HD)

        def put(at, value):
            mixed[at, lanes] = value

        def put_lse(h, at, value):
            lse[i, h : h + 1, at] = value

        attend_pair(
            bounds,
            lambda at: q[at, lanes],
            lambda at: k[at, lanes],
            lambda at: v[at, lanes],
            lambda at: kp[at, lanes],
            lambda at: vp[at, lanes],
            put,
            put_lse,
        )
        give(i).start()
        came_y(done_y)
        came_x(done_x)
        done_y, done_x = done_y + 1, done_x + 1
    last = [
        pltpu.make_async_copy(mixed, mix_out, out_l.at[10]),
        pltpu.make_async_copy(lse, lse_out, out_l.at[11]),
    ]
    for copy in last:
        copy.start()
    for u in range(done_y, len(units)):
        came_y(u)
        came_x(u - 1)
    came_x(len(units) - 1)

    for i in range(pairs):
        give(i).wait()
    for i in range(3):
        s_local(i).wait()
        s_core(i).wait()
    for u in range(len(units)):
        for r in range(1, ys):
            w_y(u, r).wait_send()
            w_fy(u, r).wait()
            for t in range(1, dp):
                w_x(u, r, t).wait_send()
                w_fx(u, r, t).wait()
    for c in range(3):
        q_core(c).wait_send()
        for r in range(1, ys):
            q_y(c, r).wait_send()
            q_far(c, r).wait_send()
    token(0).wait_send()
    token(1).wait_send()

    @pl.when(s == 1)
    def _():
        remote(made, pads, pad_s.at[0], pad_r.at[0], peer("seq", 3)).wait_send()

    @pl.when(s == 2)
    def _():
        forward_pads.wait_send()

    for copy in [w_store] + stores + late + last:
        copy.wait()


def front(info, tokens, wqkv, wo, wu, wd, gain, bias, fsdp, dp):
    local, d = tokens.shape
    half, ff = d // 2, wu.shape[1]
    pairs = half // (2 * HD)
    y, px, n = max(fsdp // 2 - 1, 1), max(dp - 1, 1), 9
    dma = pltpu.SemaphoreType.DMA
    outs = [((2 * local, half), BF16)] * 3 + [
        ((d, 2 * local), BF16),
        ((d, BLK), BF16),
        ((BLK, half), BF16),
        ((BLK, half), BF16),
        ((d, 3 * half), BF16),
        ((2 * local, half), BF16),
        ((pairs, 2, 2 * local), F32),
        ((local, half), BF16),
        ((local, d), BF16),
        ((BLK, d), BF16),
        ((d, d), BF16),
        ((d, ff), BF16),
        ((ff, d), BF16),
    ]
    buffers = [
        (local, d), (local, d), (BLK, d), (BLK, d), (d, 3 * half), (2 * local, d), (d, 2 * local), (d, BLK),
        (2 * local, half), (2 * local, half), (2 * local, half), (BLK, half), (BLK, half), (2 * local, half),
        wo.shape, wu.shape, wd.shape,
    ]
    sems = [(1,), (2,), (2,), (2,), (2,), (3,), (3,), (3,), (3, y), (3, y), (3, y), (3, y)]
    sems += [(3,)] * 4 + [(n, y)] * 2 + [(n, y, px)] * 2 + [(n, y)] * 2 + [(n, y, px)] * 2 + [(pairs,)] * 2 + [(12,)]
    return pl.pallas_call(
        functools.partial(front_body, fsdp=fsdp, dp=dp),
        in_specs=[pl.BlockSpec(memory_space=pltpu.SMEM)] + [hbm()] * 5 + [pl.BlockSpec(memory_space=pltpu.VMEM)] * 2,
        out_specs=[hbm()] * len(outs),
        out_shape=[shape(*o) for o in outs],
        scratch_shapes=[pltpu.VMEM(b, BF16) for b in buffers]
        + [pltpu.VMEM((pairs, 2, 2 * local), F32)]
        + [dma(s) for s in sems],
        compiler_params=pltpu.CompilerParams(vmem_limit_bytes=VMEM_LIMIT, collective_id=1, has_side_effects=True),
        cost_estimate=pl.CostEstimate(flops=10**10, bytes_accessed=10**8, transcendentals=0),
    )(info, tokens, wqkv, wo, wu, wd, gain, bias)


def forward_body(
    info, own, other, x, up, gains, biases, wo, wu, wd, out, g_feed, act_t, slope, n_t, branch, middle, edges, normed, feed
):
    parity = info[1]
    step, last = pl.program_id(0), pl.num_programs(0) - 1
    half = own.shape[1]
    blocks = x.shape[0] // 128

    @pl.when(step == 0)
    def _():
        w_own = wo[pl.ds(pl.multiple_of(parity * half, 128), half), :]
        w_other = wo[pl.ds(pl.multiple_of((1 - parity) * half, 128), half), :]
        branch[...] = nn(own[...], w_own) + nn(other[...], w_other)

        def rows(i, carry):
            at = pl.ds(pl.multiple_of(i * 128, 128), 128)
            hat, _ = normalise(branch[at, :])
            mid = x[at, :].astype(F32) + hat * gains[1:2, :] + biases[1:2, :]
            middle[at, :] = mid
            hat, _ = normalise(mid)
            two = (hat * gains[2:3, :] + biases[2:3, :]).astype(BF16)
            normed[at, :] = two
            n_t[:, at] = two.T
            return carry

        lax.fori_loop(0, blocks, rows, 0)
        feed[...] = jnp.zeros_like(feed)

    u = nn(normed[...], wu[...])
    th = jnp.tanh(0.7978845608 * (u + 0.044715 * (u * u * u)))
    act = (0.5 * u * (1.0 + th)).astype(BF16)
    slope[...] = (
        0.5 * (1.0 + th) + 0.5 * u * (1.0 - th * th) * (0.7978845608 + (3 * 0.044715 * 0.7978845608) * (u * u))
    ).astype(BF16)
    act_t[...] = act.T
    feed[...] += nn(act, wd[...])

    @pl.when(step == last)
    def _():
        def rows(i, carry):
            at = pl.ds(pl.multiple_of(i * 128, 128), 128)
            g = up[at, :].astype(F32)
            hat, rstd = normalise(feed[at, :])
            gain = gains[3:4, :]
            out[at, :] = (middle[at, :] + hat * gain + biases[3:4, :]).astype(BF16)
            g_feed[at, :] = norm_back(g, hat, rstd, gain).astype(BF16)
            return (
                carry[0] + jnp.sum(g * hat, axis=0, keepdims=True),
                carry[1] + jnp.sum(g, axis=0, keepdims=True),
            )

        zero = jnp.zeros((1, x.shape[1]), F32)
        a, b = lax.fori_loop(0, blocks, rows, (zero, zero))
        edges[0:1, :] = a
        edges[1:2, :] = b


def forward(info, mixed, other, x, up, gains, biases, wo, wu, wd):
    local, d = x.shape
    half, ff = mixed.shape[1], wu.shape[1]
    tile = 512
    once = lambda s: pl.BlockSpec(s, lambda *_: (0,) * len(s), pipeline_mode=pl.Buffered(1))
    return call(
        forward_body,
        (ff // tile,),
        1,
        [
            pl.BlockSpec((local, half), lambda i, info: (info[1], 0), pipeline_mode=pl.Buffered(1)),
            once(other.shape),
            once(x.shape),
            once(up.shape),
            once(gains.shape),
            once(biases.shape),
            once(wo.shape),
            pl.BlockSpec((d, tile), lambda i, info: (0, i)),
            pl.BlockSpec((tile, d), lambda i, info: (i, 0)),
        ],
        [
            full((local, d)),
            full((local, d)),
            pl.BlockSpec((tile, local), lambda i, info: (i, 0)),
            pl.BlockSpec((local, tile), lambda i, info: (0, i)),
            full((d, local)),
            full((local, d)),
            full((local, d)),
            full((2, d)),
        ],
        [
            shape((local, d), BF16),
            shape((local, d), BF16),
            shape((ff, local), BF16),
            shape((local, ff), BF16),
            shape((d, local), BF16),
            shape((local, d), F32),
            shape((local, d), F32),
            shape((2, d), F32),
        ],
        [pltpu.VMEM((local, d), BF16), pltpu.VMEM((local, d), F32)],
        flops=2 * local * d * (d + 2 * ff),
        moved=40e6,
    )(info, mixed, other, x, up, gains, biases, wo, wu, wd)


def back_body(info, g_feed, slope, wd, wu, hid_out, g_two):
    r = pl.program_id(0)
    hid = (nt(g_feed[...], wd[...]) * slope[...].astype(F32)).astype(BF16)
    pieces, _, width = hid_out.shape
    for c in range(pieces):
        hid_out[c] = hid[:, c * width : (c + 1) * width]
    part = nt(hid, wu[...])

    @pl.when(r == 0)
    def _():
        g_two[...] = part

    @pl.when(r != 0)
    def _():
        g_two[...] += part


def back(info, g_feed, slope, wd, wu, fsdp):
    local, d = g_feed.shape
    ff = wd.shape[0]
    tile = ff // fsdp
    return call(
        back_body,
        (fsdp,),
        1,
        [
            full((local, d)),
            pl.BlockSpec((local, tile), lambda i, info: (0, i)),
            pl.BlockSpec((tile, d), lambda i, info: (i, 0)),
            pl.BlockSpec((d, tile), lambda i, info: (0, i)),
        ],
        [pl.BlockSpec((PIECES, local, tile // PIECES), lambda i, info: (0, 0, i)), full((local, d))],
        [shape((PIECES, local, ff // PIECES), BF16), shape((local, d), F32)],
        flops=4 * local * d * ff,
        moved=35e6,
    )(info, g_feed, slope, wd, wu)


def middle_body(info, g, middle, branch, up, gains, wo, g_mid, d_own, d_send, gbr, edges):
    parity = info[1]
    step, last = pl.program_id(0), pl.num_programs(0) - 1
    half = d_own.shape[1]

    @pl.when(step == 0)
    def _():
        edges[...] = jnp.zeros_like(edges)

    g = g[...]
    hat, rstd = normalise(middle[...])
    edges[2:3, :] += jnp.sum(g * hat, axis=0, keepdims=True)
    edges[3:4, :] += jnp.sum(g, axis=0, keepdims=True)
    gm = up[...].astype(F32) + norm_back(g, hat, rstd, gains[2:3, :])
    g_mid[...] = gm
    hat, rstd = normalise(branch[...])
    edges[0:1, :] += jnp.sum(gm * hat, axis=0, keepdims=True)
    edges[1:2, :] += jnp.sum(gm, axis=0, keepdims=True)
    gr = norm_back(gm, hat, rstd, gains[1:2, :]).astype(BF16)
    gbr[pl.ds(pl.multiple_of(step * gr.shape[0], 16), gr.shape[0]), :] = gr

    @pl.when(step == last)
    def _():
        grad = gbr[...]
        d_send[...] = nt(grad, wo[pl.ds(pl.multiple_of((1 - parity) * half, 128), half), :]).astype(BF16)
        d_own[...] = nt(grad, wo[pl.ds(pl.multiple_of(parity * half, 128), half), :]).astype(BF16)


def middle_back(info, g, middle, branch, up, gains, wo):
    local, d = g.shape
    rows, half = 128, d // 2
    block = pl.BlockSpec((rows, d), lambda i, info: (i, 0))
    return call(
        middle_body,
        (local // rows,),
        1,
        [block, block, block, block, full(gains.shape), full(wo.shape)],
        [block, full((local, half)), full((local, half)), full((local, d)), full((4, d))],
        [
            shape((local, d), F32),
            shape((local, half), BF16),
            shape((local, half), BF16),
            shape((local, d), BF16),
            shape((4, d), F32),
        ],
        flops=2 * local * d * d,
        moved=18e6,
    )(info, g, middle, branch, up, gains, wo)


class Lane:
    names = ("core_s", "core_r", "y_s", "y_r", "x_s", "x_r", "z_s", "z_r", "zz_s", "zz_r", "xx_s", "xx_r", "own")

    @staticmethod
    def scratch(count, rows, cols, fsdp, dp, masks):
        y, parts = fsdp // 2, len(masks) + 1
        dma = pltpu.SemaphoreType.DMA
        sems = [(count,), (count,)]
        sems += [(count, max(y - 1, 1))] * 2 + [(count, max(dp - 1, 1))] * 2
        sems += [(count, len(masks))] * 4 + [(count, max(dp - 1, 1))] * 2 + [(count,)]
        return [
            pltpu.VMEM((count, y, rows, cols), BF16),
            pltpu.VMEM((count, max(y - 1, 1), rows, cols), BF16),
            pltpu.VMEM((count, max(dp - 1, 1), rows // dp, cols), BF16),
            pltpu.VMEM((count, len(masks), rows // dp, cols // parts), BF16),
        ] + [dma(s) for s in sems]

    size = 4 + 13

    def __init__(self, refs, final, fsdp, dp, masks, unit):
        self.acc, self.y_in, self.x_in, self.z_in = refs[:4]
        self.sems = dict(zip(self.names, refs[4:]))
        self.final = final
        self.ys, self.dp, self.masks = fsdp // 2, dp, masks
        self.count, _, self.rows, self.cols = self.acc.shape
        self.x = lax.axis_index("dp")
        self.part = self.cols // (len(masks) + 1)
        self.unit = unit

    def place(self, mask=0):
        at = (lax.axis_index("seq") ^ mask) // self.unit % (len(self.masks) + 1)
        return pl.ds(pl.multiple_of(at * self.part, 128), self.part)

    def band(self, mask=0):
        n = self.rows // self.dp
        return pl.ds(pl.multiple_of((self.x ^ mask) * n, 16), n)

    def core(self, u, src):
        return remote(src, self.acc.at[u], self.sems["core_s"].at[u], self.sems["core_r"].at[u], peer("fsdp", 1))

    def over_y(self, u, ry):
        s = self.sems
        return remote(
            self.acc.at[u, ry], self.y_in.at[u, ry - 1], s["y_s"].at[u, ry - 1], s["y_r"].at[u, ry - 1], peer("fsdp", 2 * ry)
        )

    def over_x(self, u, rx):
        s = self.sems
        return remote(
            self.acc.at[u, 0, self.band(rx)],
            self.x_in.at[u, rx - 1],
            s["x_s"].at[u, rx - 1],
            s["x_r"].at[u, rx - 1],
            peer("dp", rx),
        )

    def over_z(self, u, i):
        s, m = self.sems, self.masks[i]
        return remote(
            self.acc.at[u, 0, self.band(), self.place(m)],
            self.z_in.at[u, i],
            s["z_s"].at[u, i],
            s["z_r"].at[u, i],
            peer("seq", m),
        )

    def back_z(self, u, i):
        s, m = self.sems, self.masks[i]
        return remote(
            self.acc.at[u, 0, self.band(), self.place()],
            self.final.at[u, self.band(), self.place()],
            s["zz_s"].at[u, i],
            s["zz_r"].at[u, i],
            peer("seq", m),
        )

    def back_x(self, u, rx):
        s = self.sems
        at = self.final.at[u, self.band()]
        return remote(at, at, s["xx_s"].at[u, rx - 1], s["xx_r"].at[u, rx - 1], peer("dp", rx))

    def keep(self, u):
        return pltpu.make_async_copy(
            self.acc.at[u, 0, self.band(), self.place()],
            self.final.at[u, self.band(), self.place()],
            self.sems["own"].at[u],
        )

    def add(self, target, sources):
        rows = target.shape[0]
        step = 64 if rows % 64 == 0 else 16

        def body(i, carry):
            at = pl.ds(pl.multiple_of(i * step, 16), step)
            total = target[at, :].astype(F32)
            for src in sources:
                total = total + src[at, :].astype(F32)
            target[at, :] = total.astype(BF16)
            return carry

        lax.fori_loop(0, rows // step, body, 0)

    def start_y(self, u):
        for ry in range(1, self.ys):
            self.over_y(u, ry).start()

    def two(self, u):
        for ry in range(1, self.ys):
            self.over_y(u, ry).wait_recv()
        self.add(self.acc.at[u, 0], [self.y_in.at[u, ry - 1] for ry in range(1, self.ys)])
        for rx in range(1, self.dp):
            self.over_x(u, rx).start()

    def three(self, u):
        for rx in range(1, self.dp):
            self.over_x(u, rx).wait_recv()
        self.add(self.acc.at[u, 0, self.band()], [self.x_in.at[u, rx - 1] for rx in range(1, self.dp)])
        for i in range(len(self.masks)):
            self.over_z(u, i).start()

    def four(self, u):
        for i in range(len(self.masks)):
            self.over_z(u, i).wait_recv()
        self.add(
            self.acc.at[u, 0, self.band(), self.place()], [self.z_in.at[u, i] for i in range(len(self.masks))]
        )
        self.keep(u).start()
        for i in range(len(self.masks)):
            self.back_z(u, i).start()

    def five(self, u):
        self.keep(u).wait()
        for i in range(len(self.masks)):
            self.back_z(u, i).wait_recv()
        for rx in range(1, self.dp):
            self.back_x(u, rx).start()

    def six(self, u):
        for rx in range(1, self.dp):
            self.back_x(u, rx).wait_recv()

    def drain(self, u):
        for ry in range(1, self.ys):
            self.over_y(u, ry).wait_send()
        for rx in range(1, self.dp):
            self.over_x(u, rx).wait_send()
            self.back_x(u, rx).wait_send()
        for i in range(len(self.masks)):
            self.over_z(u, i).wait_send()
            self.back_z(u, i).wait_send()


def partners(fsdp, dp):
    return (
        [peer("fsdp", 1)]
        + [peer("fsdp", 2 * ry) for ry in range(1, fsdp // 2)]
        + [peer("dp", rx) for rx in range(1, dp)]
        + [peer("seq", m) for m in (1, 2, 3)]
    )


def doublings(fsdp, dp, seq):
    steps = []
    for axis, size in (("fsdp", fsdp), ("dp", dp), ("seq", seq)):
        m = 1
        while m < size:
            steps.append((axis, m))
            m *= 2
    return steps


def rear_body(
    info, d_send, d_own, act_t, hid, g_feed, two_t, mixed_rows, other, gbr, q, k, v, mixed, kp, vp, lse,
    w, n_t, np_t, tokens, theirs, padx, g_mid, gains, edges3, edges12,
    final_a, final_b, grad_in, sums,
    *rest, fsdp, dp, seq
):
    a = Lane(rest[: Lane.size], final_a, fsdp, dp, (1, 2, 3), 1)
    rest = rest[Lane.size :]
    parity = lax.axis_index("seq") % 2
    b = Lane(rest[: Lane.size], final_b.at[parity], fsdp, dp, (2,), 2)
    (
        ring, ring_b, do, dq, dk, dv, dkp, dvp, dk_sum, dv_sum, dkp_sum, dvp_sum,
        g_out, g_in, gp_out, gp_in, run, got, load, d_s, d_r, gs_s, gs_r, gp_s, gp_r, e_s, e_r, p_s, p_r,
    ) = rest[Lane.size :]
    f, s = lax.axis_index("fsdp"), lax.axis_index("seq")
    local, half = d_own.shape
    d = 2 * half
    ys = fsdp // 2
    rows = a.rows
    mate = peer("seq", 1)
    bounds = tuple(info[i] for i in range(2, 6))
    greet(partners(fsdp, dp))

    my_rows = pl.ds(pl.multiple_of(parity * local, 128), local)
    mate_rows = pl.ds(pl.multiple_of((1 - parity) * local, 128), local)
    give = remote(d_send, do.at[my_rows], d_s.at[0], d_r.at[0], mate)
    give.start()
    take = pltpu.make_async_copy(d_own, do.at[my_rows], load.at[0])
    take.start()

    def shard(r):
        return r ^ f

    def band(r):
        return pl.ds(pl.multiple_of(shard(r) * rows, 16), rows)

    def feed_phase(act_v, hid_v, g_v, two_v, att, gbr_v):
        def fetch(c):
            return [
                pltpu.make_async_copy(act_t.at[:, c], act_v.at[c], load.at[1 + c]),
                pltpu.make_async_copy(hid.at[c], hid_v.at[c], load.at[1 + PIECES + c]),
            ]

        base = 1 + 2 * PIECES
        common = [
            pltpu.make_async_copy(g_feed, g_v, load.at[base]),
            pltpu.make_async_copy(two_t, two_v, load.at[base + 1]),
        ]
        attn = [
            pltpu.make_async_copy(
                mixed_rows.at[parity], att.at[:, pl.ds(pl.multiple_of(parity * half, 128), half)], load.at[base + 2]
            ),
            pltpu.make_async_copy(
                other, att.at[:, pl.ds(pl.multiple_of((1 - parity) * half, 128), half)], load.at[base + 3]
            ),
            pltpu.make_async_copy(gbr, gbr_v, load.at[base + 4]),
        ]
        for copy in common[:1] + fetch(0) + common[1:]:
            copy.start()
        for c in range(1, PIECES):
            for copy in fetch(c):
                copy.start()
        for copy in attn:
            copy.start()
        for copy in common:
            copy.wait()

        def down(c, r):
            return nn(act_v[c, shard(r)], g_v[...])

        def up(c, r):
            return nn(two_v[band(r), :], hid_v[c])

        def step(c, carry):
            @pl.when(c < PIECES)
            def _():
                for kind in range(2):
                    pltpu.make_async_copy(
                        (act_t.at[:, c], hid.at[c])[kind],
                        (act_v.at[c], hid_v.at[c])[kind],
                        load.at[1 + kind * PIECES + c],
                    ).wait()
                for kind, make in ((0, down), (1, up)):
                    u = 2 * c + kind
                    slot = ring.at[u % 4]

                    @pl.when(c >= 2)
                    def _():
                        a.core(u - 4, slot).wait_send()

                    for ry in range(ys):
                        slot[ry] = make(c, 2 * ry + 1).astype(BF16)
                    a.core(u, slot).start()

            @pl.when(c >= 1)
            def _():
                for kind, make in ((0, down), (1, up)):
                    u = 2 * (c - 1) + kind
                    a.core(u, ring.at[u % 4]).wait_recv()
                    for ry in range(ys):
                        a.acc[u, ry] = (make(c - 1, 2 * ry) + a.acc[u, ry].astype(F32)).astype(BF16)

                    @pl.when(c == 1)
                    def _():
                        a.start_y(u)

            return carry

        lax.fori_loop(0, PIECES + 1, step, 0)
        u = 2 * PIECES
        a.core(u - 4, ring.at[0]).wait_send()
        for copy in attn:
            copy.wait()
        for ry in range(ys):
            ring[0, ry] = tn(att[:, band(2 * ry + 1)], gbr_v[...]).astype(BF16)
        a.core(u, ring.at[0]).start()
        for ry in range(ys):
            held = tn(att[:, band(2 * ry)], gbr_v[...])
            if ry == 0:
                a.core(u, ring.at[0]).wait_recv()
            a.acc[u, ry] = (held + a.acc[u, ry].astype(F32)).astype(BF16)

    def tick(t):
        plan = ((0, "two"), (-2, "start_y"), (1, "three"), (2, "four"), (3, "five"), (4, "six"), (5, "seven"))
        for offset, name in plan:
            for lane, first in ((a, 0), (b, a.count)):
                u = t - offset - first
                if name == "start_y" and lane is a and isinstance(u, int) and u < 2:
                    continue
                if name == "seven":
                    if lane is a or not isinstance(t, int) or not 0 <= u < lane.count:
                        continue
                    seven(u).start()
                    continue
                if isinstance(u, int):
                    if 0 <= u < lane.count:
                        getattr(lane, name)(u)
                elif lane is a:

                    @pl.when((u >= 0) & (u < lane.count))
                    def _():
                        getattr(lane, name)(u)

    def seven(u):
        here = final_b.at[parity, u]
        return remote(here, here, p_s.at[u], p_r.at[u], mate)

    def attention_phase(q_v, k_v, v_v, o_v, kp_v, vp_v, lse_v):
        pairs = ((q, q_v), (k, k_v), (v, v_v), (mixed, o_v), (kp, kp_v), (vp, vp_v), (lse, lse_v))
        copies = [pltpu.make_async_copy(x, y, load.at[16 + i]) for i, (x, y) in enumerate(pairs)]
        for copy in copies:
            copy.start()
        take.wait()
        for copy in copies:
            copy.wait()
        give.wait_recv()

        def step(i, carry):
            lanes = pl.ds(pl.multiple_of(i * 2 * HD, 128), 2 * HD)

            def put(at, value):
                dq[at, lanes] = value

            attend_back_pair(
                bounds,
                lambda at: q_v[at, lanes],
                lambda at: k_v[at, lanes],
                lambda at: v_v[at, lanes],
                lambda at: kp_v[at, lanes],
                lambda at: vp_v[at, lanes],
                lambda at: o_v[at, lanes],
                lambda h, at: lse_v[i, h : h + 1, at],
                lambda at: do[at, lanes],
                put,
                dk_sum,
                dv_sum,
                dkp_sum,
                dvp_sum,
            )
            dk[:, lanes] = (dk_sum[...] * 0.125).astype(BF16)
            dv[:, lanes] = dv_sum[...].astype(BF16)
            dkp[:, lanes] = (dkp_sum[...] * 0.125).astype(BF16)
            dvp[:, lanes] = dvp_sum[...].astype(BF16)
            tick(i)
            return carry

        lax.fori_loop(0, half // (2 * HD), step, 0)

    steps = doublings(fsdp, dp, seq)

    def double(i):
        axis, m = steps[i]
        return remote(run.at[i], got.at[i], e_s.at[i], e_r.at[i], peer(axis, m))

    def double_start(i):
        double(i).start()

    def double_end(i):
        double(i).wait_recv()
        run[i + 1] = run[i] + got[i]

    def project_phase(w_v, nt_v, npt_v, x_v, y_v, px_v, mid_v, own, out_v):
        pairs = (
            (w, w_v), (n_t, nt_v), (np_t, npt_v), (padx, px_v), (theirs, y_v), (tokens, x_v), (g_mid, mid_v),
        )
        copies = [pltpu.make_async_copy(x, y, load.at[16 + i]) for i, (x, y) in enumerate(pairs)]
        for copy in copies:
            copy.start()
        gain = gains[0:1, :]
        back_rows = (dq, dk, dv)
        back_pads = (None, dkp, dvp)

        def grad(c, r):
            total = nn(nt_v[band(r), :], back_rows[c][...])
            if c:
                total = total + nn(npt_v[band(r), :], back_pads[c][...])
            return total

        for copy in copies[:3]:
            copy.wait()
        for c in range(3):
            for ry in range(ys):
                ring_b[c, ry] = grad(c, 2 * ry + 1).astype(BF16)
            b.core(c, ring_b.at[c]).start()
        for c in range(3):
            for ry in range(ys):
                held = grad(c, 2 * ry)
                if ry == 0:
                    b.core(c, ring_b.at[c]).wait_recv()
                b.acc[c, ry] = (held + b.acc[c, ry].astype(F32)).astype(BF16)
        tick(4)

        def weight(c):
            return w_v[:, c * half : (c + 1) * half]

        def count(g, x):
            hat, _ = normalise(x.astype(F32))
            return jnp.sum(g * hat, axis=0, keepdims=True), jnp.sum(g, axis=0, keepdims=True)

        for copy in copies[3:]:
            copy.wait()
        g = nt(dkp[...], weight(1)) + nt(dvp[...], weight(2))
        gp_out[...] = g.astype(BF16)
        for i in range(2):
            back_pad = remote(gp_out, gp_in.at[i], gp_s.at[i], gp_r.at[i], peer("seq", 2 + i))

            @pl.when(s >= 2)
            def _():
                back_pad.start()

        edge = count(g, px_v[...])

        def through(first, source, store):
            def body(i, carry):
                at = pl.ds(pl.multiple_of(first + i * 128, 128), 128)
                here = pl.ds(pl.multiple_of(i * 128, 128), 128)
                g = nt(dq[at, :], weight(0)) + nt(dk[at, :], weight(1)) + nt(dv[at, :], weight(2))
                store(here, g)
                one, two = count(g, source[here, :])
                return carry[0] + one, carry[1] + two

            return lax.fori_loop(0, local // 128, body, edge)

        def store_out(at, value):
            g_out[at, :] = value.astype(BF16)

        def store_own(at, value):
            own[at, :] = value

        edge = through((1 - parity) * local, y_v, store_out)
        pass_rows = remote(g_out, g_in, gs_s.at[0], gs_r.at[0], mate)
        pass_rows.start()
        edge = through(parity * local, x_v, store_own)
        order = (edge[0], edges12[0:1, :], edges12[2:3, :], edges3[0:1, :])
        order += (edge[1], edges12[1:2, :], edges12[3:4, :], edges3[1:2, :])
        for i, value in enumerate(order):
            run[0, i : i + 1, :] = value
        double_start(0)
        tick(5)
        pending = 0
        t = 6
        while pending < len(steps):
            for _ in range(2):
                if pending < len(steps):
                    double_end(pending)
                    pending += 1
                    if pending < len(steps):
                        double_start(pending)
            tick(t)
            t += 1
        last = pltpu.make_async_copy(run.at[len(steps)], sums, load.at[24])
        last.start()

        pass_rows.wait_recv()
        for i in range(2):
            back_pad = remote(gp_out, gp_in.at[i], gp_s.at[i], gp_r.at[i], peer("seq", 2 + i))

            @pl.when(s < 2)
            def _():
                back_pad.wait_recv()

            @pl.when(s >= 2)
            def _():
                back_pad.wait_send()

        @pl.when(s < 2)
        def _():
            row = lax.broadcasted_iota(jnp.int32, (BLK, 1), 0)
            mine = ((s == 0) & (row < info[7])) | ((s == 1) & (row >= info[8]))
            extra = jnp.where(mine, gp_in[0].astype(F32) + gp_in[1].astype(F32), 0.0)
            at = pl.ds(pl.multiple_of(jnp.where(s == 0, 0, local - BLK), 128), BLK)
            own[at, :] += extra

        def finish(i, carry):
            at = pl.ds(pl.multiple_of(i * 128, 128), 128)
            hat, rstd = normalise(x_v[at, :].astype(F32))
            g = own[at, :] + g_in[at, :].astype(F32)
            out_v[at, :] = (mid_v[at, :] + norm_back(g, hat, rstd, gain)).astype(BF16)
            return carry

        lax.fori_loop(0, local // 128, finish, 0)
        leave = pltpu.make_async_copy(out_v, grad_in, load.at[25])
        leave.start()
        end = a.count + b.count + 5
        while t <= end:
            tick(t)
            t += 1
        for u in range(b.count):
            seven(u).wait()
        pass_rows.wait_send()
        last.wait()
        leave.wait()

    dt = lambda s, t=BF16: pltpu.VMEM(s, t)
    pl.run_scoped(
        feed_phase,
        dt((PIECES, fsdp, rows, local)),
        dt((PIECES, local, d)),
        dt((local, d)),
        dt((d, local)),
        dt((local, d)),
        dt((local, d)),
    )
    pl.run_scoped(
        attention_phase,
        dt(q.shape), dt(k.shape), dt(v.shape), dt(mixed.shape), dt(kp.shape), dt(vp.shape), dt(lse.shape, F32),
    )
    pl.run_scoped(
        project_phase,
        dt(w.shape), dt(n_t.shape), dt(np_t.shape), dt(tokens.shape), dt(theirs.shape), dt(padx.shape),
        dt(g_mid.shape, F32), dt((local, d), F32), dt((local, d)),
    )
    give.wait_send()
    for u in range(2 * PIECES - 3, 2 * PIECES + 1):
        a.core(u, ring.at[u % 4]).wait_send()
    for u in range(b.count):
        b.core(u, ring_b.at[u]).wait_send()
    for lane in (a, b):
        for u in range(lane.count):
            lane.drain(u)
    for i in range(len(steps)):
        double(i).wait_send()


def rear(info, arrays, small, sizes):
    fsdp, dp, seq = sizes
    local, half = arrays[1].shape
    d = 2 * half
    rows, y = d // fsdp, fsdp // 2
    n = 2 * PIECES + 1
    steps = len(doublings(fsdp, dp, seq))
    dma = pltpu.SemaphoreType.DMA
    vm = pltpu.VMEM
    return pl.pallas_call(
        functools.partial(rear_body, fsdp=fsdp, dp=dp, seq=seq),
        in_specs=[pl.BlockSpec(memory_space=pltpu.SMEM)]
        + [hbm()] * len(arrays)
        + [pl.BlockSpec(memory_space=pltpu.VMEM)] * len(small),
        out_specs=[hbm()] * 4,
        out_shape=[
            shape((n, rows, d), BF16),
            shape((2, 3, rows, half), BF16),
            shape((local, d), BF16),
            shape((8, d), F32),
        ],
        scratch_shapes=Lane.scratch(n, rows, d, fsdp, dp, (1, 2, 3))
        + Lane.scratch(3, rows, half, fsdp, dp, (2,))
        + [vm((4, y, rows, d), BF16), vm((3, y, rows, half), BF16)]
        + [vm((2 * local, half), BF16)] * 4
        + [vm((BLK, half), BF16)] * 2
        + [vm((2 * local, 2 * HD), F32)] * 2
        + [vm((BLK, 2 * HD), F32)] * 2
        + [vm((local, d), BF16)] * 2
        + [vm((BLK, d), BF16), vm((2, BLK, d), BF16), vm((steps + 1, 8, d), F32), vm((steps, 8, d), F32)]
        + [dma((26,)), dma((1,)), dma((1,)), dma((1,)), dma((1,)), dma((2,)), dma((2,))]
        + [dma((steps,)), dma((steps,)), dma((3,)), dma((3,))],
        compiler_params=pltpu.CompilerParams(vmem_limit_bytes=VMEM_LIMIT, collective_id=0, has_side_effects=True),
        cost_estimate=pl.CostEstimate(flops=10**10, bytes_accessed=10**8, transcendentals=0),
    )(info, *arrays, *small)


def local(
    tokens, qkv_weight, out_weight, up_weight, down_weight, norm_gain, norm_bias, caption_len, item_start, grad_out
):
    x_tok, up = tokens[0], grad_out[0]
    local_rows, d = x_tok.shape
    fsdp = lax.axis_size("fsdp")
    ff = up_weight.shape[1]
    half = d // 2
    f, s = lax.axis_index("fsdp"), lax.axis_index("seq")
    parity, slot = s % 2, s // 2
    caps, starts = caption_len[0], item_start[0]
    start = jnp.where(slot == 0, starts[0], starts[1] - SLOT)
    stop = start + jnp.where(slot == 0, caps[0], caps[1]) + IMAGE
    pad_a = jnp.where(slot == 0, 0, starts[0])
    pad_b = jnp.where(slot == 0, BLK, starts[0] + caps[0])
    info = jnp.stack(
        [f, parity, start, stop, pad_a, pad_b, s, starts[0], starts[0] + caps[0]]
    ).astype(jnp.int32)

    dp = lax.axis_size("dp")
    (q, k, v, n_t, np_t, kp, vp, w_qkv, mixed, lse, other, theirs, pads, wo, wu, wd) = front(
        info, x_tok, qkv_weight, out_weight, up_weight, down_weight, norm_gain[0:1], norm_bias[0:1], fsdp, dp
    )
    (out, g_feed, act_t, slope, two_t, branch, middle, edges3) = forward(
        info, mixed, other, x_tok, up, norm_gain, norm_bias, wo, wu, wd
    )
    hid, g_two = back(info, g_feed, slope, wd, wu, fsdp)
    g_mid, d_own, d_send, gbr, edges12 = middle_back(info, g_two, middle, branch, up, norm_gain, wo)
    rows = d // fsdp
    done, done_q, grad_in, sums = rear(
        info,
        (
            d_send, d_own, act_t.reshape(fsdp, PIECES, rows, local_rows), hid, g_feed, two_t,
            mixed.reshape(2, local_rows, half), other, gbr, q, k, v, mixed, kp, vp, lse,
            w_qkv, n_t, np_t, x_tok, theirs, pads, g_mid,
        ),
        (norm_gain, edges3, edges12),
        (fsdp, dp, lax.axis_size("seq")),
    )
    grad_qkv = jnp.concatenate([done_q[h, c] for c in range(3) for h in range(2)], axis=1).astype(F32)
    grad_proj = done[-1].astype(F32)
    grad_down = jnp.concatenate([done[2 * c] for c in range(PIECES)], axis=0).astype(F32)
    grad_up = jnp.concatenate(
        [done[2 * c + 1][:, h * rows : (h + 1) * rows] for h in range(fsdp) for c in range(PIECES)], axis=1
    ).astype(F32)
    return (out[None], grad_in[None], grad_qkv, grad_proj, grad_up, grad_down, sums[0:4], sums[4:8])


def solution(mesh):
    rows = P(("fsdp", "dp"), "seq", None)
    shard = P("fsdp", None)
    items = P(("fsdp", "dp"), None)
    return jax.shard_map(
        local,
        mesh=mesh,
        in_specs=(rows, shard, shard, shard, shard, P(), P(), items, items, rows),
        out_specs=(rows, rows, shard, shard, shard, shard, P(), P()),
        check_vma=False,
    )
```

```python
import functools

import jax
import jax.numpy as jnp
from jax import lax
from jax.experimental import pallas as pl
from jax.experimental.pallas import tpu as pltpu
from jax.sharding import PartitionSpec as P

HD = 64
IMAGE = 1024
SLOT = 1280
BLK = 256
LOG2E = 1.4426950408889634
SCALE = LOG2E / 8.0
NEG = -1e30
F32 = jnp.float32
BF16 = jnp.bfloat16
VMEM_LIMIT = 60 * 1024 * 1024
PIECES = 4


def nn(a, b):
    return lax.dot_general(a, b, (((1,), (0,)), ((), ())), preferred_element_type=F32)


def nt(a, b):
    return lax.dot_general(a, b, (((1,), (1,)), ((), ())), preferred_element_type=F32)


def tn(a, b):
    return lax.dot_general(a, b, (((0,), (0,)), ((), ())), preferred_element_type=F32)


def normalise(v):
    mean = jnp.mean(v, axis=-1, keepdims=True)
    centred = v - mean
    var = jnp.mean(centred * centred, axis=-1, keepdims=True)
    rstd = lax.rsqrt(var + 1e-05)
    return centred * rstd, rstd


def norm_back(g, hat, rstd, gain):
    gg = g * gain
    return rstd * (
        gg - jnp.mean(gg, axis=-1, keepdims=True) - hat * jnp.mean(gg * hat, axis=-1, keepdims=True)
    )


def call(body, grid, prefetch, in_specs, out_specs, out_shape, scratch=(), flops=0, moved=0):
    return pl.pallas_call(
        body,
        grid_spec=pltpu.PrefetchScalarGridSpec(
            num_scalar_prefetch=prefetch,
            grid=grid,
            in_specs=in_specs,
            out_specs=out_specs,
            scratch_shapes=list(scratch),
        ),
        out_shape=out_shape,
        compiler_params=pltpu.CompilerParams(vmem_limit_bytes=VMEM_LIMIT),
        cost_estimate=pl.CostEstimate(flops=int(flops), bytes_accessed=int(moved), transcendentals=0),
    )


def full(shape):
    zeros = (0,) * len(shape)
    return pl.BlockSpec(shape, lambda *_: zeros)


def hbm():
    return pl.BlockSpec(memory_space=pl.ANY)


def shape(dims, dtype):
    return jax.ShapeDtypeStruct(dims, dtype)


def attend_pair(bounds, q, k, v, kp, vp, o, lse):
    start, stop, pad_a, pad_b = bounds
    lane = lax.broadcasted_iota(jnp.int32, (1, 2 * HD), 1)
    row = lax.broadcasted_iota(jnp.int32, (BLK, 1), 0)
    col = lax.broadcasted_iota(jnp.int32, (1, BLK), 1)
    causal = col <= row
    pad_col = (col < pad_a) | (col >= pad_b)
    count = SLOT // BLK
    for i in range(count):
        n = (i + 1) * BLK
        qi = q(slice(i * BLK, n))
        edge = i in (0, count - 1)
        pos_q = row + i * BLK
        in_q = (pos_q >= start) & (pos_q < stop)
        masks = []
        for j in range(i + 1):
            pos_k = col + j * BLK
            mask = None
            if edge:
                in_k = (pos_k >= start) & (pos_k < stop)
                mask = (in_q & in_k) | (~in_q & ~in_k)
            elif j == 0:
                mask = jnp.broadcast_to(pos_k >= start, (BLK, BLK))
            if j == i:
                mask = causal if mask is None else mask & causal
            masks.append(mask)
        outs = []
        for h in range(2):
            qh = jnp.where(lane // HD == h, qi, jnp.zeros_like(qi))
            blocks = []
            for j in range(i + 1):
                s = nt(qh, k(slice(j * BLK, (j + 1) * BLK))) * SCALE
                if masks[j] is not None:
                    s = jnp.where(masks[j], s, NEG)
                blocks.append(s)
            if edge:
                s = nt(qh, kp(slice(None))) * SCALE
                blocks.append(jnp.where(~in_q & pad_col, s, NEG))
            top = functools.reduce(jnp.maximum, blocks)
            top = jnp.max(top, axis=1, keepdims=True)
            probs = [jnp.exp2(s - top) for s in blocks]
            total = jnp.sum(functools.reduce(jnp.add, probs), axis=1, keepdims=True)
            probs = [x.astype(BF16) for x in probs]
            mixed = nn(jnp.concatenate(probs[: i + 1], axis=1), v(slice(0, n)))
            if edge:
                mixed = mixed + nn(probs[-1], vp(slice(None)))
            outs.append(mixed * (1.0 / total))
            level = jnp.broadcast_to(top + jnp.log2(total), (BLK, 128))
            lse(h, slice(i * BLK, n), level.T[0:1, :])
        o(slice(i * BLK, n), jnp.where(lane < HD, outs[0], outs[1]).astype(BF16))


def split_heads(x):
    lane = lax.broadcasted_iota(jnp.int32, (1, 2 * HD), 1)
    zero = jnp.zeros_like(x)
    return [jnp.where(lane // HD == h, x, zero) for h in range(2)]


def back_block(i, q, o, lse, do):
    pick = (
        lax.broadcasted_iota(jnp.int32, (8, 2 * HD), 1) // HD
        == lax.broadcasted_iota(jnp.int32, (8, 2 * HD), 0)
    ).astype(F32)
    rows = slice(i * BLK, (i + 1) * BLK)
    do_i = do(rows)
    qs = jnp.concatenate(split_heads(q(rows)), axis=0)
    ds = jnp.concatenate(split_heads(do_i), axis=0)
    level = jnp.concatenate([lse(0, rows), lse(1, rows)], axis=1)
    inner = lax.dot_general(
        pick,
        do_i.astype(F32) * o(rows).astype(F32),
        (((1,), (1,)), ((), ())),
        precision=lax.Precision.HIGHEST,
        preferred_element_type=F32,
    )
    inner = jnp.concatenate([inner[0:1, :], inner[1:2, :]], axis=1)

    def block(kj, vj, mask):
        s = nt(kj, qs) * SCALE - level
        if mask is not None:
            s = jnp.where(mask, s, NEG)
        p = jnp.exp2(s)
        g = p * (nt(vj, ds) - inner)
        p, g = p.astype(BF16), g.astype(BF16)
        halves = split_heads(kj)
        part = tn(g[:, :BLK], halves[0]) + tn(g[:, BLK:], halves[1])
        return nn(g, qs), nn(p, ds), part

    pos_q = lax.broadcasted_iota(jnp.int32, (1, 2 * BLK), 1) % BLK + i * BLK
    return block, pos_q


def attend_back_pads(bounds, q, kp, vp, o, lse, do, dq_pad):
    start, stop, pad_a, pad_b = bounds
    row = lax.broadcasted_iota(jnp.int32, (BLK, 1), 0)
    pad_row = (row < pad_a) | (row >= pad_b)
    gk = gv = 0.0
    for n, i in enumerate((0, SLOT // BLK - 1)):
        block, pos_q = back_block(i, q, o, lse, do)
        one, two, part = block(kp, vp, ~((pos_q >= start) & (pos_q < stop)) & pad_row)
        gk, gv = gk + one, gv + two
        dq_pad(n, part)
    return gk, gv


def attend_back_pair(bounds, q, k, v, o, lse, do, dq_pad, dq, dk_sum, dv_sum):
    start, stop = bounds[:2]
    row = lax.broadcasted_iota(jnp.int32, (BLK, 1), 0)
    causal = row <= lax.broadcasted_iota(jnp.int32, (1, 2 * BLK), 1) % BLK
    dk_sum[...] = jnp.zeros_like(dk_sum)
    dv_sum[...] = jnp.zeros_like(dv_sum)
    count = SLOT // BLK
    for i in range(count):
        block, pos_q = back_block(i, q, o, lse, do)
        edge = i in (0, count - 1)
        in_q = (pos_q >= start) & (pos_q < stop)
        dq_sum = dq_pad(0 if i == 0 else 1) if edge else jnp.zeros((BLK, 2 * HD), F32)
        for j in range(i + 1):
            keys = slice(j * BLK, (j + 1) * BLK)
            pos_k = row + j * BLK
            mask = None
            if edge:
                in_k = (pos_k >= start) & (pos_k < stop)
                mask = (in_q & in_k) | (~in_q & ~in_k)
            elif j == 0:
                mask = jnp.broadcast_to(pos_k >= start, (BLK, 2 * BLK))
            if j == i:
                mask = causal if mask is None else mask & causal
            gk, gv, part = block(k(keys), v(keys), mask)
            dk_sum[keys, :] += gk
            dv_sum[keys, :] += gv
            dq_sum = dq_sum + part
        dq(slice(i * BLK, (i + 1) * BLK), (dq_sum * 0.125).astype(BF16))


def peer(axis, mask):
    return {axis: lax.axis_index(axis) ^ mask}


def greet(partners):
    barrier = pltpu.get_barrier_semaphore()
    for p in partners:
        pl.semaphore_signal(barrier, inc=1, device_id=p, device_id_type=pl.DeviceIdType.MESH)
    pl.semaphore_wait(barrier, len(partners))


def remote(src, dst, send, recv, to):
    return pltpu.make_async_remote_copy(
        src_ref=src, dst_ref=dst, send_sem=send, recv_sem=recv, device_id=to, device_id_type=pl.DeviceIdType.MESH
    )


def slot_bounds(caps, starts):
    s = lax.axis_index("seq")
    late = s >= 2
    start = jnp.where(late, starts[0, 1] - SLOT, starts[0, 0])
    stop = start + jnp.where(late, caps[0, 1], caps[0, 0]) + IMAGE
    pad_a = jnp.where(late, starts[0, 0], 0)
    pad_b = jnp.where(late, starts[0, 0] + caps[0, 0], BLK)
    return start, stop, pad_a, pad_b


def front_body(
    caps, starts, tokens, wqkv, wo, wu, wd, gains, biases,
    q_out, k_out, v_out, n_out, np_out, kp_out, vp_out, w_out, mix_out, own_out, lse_out, other, tok_out, pad_out, wo_all, wu_all, wd_all,
    mine, theirs, pads, made, w, normed, n_t, np_t, q, k, v, kp, vp, mixed, held_o, held_u, held_d, lse,
    tok_l, tok_s, tok_r, pad_s, pad_r, q_l, q_cs, q_cr, q_ys, q_yr, q_fs, q_fr,
    h_l, s_l, s_cs, s_cr, y_s, y_r, x_s, x_r, fy_s, fy_r, fx_s, fx_r, o_s, o_r, out_l,
    *, fsdp, dp
):
    f, x, s = lax.axis_index("fsdp"), lax.axis_index("dp"), lax.axis_index("seq")
    parity = s % 2
    local, d = tokens.shape
    half = d // 2
    ys = fsdp // 2
    bounds = slot_bounds(caps, starts)
    gain, bias = gains[0:1, :], biases[0:1, :]
    core, mate = peer("fsdp", 1), peer("seq", 1)
    greet(
        [core]
        + [peer("fsdp", 2 * r) for r in range(1, ys)]
        + [peer("dp", r) for r in range(1, dp)]
        + [mate, peer("seq", 3)]
    )

    cuts = ((0, BLK), (BLK, local - BLK))

    def token(i):
        at = pl.ds(*cuts[i])
        return remote(tokens.at[at], theirs.at[at], tok_s.at[i], tok_r.at[i], mate)

    load = pltpu.make_async_copy(tokens, mine, tok_l.at[0])
    load.start()
    token(0).start()
    token(1).start()

    rows = wqkv.shape[0]

    def band(r):
        return pl.ds(pl.multiple_of((f ^ r) * rows, 16), rows)

    def source(c):
        return wqkv.at[:, pl.ds(pl.multiple_of(c * d + parity * half, 128), half)]

    def cols(c):
        return pl.ds(c * half, half)

    def q_local(c):
        return pltpu.make_async_copy(source(c), w.at[band(0), cols(c)], q_l.at[c])

    def q_core(c):
        return remote(source(c), w.at[band(0), cols(c)], q_cs.at[c], q_cr.at[c], core)

    def q_y(c, r):
        at = (c, r - 1)
        return remote(source(c), w.at[band(0), cols(c)], q_ys.at[at], q_yr.at[at], peer("fsdp", 2 * r))

    def q_far(c, r):
        at = (c, r - 1)
        here = w.at[band(2 * r), cols(c)]
        return remote(here, here, q_fs.at[at], q_fr.at[at], core)

    for c in range(3):
        for r in range(1, ys):
            q_y(c, r).start()
        q_core(c).start()
        q_local(c).start()

    shards, wholes = (held_o, held_u, held_d), (wo_all, wu_all, wd_all)

    def hold(i):
        return pltpu.make_async_copy((wo, wu, wd)[i], shards[i], h_l.at[i])

    def whole_shard(i):
        n = shards[i].shape[0]
        return wholes[i].at[pl.ds(pl.multiple_of(f * n, 16), n)]

    def s_local(i):
        return pltpu.make_async_copy(shards[i], whole_shard(i), s_l.at[i])

    def s_core(i):
        return remote(shards[i], whole_shard(i), s_cs.at[i], s_cr.at[i], core)

    units = [(0, 0)] + [(1, j) for j in range(4)] + [(2, j) for j in range(4)]

    def piece(u, owner, part, shard=False):
        which, j = units[u]
        n = shards[which].shape[0]
        sub = n // dp
        base = part * sub if shard else owner * n + part * sub
        ref = shards[which] if shard else wholes[which]
        if which == 0:
            return ref.at[pl.ds(pl.multiple_of(base, 16), sub)]
        if which == 1:
            wide = ref.shape[1] // 4
            return ref.at[pl.ds(pl.multiple_of(base, 16), sub), pl.ds(j * wide, wide)]
        return ref.at[pl.ds(pl.multiple_of(base + j * (sub // 4), 16), sub // 4)]

    def w_y(u, r):
        at = (u, r - 1)
        return remote(piece(u, f, x, True), piece(u, f, x), y_s.at[at], y_r.at[at], peer("fsdp", 2 * r))

    def w_x(u, r, t):
        at = (u, r - 1, t - 1)
        here = piece(u, f ^ (2 * r), x)
        return remote(here, here, x_s.at[at], x_r.at[at], peer("dp", t))

    def w_fy(u, r):
        at = (u, r - 1)
        here = piece(u, f ^ (2 * r), x)
        return remote(here, here, fy_s.at[at], fy_r.at[at], core)

    def w_fx(u, r, t):
        at = (u, r - 1, t - 1)
        here = piece(u, f ^ (2 * r), x ^ t)
        return remote(here, here, fx_s.at[at], fx_r.at[at], core)

    def issue(u):
        if u < len(units):
            for r in range(1, ys):
                w_y(u, r).start()

    def came_y(u):
        for r in range(1, ys):
            w_y(u, r).wait_recv()
        issue(u + 3)
        for r in range(1, ys):
            for t in range(1, dp):
                w_x(u, r, t).start()
            w_fy(u, r).start()

    def came_x(u):
        for r in range(1, ys):
            for t in range(1, dp):
                w_x(u, r, t).wait_recv()
                w_fx(u, r, t).start()

    def normalise_rows(src, at, count):
        def body(i, carry):
            here = pl.ds(pl.multiple_of(i * 128, 128), 128)
            there = pl.ds(pl.multiple_of(at + i * 128, 128), 128)
            hat, _ = normalise(src[here, :].astype(F32))
            value = (hat * gain + bias).astype(BF16)
            normed[there, :] = value
            n_t[:, there] = value.T
            return carry

        lax.fori_loop(count[0], count[1], body, 0)

    def project(at, c):
        here = pl.ds(pl.multiple_of(at, 128), local)
        (q, k, v)[c][here, :] = nn(normed[here, :], w[:, c * half : (c + 1) * half]).astype(BF16)

    for i in range(3):
        hold(i).start()
    load.wait()
    normalise_rows(mine, parity * local, (0, local // 128))
    for c in range(3):
        q_local(c).wait()
        q_core(c).wait_recv()
        for r in range(1, ys):
            q_y(c, r).wait_recv()
            q_far(c, r).start()
        if c == 0:
            for i in range(3):
                hold(i).wait()
            issue(0)
            for i in range(3):
                s_local(i).start()
                s_core(i).start()
        elif c == 1:
            issue(1)
        else:
            issue(2)
        for r in range(1, ys):
            q_far(c, r).wait_recv()
        if c == 0:
            token(0).wait_recv()
            index = lax.broadcasted_iota(jnp.int32, (BLK, 1), 0)
            made[...] = jnp.where(
                index < starts[0, 0], theirs[0:BLK, :].astype(F32), mine[local - BLK : local, :].astype(F32)
            ).astype(BF16)

            @pl.when(s < 2)
            def _():
                pads[...] = made[...]

        project(parity * local, c)
        if c == 0:

            @pl.when(s == 1)
            def _():
                remote(made, pads, pad_s.at[0], pad_r.at[0], peer("seq", 3)).start()

    w_store = pltpu.make_async_copy(w, w_out, out_l.at[0])
    w_store.start()
    forward_pads = remote(pads, pads, pad_s.at[1], pad_r.at[1], mate)

    @pl.when(s == 2)
    def _():
        remote(made, pads, pad_s.at[0], pad_r.at[0], peer("seq", 3)).wait_recv()
        forward_pads.start()

    away = (1 - parity) * local
    normalise_rows(theirs, away, (0, BLK // 128))
    came_y(0)
    token(1).wait_recv()
    normalise_rows(theirs, away, (BLK // 128, local // 128))
    for c in range(3):
        project(away, c)
    stores = [
        pltpu.make_async_copy(a, b, out_l.at[1 + i])
        for i, (a, b) in enumerate(((q, q_out), (k, k_out), (v, v_out), (n_t, n_out), (theirs, tok_out)))
    ]
    for copy in stores:
        copy.start()
    came_y(1)
    came_x(0)

    @pl.when(s == 3)
    def _():
        forward_pads.wait_recv()

    hat, _ = normalise(pads[...].astype(F32))
    value = (hat * gain + bias).astype(BF16)
    np_t[...] = value.T
    kp[...] = nn(value, w[:, half : 2 * half]).astype(BF16)
    vp[...] = nn(value, w[:, 2 * half :]).astype(BF16)
    late = [
        pltpu.make_async_copy(a, b, out_l.at[6 + i])
        for i, (a, b) in enumerate(((np_t, np_out), (kp, kp_out), (vp, vp_out), (pads, pad_out)))
    ]
    for copy in late:
        copy.start()
    came_y(2)
    came_x(1)

    def give(i):
        lanes = pl.ds(pl.multiple_of(i * 2 * HD, 128), 2 * HD)
        return remote(
            mixed.at[pl.ds(pl.multiple_of(away, 16), local), lanes], other.at[:, lanes], o_s.at[i], o_r.at[i], mate
        )

    pairs = half // (2 * HD)
    done_y, done_x = 3, 2
    for i in range(pairs):
        lanes = slice(i * 2 * HD, (i + 1) * 2 * HD)

        def put(at, value):
            mixed[at, lanes] = value

        def put_lse(h, at, value):
            lse[i, h : h + 1, at] = value

        attend_pair(
            bounds,
            lambda at: q[at, lanes],
            lambda at: k[at, lanes],
            lambda at: v[at, lanes],
            lambda at: kp[at, lanes],
            lambda at: vp[at, lanes],
            put,
            put_lse,
        )
        give(i).start()
        came_y(done_y)
        came_x(done_x)
        done_y, done_x = done_y + 1, done_x + 1
    last = [
        pltpu.make_async_copy(mixed, mix_out, out_l.at[10]),
        pltpu.make_async_copy(lse, lse_out, out_l.at[11]),
        pltpu.make_async_copy(
            mixed.at[pl.ds(pl.multiple_of(parity * local, 16), local)], own_out, out_l.at[12]
        ),
    ]
    for copy in last:
        copy.start()
    for u in range(done_y, len(units)):
        came_y(u)
        came_x(u - 1)
    came_x(len(units) - 1)

    for i in range(pairs):
        give(i).wait()
    for i in range(3):
        s_local(i).wait()
        s_core(i).wait()
    for u in range(len(units)):
        for r in range(1, ys):
            w_y(u, r).wait_send()
            w_fy(u, r).wait()
            for t in range(1, dp):
                w_x(u, r, t).wait_send()
                w_fx(u, r, t).wait()
    for c in range(3):
        q_core(c).wait_send()
        for r in range(1, ys):
            q_y(c, r).wait_send()
            q_far(c, r).wait_send()
    token(0).wait_send()
    token(1).wait_send()

    @pl.when(s == 1)
    def _():
        remote(made, pads, pad_s.at[0], pad_r.at[0], peer("seq", 3)).wait_send()

    @pl.when(s == 2)
    def _():
        forward_pads.wait_send()

    for copy in [w_store] + stores + late + last:
        copy.wait()


def front(caps, starts, tokens, wqkv, wo, wu, wd, gain, bias, fsdp, dp):
    local, d = tokens.shape
    half, ff = d // 2, wu.shape[1]
    pairs = half // (2 * HD)
    y, px, n = max(fsdp // 2 - 1, 1), max(dp - 1, 1), 9
    dma = pltpu.SemaphoreType.DMA
    outs = [((2 * local, half), BF16)] * 3 + [
        ((d, 2 * local), BF16),
        ((d, BLK), BF16),
        ((BLK, half), BF16),
        ((BLK, half), BF16),
        ((d, 3 * half), BF16),
        ((2 * local, half), BF16),
        ((local, half), BF16),
        ((pairs, 2, 2 * local), F32),
        ((local, half), BF16),
        ((local, d), BF16),
        ((BLK, d), BF16),
        ((d, d), BF16),
        ((d, ff), BF16),
        ((ff, d), BF16),
    ]
    buffers = [
        (local, d), (local, d), (BLK, d), (BLK, d), (d, 3 * half), (2 * local, d), (d, 2 * local), (d, BLK),
        (2 * local, half), (2 * local, half), (2 * local, half), (BLK, half), (BLK, half), (2 * local, half),
        wo.shape, wu.shape, wd.shape,
    ]
    sems = [(1,), (2,), (2,), (2,), (2,), (3,), (3,), (3,), (3, y), (3, y), (3, y), (3, y)]
    sems += [(3,)] * 4 + [(n, y)] * 2 + [(n, y, px)] * 2 + [(n, y)] * 2 + [(n, y, px)] * 2 + [(pairs,)] * 2 + [(13,)]
    return pl.pallas_call(
        functools.partial(front_body, fsdp=fsdp, dp=dp),
        in_specs=[pl.BlockSpec(memory_space=pltpu.SMEM)] * 2 + [hbm()] * 5 + [pl.BlockSpec(memory_space=pltpu.VMEM)] * 2,
        out_specs=[hbm()] * len(outs),
        out_shape=[shape(*o) for o in outs],
        scratch_shapes=[pltpu.VMEM(b, BF16) for b in buffers]
        + [pltpu.VMEM((pairs, 2, 2 * local), F32)]
        + [dma(s) for s in sems],
        compiler_params=pltpu.CompilerParams(vmem_limit_bytes=VMEM_LIMIT, collective_id=1, has_side_effects=True),
        cost_estimate=pl.CostEstimate(flops=10**10, bytes_accessed=10**8, transcendentals=0),
    )(caps, starts, tokens, wqkv, wo, wu, wd, gain, bias)


def forward_body(
    own, other, x, up, gains, biases, wo, wu, wd, out, g_feed, act_t, slope, n_t, branch, middle, edges, normed, feed
):
    parity = lax.axis_index("seq") % 2
    step, last = pl.program_id(0), pl.num_programs(0) - 1
    half = own.shape[1]
    blocks = x.shape[0] // 128

    @pl.when(step == 0)
    def _():
        w_own = wo[pl.ds(pl.multiple_of(parity * half, 128), half), :]
        w_other = wo[pl.ds(pl.multiple_of((1 - parity) * half, 128), half), :]
        branch[...] = nn(own[...], w_own) + nn(other[...], w_other)

        def rows(i, carry):
            at = pl.ds(pl.multiple_of(i * 128, 128), 128)
            hat, _ = normalise(branch[at, :])
            mid = x[at, :].astype(F32) + hat * gains[1:2, :] + biases[1:2, :]
            middle[at, :] = mid
            hat, _ = normalise(mid)
            two = (hat * gains[2:3, :] + biases[2:3, :]).astype(BF16)
            normed[at, :] = two
            n_t[:, at] = two.T
            return carry

        lax.fori_loop(0, blocks, rows, 0)
        feed[...] = jnp.zeros_like(feed)

    u = nn(normed[...], wu[...])
    th = jnp.tanh(0.7978845608 * (u + 0.044715 * (u * u * u)))
    act = (0.5 * u * (1.0 + th)).astype(BF16)
    slope[...] = (
        0.5 * (1.0 + th) + 0.5 * u * (1.0 - th * th) * (0.7978845608 + (3 * 0.044715 * 0.7978845608) * (u * u))
    ).astype(BF16)
    act_t[...] = act.T
    feed[...] += nn(act, wd[...])

    @pl.when(step == last)
    def _():
        def rows(i, carry):
            at = pl.ds(pl.multiple_of(i * 128, 128), 128)
            g = up[at, :].astype(F32)
            hat, rstd = normalise(feed[at, :])
            gain = gains[3:4, :]
            out[at, :] = (middle[at, :] + hat * gain + biases[3:4, :]).astype(BF16)
            g_feed[at, :] = norm_back(g, hat, rstd, gain).astype(BF16)
            return (
                carry[0] + jnp.sum(g * hat, axis=0, keepdims=True),
                carry[1] + jnp.sum(g, axis=0, keepdims=True),
            )

        zero = jnp.zeros((1, x.shape[1]), F32)
        a, b = lax.fori_loop(0, blocks, rows, (zero, zero))
        edges[0:1, :] = a
        edges[1:2, :] = b


def forward(mixed, other, x, up, gains, biases, wo, wu, wd):
    local, d = x.shape
    half, ff = mixed.shape[1], wu.shape[1]
    tile = 512
    once = lambda s: pl.BlockSpec(s, lambda *_: (0,) * len(s), pipeline_mode=pl.Buffered(1))
    return call(
        forward_body,
        (ff // tile,),
        0,
        [
            once(mixed.shape),
            once(other.shape),
            once(x.shape),
            once(up.shape),
            once(gains.shape),
            once(biases.shape),
            once(wo.shape),
            pl.BlockSpec((d, tile), lambda i: (0, i)),
            pl.BlockSpec((tile, d), lambda i: (i, 0)),
        ],
        [
            full((local, d)),
            full((local, d)),
            pl.BlockSpec((tile, local), lambda i: (i, 0)),
            pl.BlockSpec((local, tile), lambda i: (0, i)),
            full((d, local)),
            full((local, d)),
            full((local, d)),
            full((2, d)),
        ],
        [
            shape((local, d), BF16),
            shape((local, d), BF16),
            shape((ff, local), BF16),
            shape((local, ff), BF16),
            shape((d, local), BF16),
            shape((local, d), F32),
            shape((local, d), F32),
            shape((2, d), F32),
        ],
        [pltpu.VMEM((local, d), BF16), pltpu.VMEM((local, d), F32)],
        flops=2 * local * d * (d + 2 * ff),
        moved=40e6,
    )(mixed, other, x, up, gains, biases, wo, wu, wd)


class Lane:
    @staticmethod
    def scratch(count, rows, cols, fsdp, dp, masks):
        y, x, z = max(fsdp // 2 - 1, 1), max(dp - 1, 1), len(masks)
        dma = pltpu.SemaphoreType.DMA
        sems = [(count,)] * 2 + [(count, y)] * 2 + [(count, x)] * 2 + [(count, z)] * 4 + [(count, x)] * 2 + [(count,)] * 3
        return (
            [
                pltpu.VMEM((count, fsdp // 2, rows, cols), BF16),
                pltpu.VMEM((count, y, rows, cols), BF16),
                pltpu.VMEM((count, x, rows // dp, cols), BF16),
            ]
            + [pltpu.VMEM((count, rows // dp, cols >> (i + 1)), BF16) for i in range(z)]
            + [dma(s) for s in sems]
        )

    @staticmethod
    def size(masks):
        return 3 + len(masks) + 15

    def __init__(self, refs, final, fsdp, dp, masks, both=None):
        z = len(masks)
        self.acc, self.y_in, self.x_in = refs[:3]
        self.z_in = refs[3 : 3 + z]
        names = ("core_s", "core_r", "y_s", "y_r", "x_s", "x_r", "z_s", "z_r", "zz_s", "zz_r", "xx_s", "xx_r", "own")
        names += ("pair_s", "pair_r")
        self.both = both
        self.sems = dict(zip(names, refs[3 + z :]))
        self.final = final
        self.ys, self.dp, self.masks = fsdp // 2, dp, masks
        self.count, _, self.rows, self.cols = self.acc.shape
        self.x = lax.axis_index("dp")
        s = lax.axis_index("seq")
        self.bits = [s // m % 2 for m in masks]
        self.stages = [self.from_y, self.from_x]
        self.stages += [functools.partial(self.from_z, i) for i in range(z)]
        self.stages += [functools.partial(self.back_from_z, i) for i in reversed(range(z))]
        self.stages += [self.from_pair] if both is not None else []
        self.stages += [self.back_from_x]

    def place(self, level, away=False):
        at = 0
        for i in range(level):
            bit = self.bits[i]
            if away and i == level - 1:
                bit = 1 - bit
            at = at + bit * (self.cols >> (i + 1))
        if level == 0:
            return pl.ds(0, self.cols)
        return pl.ds(pl.multiple_of(at, 128), self.cols >> level)

    def band(self, mask=0):
        n = self.rows // self.dp
        return pl.ds(pl.multiple_of((self.x ^ mask) * n, 16), n)

    def core(self, u, src):
        return remote(src, self.acc.at[u], self.sems["core_s"].at[u], self.sems["core_r"].at[u], peer("fsdp", 1))

    def over_y(self, u, ry):
        s = self.sems
        return remote(
            self.acc.at[u, ry], self.y_in.at[u, ry - 1], s["y_s"].at[u, ry - 1], s["y_r"].at[u, ry - 1], peer("fsdp", 2 * ry)
        )

    def over_x(self, u, rx):
        s = self.sems
        return remote(
            self.acc.at[u, 0, self.band(rx)],
            self.x_in.at[u, rx - 1],
            s["x_s"].at[u, rx - 1],
            s["x_r"].at[u, rx - 1],
            peer("dp", rx),
        )

    def over_z(self, u, i):
        s = self.sems
        return remote(
            self.acc.at[u, 0, self.band(), self.place(i + 1, True)],
            self.z_in[i].at[u],
            s["z_s"].at[u, i],
            s["z_r"].at[u, i],
            peer("seq", self.masks[i]),
        )

    def back_z(self, u, i):
        s = self.sems
        at = self.final.at[u, self.band(), self.place(i + 1)]
        last = i == len(self.masks) - 1
        src = self.acc.at[u, 0, self.band(), self.place(i + 1)] if last else at
        return remote(src, at, s["zz_s"].at[u, i], s["zz_r"].at[u, i], peer("seq", self.masks[i]))

    def back_x(self, u, rx):
        s = self.sems
        at = self.final.at[u, self.band()] if self.both is None else self.both.at[:, u, self.band()]
        return remote(at, at, s["xx_s"].at[u, rx - 1], s["xx_r"].at[u, rx - 1], peer("dp", rx))

    def keep(self, u):
        at = self.place(len(self.masks))
        return pltpu.make_async_copy(
            self.acc.at[u, 0, self.band(), at], self.final.at[u, self.band(), at], self.sems["own"].at[u]
        )

    def add(self, target, sources):
        rows = target.shape[0]
        step = 64 if rows % 64 == 0 else 16

        def body(i, carry):
            at = pl.ds(pl.multiple_of(i * step, 16), step)
            total = target[at, :].astype(F32)
            for src in sources:
                total = total + src[at, :].astype(F32)
            target[at, :] = total.astype(BF16)
            return carry

        lax.fori_loop(0, rows // step, body, 0)

    def start_y(self, u):
        for ry in range(1, self.ys):
            self.over_y(u, ry).start()

    def from_y(self, u):
        for ry in range(1, self.ys):
            self.over_y(u, ry).wait_recv()
        self.add(self.acc.at[u, 0], [self.y_in.at[u, ry - 1] for ry in range(1, self.ys)])
        for rx in range(1, self.dp):
            self.over_x(u, rx).start()

    def from_x(self, u):
        for rx in range(1, self.dp):
            self.over_x(u, rx).wait_recv()
        self.add(self.acc.at[u, 0, self.band()], [self.x_in.at[u, rx - 1] for rx in range(1, self.dp)])
        self.over_z(u, 0).start()

    def from_z(self, i, u):
        self.over_z(u, i).wait_recv()
        self.add(self.acc.at[u, 0, self.band(), self.place(i + 1)], [self.z_in[i].at[u]])
        if i + 1 < len(self.masks):
            self.over_z(u, i + 1).start()
        else:
            self.keep(u).start()
            self.back_z(u, i).start()

    def back_from_z(self, i, u):
        if i == len(self.masks) - 1:
            self.keep(u).wait()
        self.back_z(u, i).wait_recv()
        if i:
            self.back_z(u, i - 1).start()
        elif self.both is not None:
            self.pair(u).start()
        else:
            for rx in range(1, self.dp):
                self.back_x(u, rx).start()

    def pair(self, u):
        at = self.final.at[u, self.band()]
        return remote(at, at, self.sems["pair_s"].at[u], self.sems["pair_r"].at[u], peer("seq", 1))

    def from_pair(self, u):
        self.pair(u).wait_recv()
        for rx in range(1, self.dp):
            self.back_x(u, rx).start()

    def back_from_x(self, u):
        for rx in range(1, self.dp):
            self.back_x(u, rx).wait_recv()

    def drain(self, u):
        for ry in range(1, self.ys):
            self.over_y(u, ry).wait_send()
        for rx in range(1, self.dp):
            self.over_x(u, rx).wait_send()
            self.back_x(u, rx).wait_send()
        for i in range(len(self.masks)):
            self.over_z(u, i).wait_send()
            self.back_z(u, i).wait_send()
        if self.both is not None:
            self.pair(u).wait_send()


def partners(fsdp, dp):
    return (
        [peer("fsdp", 1)]
        + [peer("fsdp", 2 * ry) for ry in range(1, fsdp // 2)]
        + [peer("dp", rx) for rx in range(1, dp)]
        + [peer("seq", m) for m in (1, 2, 3)]
    )


def doublings(fsdp, dp, seq):
    steps = []
    for axis, size in (("fsdp", fsdp), ("dp", dp), ("seq", seq)):
        m = 1
        while m < size:
            steps.append((axis, m))
            m *= 2
    return steps


def rear_body(
    caps, starts, act_t, g_feed, two_t, slope, wd, wu, wo, middle, branch, upstream, mixed_own, other,
    q, k, v, mixed, kp, vp, lse, w, n_t, np_t, tokens, theirs, padx, gains, edges3,
    final_a, final_b, grad_in, sums, g_mid,
    *rest, fsdp, dp, seq
):
    size_a, size_b = Lane.size((1, 2)), Lane.size((2,))
    a = Lane(rest[:size_a], final_a, fsdp, dp, (1, 2))
    rest = rest[size_a:]
    parity = lax.axis_index("seq") % 2
    b = Lane(rest[:size_b], final_b.at[parity], fsdp, dp, (2,), final_b)
    (
        ring, ring_b, do, dq, dk, dv, dkp, dvp, dk_sum, dv_sum, edges0,
        g_out, g_in, gp_out, gp_in, run, got, d_send, edges12,
        load, tiles_l, blocks_l, mid_s, d_s, d_r, gs_s, gs_r, gp_s, gp_r, e_s, e_r,
    ) = rest[size_b:]
    f, s = lax.axis_index("fsdp"), lax.axis_index("seq")
    local, d = tokens.shape
    half = d // 2
    ys = fsdp // 2
    rows = a.rows
    mate = peer("seq", 1)
    bounds = slot_bounds(caps, starts)
    greet(partners(fsdp, dp))

    my_rows = pl.ds(pl.multiple_of(parity * local, 128), local)
    give = remote(d_send, do.at[my_rows], d_s.at[0], d_r.at[0], mate)

    def shard(r):
        return r ^ f

    def band(r):
        return pl.ds(pl.multiple_of(shard(r) * rows, 16), rows)

    def give_and_take(c, first, make):
        @pl.when(c < PIECES)
        def _():
            u = first + c
            slot = ring.at[u % 4]
            if first:
                a.core(u - 4, slot).wait_send()
            for ry in range(ys):
                slot[ry] = make(c, 2 * ry + 1).astype(BF16)
            a.core(u, slot).start()

        @pl.when(c >= 1)
        def _():
            u = first + c - 1
            a.core(u, ring.at[u % 4]).wait_recv()
            for ry in range(ys):
                a.acc[u, ry] = (make(c - 1, 2 * ry) + a.acc[u, ry].astype(F32)).astype(BF16)

    def feed_phase(g_v, two_v, hid_v, gbr_v):
        common = [
            pltpu.make_async_copy(g_feed, g_v, load.at[0]),
            pltpu.make_async_copy(two_t, two_v, load.at[1]),
        ]

        def down_phase(act_v):
            def fetch(c):
                return pltpu.make_async_copy(act_t.at[:, c], act_v.at[c], load.at[2 + c])

            for copy in (common[0], fetch(0), fetch(1), common[1], fetch(2), fetch(3)):
                copy.start()
            common[0].wait()

            def step(c, carry):
                @pl.when(c < PIECES)
                def _():
                    fetch(c).wait()

                give_and_take(c, 0, lambda c, r: nn(act_v[c, shard(r)], g_v[...]))

                @pl.when((c >= 1) & (c <= 2))
                def _():
                    a.start_y(c - 1)

                return carry

            lax.fori_loop(0, PIECES + 1, step, 0)
            common[1].wait()

        def back_phase(g_two):
            count = 2 * fsdp
            wide = wd.shape[0] // count
            piece = wide // 2

            def tile_phase(wd_v, wu_v, slope_v):
                def fetch(j, slot):
                    at = pl.ds(pl.multiple_of(j * wide, 128), wide)
                    return [
                        pltpu.make_async_copy(wd.at[at], wd_v.at[slot], tiles_l.at[0, slot]),
                        pltpu.make_async_copy(slope.at[:, at], slope_v.at[slot], tiles_l.at[1, slot]),
                        pltpu.make_async_copy(wu.at[:, at], wu_v.at[slot], tiles_l.at[2, slot]),
                    ]

                for copy in fetch(0, 0):
                    copy.start()

                def step(j, carry):
                    slot = j % 2

                    @pl.when(j + 1 < count)
                    def _():
                        for copy in fetch(j + 1, 1 - slot):
                            copy.start()

                    for copy in fetch(j, slot):
                        copy.wait()
                    h = (nt(g_v[...], wd_v[slot]) * slope_v[slot].astype(F32)).astype(BF16)
                    at = pl.ds(pl.multiple_of(j // 2 * piece, 128), piece)
                    for i in range(2):
                        hid_v[j % 2 * 2 + i, :, at] = h[:, i * piece : (i + 1) * piece]
                    part = nt(h, wu_v[slot])

                    @pl.when(j == 0)
                    def _():
                        g_two[...] = part

                    @pl.when(j != 0)
                    def _():
                        g_two[...] += part

                    @pl.when(j == count // 2)
                    def _():
                        tick(0)

                    return carry

                lax.fori_loop(0, count, step, 0)

            pl.run_scoped(tile_phase, dt((2, wide, d)), dt((2, d, wide)), dt((2, local, wide)))

            def middle_phase(mid_v, br_v, up_v, gm_v, wo_v):
                load_wo = pltpu.make_async_copy(wo, wo_v, load.at[6])
                load_wo.start()

                def fetch(i, slot):
                    at = pl.ds(pl.multiple_of(i * 128, 128), 128)
                    return [
                        pltpu.make_async_copy(middle.at[at], mid_v.at[slot], blocks_l.at[0, slot]),
                        pltpu.make_async_copy(branch.at[at], br_v.at[slot], blocks_l.at[1, slot]),
                        pltpu.make_async_copy(upstream.at[at], up_v.at[slot], blocks_l.at[2, slot]),
                    ]

                def leave(i, slot):
                    at = pl.ds(pl.multiple_of(i * 128, 128), 128)
                    return pltpu.make_async_copy(gm_v.at[slot], g_mid.at[at], mid_s.at[slot])

                count = local // 128
                for copy in fetch(0, 0):
                    copy.start()
                edges12[...] = jnp.zeros_like(edges12)
                tick(1)

                def step(i, carry):
                    slot = i % 2

                    @pl.when(i + 1 < count)
                    def _():
                        for copy in fetch(i + 1, 1 - slot):
                            copy.start()

                    for copy in fetch(i, slot):
                        copy.wait()
                    at = pl.ds(pl.multiple_of(i * 128, 128), 128)
                    g = g_two[at, :]
                    hat, rstd = normalise(mid_v[slot])
                    edges12[2:3, :] += jnp.sum(g * hat, axis=0, keepdims=True)
                    edges12[3:4, :] += jnp.sum(g, axis=0, keepdims=True)
                    gm = up_v[slot].astype(F32) + norm_back(g, hat, rstd, gains[2:3, :])

                    @pl.when(i >= 2)
                    def _():
                        leave(i - 2, slot).wait()

                    gm_v[slot] = gm
                    leave(i, slot).start()
                    hat, rstd = normalise(br_v[slot])
                    edges12[0:1, :] += jnp.sum(gm * hat, axis=0, keepdims=True)
                    edges12[1:2, :] += jnp.sum(gm, axis=0, keepdims=True)
                    gbr_v[at, :] = norm_back(gm, hat, rstd, gains[1:2, :]).astype(BF16)
                    return carry

                lax.fori_loop(0, count, step, 0)
                load_wo.wait()
                grad = gbr_v[...]
                d_send[...] = nt(grad, wo_v[pl.ds(pl.multiple_of((1 - parity) * half, 128), half), :]).astype(BF16)
                give.start()
                do[my_rows, :] = nt(grad, wo_v[pl.ds(pl.multiple_of(parity * half, 128), half), :]).astype(BF16)
                for i in (count - 2, count - 1):
                    leave(i, i % 2).wait()

            pl.run_scoped(
                middle_phase,
                dt((2, 128, d), F32), dt((2, 128, d), F32), dt((2, 128, d)), dt((2, 128, d), F32), dt((d, d)),
            )

        def up_phase(att):
            attn = [
                pltpu.make_async_copy(
                    mixed_own, att.at[:, pl.ds(pl.multiple_of(parity * half, 128), half)], load.at[7]
                ),
                pltpu.make_async_copy(
                    other, att.at[:, pl.ds(pl.multiple_of((1 - parity) * half, 128), half)], load.at[8]
                ),
            ]
            for copy in attn:
                copy.start()

            def step(c, carry):
                give_and_take(c, PIECES, lambda c, r: nn(two_v[band(r), :], hid_v[c]))

                @pl.when(c == 1)
                def _():
                    tick(2)

                return carry

            lax.fori_loop(0, PIECES + 1, step, 0)
            u = 2 * PIECES
            slot = ring.at[u % 4]
            a.core(u - 4, slot).wait_send()
            for copy in attn:
                copy.wait()
            for ry in range(ys):
                slot[ry] = tn(att[:, band(2 * ry + 1)], gbr_v[...]).astype(BF16)
            a.core(u, slot).start()
            for ry in range(ys):
                held = tn(att[:, band(2 * ry)], gbr_v[...])
                if ry == 0:
                    a.core(u, slot).wait_recv()
                a.acc[u, ry] = (held + a.acc[u, ry].astype(F32)).astype(BF16)

        pl.run_scoped(down_phase, dt((PIECES, fsdp, rows, local)))
        pl.run_scoped(back_phase, dt((local, d), F32))
        pl.run_scoped(up_phase, dt((local, d)))

    def starts_of(lane, t):
        if lane is b:
            return (2,) if t == a.count - 1 else ()
        if t < 0 or t + 3 >= a.count:
            return ()
        return (t + 2,) if t < 3 else (t + 2, t + 3) if t == 3 else (t + 3,)

    def tick(t):
        for lane, first in ((a, 0), (b, a.count)):
            for k, stage in enumerate(lane.stages):
                u = t - k - first
                if isinstance(t, int):
                    if 0 <= u < lane.count:
                        stage(u)
                    if k == 0:
                        for other in starts_of(lane, t):
                            lane.start_y(other)
                elif lane is a:

                    @pl.when(u >= 0)
                    def _():
                        stage(u)

                    if k == 0:

                        @pl.when(u + 3 < lane.count)
                        def _():
                            lane.start_y(u + 3)

    first = remote(gp_out, gp_in, gp_s.at[0], gp_r.at[0], mate)
    second = remote(gp_out, gp_in, gp_s.at[0], gp_r.at[0], peer("seq", 3))
    third = remote(gp_in, gp_in, gp_s.at[0], gp_r.at[0], mate)

    def count_edges(g, x):
        hat, _ = normalise(x.astype(F32))
        return jnp.sum(g * hat, axis=0, keepdims=True), jnp.sum(g, axis=0, keepdims=True)

    def attention_phase(q_v, k_v, v_v, o_v, kp_v, vp_v, lse_v, wkv_v, px_v, dq_pad):
        pairs = ((q, q_v), (mixed, o_v), (kp, kp_v), (vp, vp_v), (lse, lse_v), (w.at[:, pl.ds(half, 2 * half)], wkv_v))
        pairs += ((padx, px_v), (k, k_v), (v, v_v))
        copies = [pltpu.make_async_copy(x, y, load.at[9 + i]) for i, (x, y) in enumerate(pairs)]
        for copy in copies:
            copy.start()
        tick(3)
        for copy in copies:
            copy.wait()
        give.wait_recv()

        def views(i):
            lanes = pl.ds(pl.multiple_of(i * 2 * HD, 128), 2 * HD)
            return (
                lanes,
                lambda at: q_v[at, lanes],
                lambda at: o_v[at, lanes],
                lambda h, at: lse_v[i, h : h + 1, at],
                lambda at: do[at, lanes],
            )

        def pad_step(i, carry):
            lanes, q_of, o_of, lse_of, do_of = views(i)

            def put_pad(n, value):
                dq_pad[n, :, lanes] = value

            gk, gv = attend_back_pads(bounds, q_of, kp_v[:, lanes], vp_v[:, lanes], o_of, lse_of, do_of, put_pad)
            dkp[:, lanes] = (gk * 0.125).astype(BF16)
            dvp[:, lanes] = gv.astype(BF16)
            return carry

        lax.fori_loop(0, half // (2 * HD), pad_step, 0)
        g = nt(dkp[...], wkv_v[:, 0:half]) + nt(dvp[...], wkv_v[:, half:])
        gp_out[...] = g.astype(BF16)

        @pl.when(s == 3)
        def _():
            first.start()

        one, two = count_edges(g, px_v[...])
        edges0[0:1, :] = one
        edges0[1:2, :] = two

        def step(i, carry):
            lanes, q_of, o_of, lse_of, do_of = views(i)

            def put(at, value):
                dq[at, lanes] = value

            attend_back_pair(
                bounds,
                q_of,
                lambda at: k_v[at, lanes],
                lambda at: v_v[at, lanes],
                o_of,
                lse_of,
                do_of,
                lambda n: dq_pad[n, :, lanes],
                put,
                dk_sum,
                dv_sum,
            )
            dk[:, lanes] = (dk_sum[...] * 0.125).astype(BF16)
            dv[:, lanes] = dv_sum[...].astype(BF16)
            tick(i + 4)

            @pl.when((s == 2) & (i == 1))
            def _():
                first.wait_recv()
                gp_out[...] = (gp_out[...].astype(F32) + gp_in[...].astype(F32)).astype(BF16)
                second.start()

            @pl.when((s == 1) & (i == 3))
            def _():
                second.wait_recv()
                third.start()

            return carry

        lax.fori_loop(0, half // (2 * HD), step, 0)

    steps = doublings(fsdp, dp, seq)

    def double(i):
        axis, m = steps[i]
        return remote(run.at[i], got.at[i], e_s.at[i], e_r.at[i], peer(axis, m))

    def double_start(i):
        double(i).start()

    def double_end(i):
        double(i).wait_recv()
        run[i + 1] = run[i] + got[i]

    def project_phase(w_v, nt_v, npt_v, x_v, y_v, mid_v, own, out_v):
        pairs = ((w, w_v), (theirs, y_v), (n_t, nt_v), (np_t, npt_v), (tokens, x_v), (g_mid, mid_v))
        copies = [pltpu.make_async_copy(x, y, load.at[18 + i]) for i, (x, y) in enumerate(pairs)]
        for copy in copies:
            copy.start()
        gain = gains[0:1, :]
        back_rows = (dq, dk, dv)
        back_pads = (None, dkp, dvp)

        def grad(c, r):
            total = nn(nt_v[band(r), :], back_rows[c][...])
            if c:
                total = total + nn(npt_v[band(r), :], back_pads[c][...])
            return total

        def weight(c):
            return w_v[:, c * half : (c + 1) * half]

        def through(first_row, source, store, edge):
            def body(i, carry):
                at = pl.ds(pl.multiple_of(first_row + i * 128, 128), 128)
                here = pl.ds(pl.multiple_of(i * 128, 128), 128)
                g = nt(dq[at, :], weight(0)) + nt(dk[at, :], weight(1)) + nt(dv[at, :], weight(2))
                store(i, here, g)
                one, two = count_edges(g, source[here, :])
                return carry[0] + one, carry[1] + two

            return lax.fori_loop(0, local // 128, body, edge)

        def pass_rows(i):
            at = pl.ds(pl.multiple_of(i * 128, 128), 128)
            return remote(g_out.at[at], g_in.at[at], gs_s.at[i], gs_r.at[i], mate)

        def store_out(i, at, value):
            g_out[at, :] = value.astype(BF16)
            pass_rows(i).start()

        def store_own(i, at, value):
            own[at, :] = value

        for copy in copies[:2]:
            copy.wait()
        edge = through((1 - parity) * local, y_v, store_out, (edges0[0:1, :], edges0[1:2, :]))
        for copy in copies[2:]:
            copy.wait()
        for c in range(3):
            for ry in range(ys):
                ring_b[c, ry] = grad(c, 2 * ry + 1).astype(BF16)
            b.core(c, ring_b.at[c]).start()
        for c in range(3):
            for ry in range(ys):
                held = grad(c, 2 * ry)
                if ry == 0:
                    b.core(c, ring_b.at[c]).wait_recv()
                b.acc[c, ry] = (held + b.acc[c, ry].astype(F32)).astype(BF16)
        b.start_y(0)
        b.start_y(1)
        tick(8)
        edge = through(parity * local, x_v, store_own, edge)
        order = (edge[0], edges12[0:1, :], edges12[2:3, :], edges3[0:1, :])
        order += (edge[1], edges12[1:2, :], edges12[3:4, :], edges3[1:2, :])
        for i, value in enumerate(order):
            run[0, i : i + 1, :] = value
        leave = pltpu.make_async_copy(out_v, grad_in, load.at[25])

        def finish_rows():
            for i in range(local // 128):
                pass_rows(i).wait_recv()

            @pl.when(s == 1)
            def _():
                third.wait_send()

            @pl.when(s == 0)
            def _():
                third.wait_recv()

            @pl.when(s == 2)
            def _():
                second.wait_send()

            @pl.when(s == 3)
            def _():
                first.wait_send()

            @pl.when(s < 2)
            def _():
                row = lax.broadcasted_iota(jnp.int32, (BLK, 1), 0)
                mine = ((s == 0) & (row < starts[0, 0])) | ((s == 1) & (row >= starts[0, 0] + caps[0, 0]))
                extra = jnp.where(mine, gp_in[...].astype(F32), 0.0)
                at = pl.ds(pl.multiple_of(jnp.where(s == 0, 0, local - BLK), 128), BLK)
                own[at, :] += extra

            def finish(i, carry):
                at = pl.ds(pl.multiple_of(i * 128, 128), 128)
                hat, rstd = normalise(x_v[at, :].astype(F32))
                g = own[at, :] + g_in[at, :].astype(F32)
                out_v[at, :] = (mid_v[at, :] + norm_back(g, hat, rstd, gain)).astype(BF16)
                return carry

            lax.fori_loop(0, local // 128, finish, 0)
            leave.start()

        double_start(0)
        end = max(a.count + len(a.stages), a.count + b.count + len(b.stages))
        pending = 0
        for t in range(9, end):
            tick(t)
            if pending < len(steps):
                double_end(pending)
                pending += 1
                if pending < len(steps):
                    double_start(pending)
            if t == 13:
                finish_rows()
        for i in range(pending, len(steps)):
            double_end(i)
            if i + 1 < len(steps):
                double_start(i + 1)
        last = pltpu.make_async_copy(run.at[len(steps)], sums, load.at[24])
        last.start()

        for i in range(local // 128):
            pass_rows(i).wait_send()
        last.wait()
        leave.wait()

    dt = lambda s, t=BF16: pltpu.VMEM(s, t)
    pl.run_scoped(
        feed_phase,
        dt((local, d)),
        dt((d, local)),
        dt((PIECES, local, d)),
        dt((local, d)),
    )
    pl.run_scoped(
        attention_phase,
        dt(q.shape), dt(k.shape), dt(v.shape), dt(mixed.shape), dt(kp.shape), dt(vp.shape), dt(lse.shape, F32),
        dt((d, 2 * half)), dt(padx.shape), dt((2, BLK, half), F32),
    )
    pl.run_scoped(
        project_phase,
        dt(w.shape), dt(n_t.shape), dt(np_t.shape), dt(tokens.shape), dt(theirs.shape),
        dt(g_mid.shape, F32), dt((local, d), F32), dt((local, d)),
    )
    give.wait_send()
    for u in range(2 * PIECES - 3, 2 * PIECES + 1):
        a.core(u, ring.at[u % 4]).wait_send()
    for u in range(b.count):
        b.core(u, ring_b.at[u]).wait_send()
    for lane in (a, b):
        for u in range(lane.count):
            lane.drain(u)
    for i in range(len(steps)):
        double(i).wait_send()


def rear(caps, starts, arrays, small, sizes):
    fsdp, dp, seq = sizes
    local, d = arrays[1].shape
    half = d // 2
    rows, y = d // fsdp, fsdp // 2
    n = 2 * PIECES + 1
    steps = len(doublings(fsdp, dp, seq))
    dma = pltpu.SemaphoreType.DMA
    vm = pltpu.VMEM
    return pl.pallas_call(
        functools.partial(rear_body, fsdp=fsdp, dp=dp, seq=seq),
        in_specs=[pl.BlockSpec(memory_space=pltpu.SMEM)] * 2
        + [hbm()] * len(arrays)
        + [pl.BlockSpec(memory_space=pltpu.VMEM)] * len(small),
        out_specs=[hbm()] * 5,
        out_shape=[
            shape((n, rows, d), BF16),
            shape((2, 3, rows, half), BF16),
            shape((local, d), BF16),
            shape((8, d), F32),
            shape((local, d), F32),
        ],
        scratch_shapes=Lane.scratch(n, rows, d, fsdp, dp, (1, 2))
        + Lane.scratch(3, rows, half, fsdp, dp, (2,))
        + [vm((4, y, rows, d), BF16), vm((3, y, rows, half), BF16)]
        + [vm((2 * local, half), BF16)] * 4
        + [vm((BLK, half), BF16)] * 2
        + [vm((2 * local, 2 * HD), F32)] * 2
        + [vm((2, d), F32)]
        + [vm((local, d), BF16)] * 2
        + [vm((BLK, d), BF16)] * 2
        + [vm((steps + 1, 8, d), F32), vm((steps, 8, d), F32), vm((local, half), BF16), vm((4, d), F32)]
        + [dma((26,)), dma((3, 2)), dma((3, 2)), dma((2,)), dma((1,)), dma((1,))]
        + [dma((local // 128,))] * 2
        + [dma((1,))] * 2
        + [dma((steps,)), dma((steps,))],
        compiler_params=pltpu.CompilerParams(vmem_limit_bytes=VMEM_LIMIT, collective_id=0, has_side_effects=True),
        cost_estimate=pl.CostEstimate(flops=10**10, bytes_accessed=10**8, transcendentals=0),
    )(caps, starts, *arrays, *small)


def deliver_body(done, done_q, grad_in, sums, qkv, proj, up, down, out, gain, bias, a, b, c_in, s_in, wide, q_wide, load, sem):
    rows, d = a.shape[1:]
    half = b.shape[3]
    loads = [pltpu.make_async_copy(done.at[i], a.at[i], load.at[i]) for i in range(a.shape[0])]
    loads += [
        pltpu.make_async_copy(done_q, b, load.at[9]),
        pltpu.make_async_copy(grad_in, c_in, load.at[10]),
        pltpu.make_async_copy(sums, s_in, load.at[11]),
    ]
    for copy in loads:
        copy.start()
    stores = []

    def store(src, dst):
        copy = pltpu.make_async_copy(src, dst, sem.at[len(stores)])
        copy.start()
        stores.append(copy)

    shards = d // rows
    for i in range(a.shape[0]):
        loads[i].wait()
        wide[i] = a[i].astype(F32)
        if i == 2 * PIECES:
            store(wide.at[i], proj)
        elif i < PIECES:
            store(wide.at[i], down.at[pl.ds(i * rows, rows)])
        else:
            for h in range(shards):
                at = (h * PIECES + i - PIECES) * rows
                store(wide.at[i, :, pl.ds(h * rows, rows)], up.at[:, pl.ds(at, rows)])
    for copy in loads[a.shape[0] :]:
        copy.wait()
    for h in range(2):
        for i in range(3):
            q_wide[h, i] = b[h, i].astype(F32)
            store(q_wide.at[h, i], qkv.at[:, pl.ds((2 * i + h) * half, half)])
    store(c_in, out)
    gain[...] = s_in[0:4, :]
    bias[...] = s_in[4:8, :]
    for copy in stores:
        copy.wait()


def deliver(done, done_q, grad_in, sums, ff):
    n, rows, d = done.shape
    half = done_q.shape[3]
    count = PIECES + PIECES * (d // rows) + 1 + 6 + 1
    vm, dma = pltpu.VMEM, pltpu.SemaphoreType.DMA
    small = pl.BlockSpec(memory_space=pltpu.VMEM)
    return pl.pallas_call(
        deliver_body,
        in_specs=[hbm()] * 4,
        out_specs=[hbm()] * 5 + [small, small],
        out_shape=[
            shape((rows, 6 * half), F32),
            shape((rows, d), F32),
            shape((rows, ff), F32),
            shape((PIECES * rows, d), F32),
            shape(grad_in.shape, BF16),
            shape((4, d), F32),
            shape((4, d), F32),
        ],
        scratch_shapes=[
            vm(done.shape, BF16),
            vm(done_q.shape, BF16),
            vm(grad_in.shape, BF16),
            vm(sums.shape, F32),
            vm(done.shape, F32),
            vm(done_q.shape, F32),
            dma((12,)),
            dma((count,)),
        ],
        compiler_params=pltpu.CompilerParams(vmem_limit_bytes=VMEM_LIMIT),
        cost_estimate=pl.CostEstimate(flops=10**7, bytes_accessed=2 * 10**7, transcendentals=0),
    )(done, done_q, grad_in, sums)


def local(
    tokens, qkv_weight, out_weight, up_weight, down_weight, norm_gain, norm_bias, caption_len, item_start, grad_out
):
    x_tok, up = tokens[0], grad_out[0]
    local_rows, d = x_tok.shape
    fsdp, dp, seq = (lax.axis_size(axis) for axis in ("fsdp", "dp", "seq"))
    ff = up_weight.shape[1]
    (q, k, v, n_t, np_t, kp, vp, w_qkv, mixed, mixed_own, lse, other, theirs, pads, wo, wu, wd) = front(
        caption_len, item_start, x_tok, qkv_weight, out_weight, up_weight, down_weight, norm_gain, norm_bias, fsdp, dp
    )
    (out, g_feed, act_t, slope, two_t, branch, middle, edges3) = forward(
        mixed_own, other, x_tok, up, norm_gain, norm_bias, wo, wu, wd
    )
    done, done_q, grad_in, sums, _ = rear(
        caption_len,
        item_start,
        (
            act_t.reshape(fsdp, PIECES, d // fsdp, local_rows), g_feed, two_t, slope, wd, wu, wo,
            middle, branch, up, mixed_own, other, q, k, v, mixed, kp, vp, lse, w_qkv, n_t, np_t, x_tok, theirs, pads,
        ),
        (norm_gain, edges3),
        (fsdp, dp, seq),
    )
    grad_qkv, grad_proj, grad_up, grad_down, grad_in, grad_gain, grad_bias = deliver(done, done_q, grad_in, sums, ff)
    return (out[None], grad_in[None], grad_qkv, grad_proj, grad_up, grad_down, grad_gain, grad_bias)


def solution(mesh):
    rows = P(("fsdp", "dp"), "seq", None)
    shard = P("fsdp", None)
    items = P(("fsdp", "dp"), None)
    return jax.shard_map(
        local,
        mesh=mesh,
        in_specs=(rows, shard, shard, shard, shard, P(), P(), items, items, rows),
        out_specs=(rows, rows, shard, shard, shard, shard, P(), P()),
        check_vma=False,
    )
```

```python
import functools

import jax
import jax.numpy as jnp
from jax import lax
from jax.experimental import pallas as pl
from jax.experimental.pallas import tpu as pltpu
from jax.sharding import PartitionSpec as P

HD = 64
IMAGE = 1024
SLOT = 1280
BLK = 256
LOG2E = 1.4426950408889634
SCALE = LOG2E / 8.0
NEG = -1e30
F32 = jnp.float32
BF16 = jnp.bfloat16
VMEM_LIMIT = 60 * 1024 * 1024
PIECES = 4


def nn(a, b):
    return lax.dot_general(a, b, (((1,), (0,)), ((), ())), preferred_element_type=F32)


def nt(a, b):
    return lax.dot_general(a, b, (((1,), (1,)), ((), ())), preferred_element_type=F32)


def tn(a, b):
    return lax.dot_general(a, b, (((0,), (0,)), ((), ())), preferred_element_type=F32)


def normalise(v):
    mean = jnp.mean(v, axis=-1, keepdims=True)
    centred = v - mean
    var = jnp.mean(centred * centred, axis=-1, keepdims=True)
    rstd = lax.rsqrt(var + 1e-05)
    return centred * rstd, rstd


def norm_back(g, hat, rstd, gain):
    gg = g * gain
    return rstd * (
        gg - jnp.mean(gg, axis=-1, keepdims=True) - hat * jnp.mean(gg * hat, axis=-1, keepdims=True)
    )


def call(body, grid, prefetch, in_specs, out_specs, out_shape, scratch=(), flops=0, moved=0):
    return pl.pallas_call(
        body,
        grid_spec=pltpu.PrefetchScalarGridSpec(
            num_scalar_prefetch=prefetch,
            grid=grid,
            in_specs=in_specs,
            out_specs=out_specs,
            scratch_shapes=list(scratch),
        ),
        out_shape=out_shape,
        compiler_params=pltpu.CompilerParams(vmem_limit_bytes=VMEM_LIMIT),
        cost_estimate=pl.CostEstimate(flops=int(flops), bytes_accessed=int(moved), transcendentals=0),
    )


def full(shape):
    zeros = (0,) * len(shape)
    return pl.BlockSpec(shape, lambda *_: zeros)


def hbm():
    return pl.BlockSpec(memory_space=pl.ANY)


def shape(dims, dtype):
    return jax.ShapeDtypeStruct(dims, dtype)


def attend_pair(bounds, q, k, v, kp, vp, o, lse):
    start, stop, pad_a, pad_b = bounds
    lane = lax.broadcasted_iota(jnp.int32, (1, 2 * HD), 1)
    row = lax.broadcasted_iota(jnp.int32, (BLK, 1), 0)
    col = lax.broadcasted_iota(jnp.int32, (1, BLK), 1)
    causal = col <= row
    pad_col = (col < pad_a) | (col >= pad_b)
    count = SLOT // BLK
    for i in range(count):
        n = (i + 1) * BLK
        qi = q(slice(i * BLK, n))
        edge = i in (0, count - 1)
        pos_q = row + i * BLK
        in_q = (pos_q >= start) & (pos_q < stop)
        masks = []
        for j in range(i + 1):
            pos_k = col + j * BLK
            mask = None
            if edge:
                in_k = (pos_k >= start) & (pos_k < stop)
                mask = (in_q & in_k) | (~in_q & ~in_k)
            elif j == 0:
                mask = jnp.broadcast_to(pos_k >= start, (BLK, BLK))
            if j == i:
                mask = causal if mask is None else mask & causal
            masks.append(mask)
        outs = []
        for h in range(2):
            qh = jnp.where(lane // HD == h, qi, jnp.zeros_like(qi))
            blocks = []
            for j in range(i + 1):
                s = nt(qh, k(slice(j * BLK, (j + 1) * BLK))) * SCALE
                if masks[j] is not None:
                    s = jnp.where(masks[j], s, NEG)
                blocks.append(s)
            if edge:
                s = nt(qh, kp(slice(None))) * SCALE
                blocks.append(jnp.where(~in_q & pad_col, s, NEG))
            top = functools.reduce(jnp.maximum, blocks)
            top = jnp.max(top, axis=1, keepdims=True)
            probs = [jnp.exp2(s - top) for s in blocks]
            total = jnp.sum(functools.reduce(jnp.add, probs), axis=1, keepdims=True)
            probs = [x.astype(BF16) for x in probs]
            mixed = nn(jnp.concatenate(probs[: i + 1], axis=1), v(slice(0, n)))
            if edge:
                mixed = mixed + nn(probs[-1], vp(slice(None)))
            outs.append(mixed * (1.0 / total))
            level = jnp.broadcast_to(top + jnp.log2(total), (BLK, 128))
            lse(h, slice(i * BLK, n), level.T[0:1, :])
        o(slice(i * BLK, n), jnp.where(lane < HD, outs[0], outs[1]).astype(BF16))


def split_heads(x):
    lane = lax.broadcasted_iota(jnp.int32, (1, 2 * HD), 1)
    zero = jnp.zeros_like(x)
    return [jnp.where(lane // HD == h, x, zero) for h in range(2)]


def back_block(i, q, o, lse, do):
    pick = (
        lax.broadcasted_iota(jnp.int32, (8, 2 * HD), 1) // HD
        == lax.broadcasted_iota(jnp.int32, (8, 2 * HD), 0)
    ).astype(F32)
    rows = slice(i * BLK, (i + 1) * BLK)
    do_i = do(rows)
    qs = jnp.concatenate(split_heads(q(rows)), axis=0)
    ds = jnp.concatenate(split_heads(do_i), axis=0)
    level = jnp.concatenate([lse(0, rows), lse(1, rows)], axis=1)
    inner = lax.dot_general(
        pick,
        do_i.astype(F32) * o(rows).astype(F32),
        (((1,), (1,)), ((), ())),
        precision=lax.Precision.HIGHEST,
        preferred_element_type=F32,
    )
    inner = jnp.concatenate([inner[0:1, :], inner[1:2, :]], axis=1)

    def block(kj, vj, mask):
        s = nt(kj, qs) * SCALE - level
        if mask is not None:
            s = jnp.where(mask, s, NEG)
        p = jnp.exp2(s)
        g = p * (nt(vj, ds) - inner)
        p, g = p.astype(BF16), g.astype(BF16)
        halves = split_heads(kj)
        part = tn(g[:, :BLK], halves[0]) + tn(g[:, BLK:], halves[1])
        return nn(g, qs), nn(p, ds), part

    pos_q = lax.broadcasted_iota(jnp.int32, (1, 2 * BLK), 1) % BLK + i * BLK
    return block, pos_q


def attend_back_pads(bounds, q, kp, vp, o, lse, do, dq_pad):
    start, stop, pad_a, pad_b = bounds
    row = lax.broadcasted_iota(jnp.int32, (BLK, 1), 0)
    pad_row = (row < pad_a) | (row >= pad_b)
    gk = gv = 0.0
    for n, i in enumerate((0, SLOT // BLK - 1)):
        block, pos_q = back_block(i, q, o, lse, do)
        one, two, part = block(kp, vp, ~((pos_q >= start) & (pos_q < stop)) & pad_row)
        gk, gv = gk + one, gv + two
        dq_pad(n, part)
    return gk, gv


def attend_back_pair(bounds, q, k, v, o, lse, do, dq_pad, dq, dk_sum, dv_sum):
    start, stop = bounds[:2]
    row = lax.broadcasted_iota(jnp.int32, (BLK, 1), 0)
    causal = row <= lax.broadcasted_iota(jnp.int32, (1, 2 * BLK), 1) % BLK
    dk_sum[...] = jnp.zeros_like(dk_sum)
    dv_sum[...] = jnp.zeros_like(dv_sum)
    count = SLOT // BLK
    for i in range(count):
        block, pos_q = back_block(i, q, o, lse, do)
        edge = i in (0, count - 1)
        in_q = (pos_q >= start) & (pos_q < stop)
        dq_sum = dq_pad(0 if i == 0 else 1) if edge else jnp.zeros((BLK, 2 * HD), F32)
        for j in range(i + 1):
            keys = slice(j * BLK, (j + 1) * BLK)
            pos_k = row + j * BLK
            mask = None
            if edge:
                in_k = (pos_k >= start) & (pos_k < stop)
                mask = (in_q & in_k) | (~in_q & ~in_k)
            elif j == 0:
                mask = jnp.broadcast_to(pos_k >= start, (BLK, 2 * BLK))
            if j == i:
                mask = causal if mask is None else mask & causal
            gk, gv, part = block(k(keys), v(keys), mask)
            dk_sum[keys, :] += gk
            dv_sum[keys, :] += gv
            dq_sum = dq_sum + part
        dq(slice(i * BLK, (i + 1) * BLK), (dq_sum * 0.125).astype(BF16))


def peer(axis, mask):
    return {axis: lax.axis_index(axis) ^ mask}


def greet(partners):
    barrier = pltpu.get_barrier_semaphore()
    for p in partners:
        pl.semaphore_signal(barrier, inc=1, device_id=p, device_id_type=pl.DeviceIdType.MESH)
    pl.semaphore_wait(barrier, len(partners))


def remote(src, dst, send, recv, to):
    return pltpu.make_async_remote_copy(
        src_ref=src, dst_ref=dst, send_sem=send, recv_sem=recv, device_id=to, device_id_type=pl.DeviceIdType.MESH
    )


def slot_bounds(caps, starts):
    s = lax.axis_index("seq")
    late = s >= 2
    start = jnp.where(late, starts[0, 1] - SLOT, starts[0, 0])
    stop = start + jnp.where(late, caps[0, 1], caps[0, 0]) + IMAGE
    pad_a = jnp.where(late, starts[0, 0], 0)
    pad_b = jnp.where(late, starts[0, 0] + caps[0, 0], BLK)
    return start, stop, pad_a, pad_b


def front_body(
    caps, starts, tokens, wqkv, wo, wu, wd, gains, biases,
    q_out, k_out, v_out, n_out, np_out, kp_out, vp_out, w_out, mix_out, own_out, lse_out, other, tok_out, pad_out, wo_all, wu_all, wd_all,
    mine, theirs, pads, made, w, normed, n_t, np_t, q, k, v, kp, vp, mixed, held_o, held_u, held_d, lse,
    tok_l, tok_s, tok_r, pad_s, pad_r, q_l, q_cs, q_cr, q_ys, q_yr, q_fs, q_fr,
    h_l, s_l, s_cs, s_cr, y_s, y_r, x_s, x_r, fy_s, fy_r, fx_s, fx_r, o_s, o_r, out_l,
    *, fsdp, dp
):
    f, x, s = lax.axis_index("fsdp"), lax.axis_index("dp"), lax.axis_index("seq")
    parity = s % 2
    local, d = tokens.shape
    half = d // 2
    ys = fsdp // 2
    bounds = slot_bounds(caps, starts)
    gain, bias = gains[0:1, :], biases[0:1, :]
    core, mate = peer("fsdp", 1), peer("seq", 1)
    greet(
        [core]
        + [peer("fsdp", 2 * r) for r in range(1, ys)]
        + [peer("dp", r) for r in range(1, dp)]
        + [mate, peer("seq", 3)]
    )

    cuts = ((0, BLK), (BLK, local - BLK))

    def token(i):
        at = pl.ds(*cuts[i])
        return remote(tokens.at[at], theirs.at[at], tok_s.at[i], tok_r.at[i], mate)

    load = pltpu.make_async_copy(tokens, mine, tok_l.at[0])
    load.start()
    token(0).start()
    token(1).start()

    rows = wqkv.shape[0]

    def band(r):
        return pl.ds(pl.multiple_of((f ^ r) * rows, 16), rows)

    def source(c):
        return wqkv.at[:, pl.ds(pl.multiple_of(c * d + parity * half, 128), half)]

    def cols(c):
        return pl.ds(c * half, half)

    def q_local(c):
        return pltpu.make_async_copy(source(c), w.at[band(0), cols(c)], q_l.at[c])

    def q_core(c):
        return remote(source(c), w.at[band(0), cols(c)], q_cs.at[c], q_cr.at[c], core)

    def q_y(c, r):
        at = (c, r - 1)
        return remote(source(c), w.at[band(0), cols(c)], q_ys.at[at], q_yr.at[at], peer("fsdp", 2 * r))

    def q_far(c, r):
        at = (c, r - 1)
        here = w.at[band(2 * r), cols(c)]
        return remote(here, here, q_fs.at[at], q_fr.at[at], core)

    for c in range(3):
        for r in range(1, ys):
            q_y(c, r).start()
        q_core(c).start()
        q_local(c).start()

    shards, wholes = (held_o, held_u, held_d), (wo_all, wu_all, wd_all)

    def hold(i):
        return pltpu.make_async_copy((wo, wu, wd)[i], shards[i], h_l.at[i])

    def whole_shard(i):
        n = shards[i].shape[0]
        return wholes[i].at[pl.ds(pl.multiple_of(f * n, 16), n)]

    def s_local(i):
        return pltpu.make_async_copy(shards[i], whole_shard(i), s_l.at[i])

    def s_core(i):
        return remote(shards[i], whole_shard(i), s_cs.at[i], s_cr.at[i], core)

    units = [(0, 0)] + [(1, j) for j in range(4)] + [(2, j) for j in range(4)]

    def piece(u, owner, part, shard=False):
        which, j = units[u]
        n = shards[which].shape[0]
        sub = n // dp
        base = part * sub if shard else owner * n + part * sub
        ref = shards[which] if shard else wholes[which]
        if which == 0:
            return ref.at[pl.ds(pl.multiple_of(base, 16), sub)]
        if which == 1:
            wide = ref.shape[1] // 4
            return ref.at[pl.ds(pl.multiple_of(base, 16), sub), pl.ds(j * wide, wide)]
        return ref.at[pl.ds(pl.multiple_of(base + j * (sub // 4), 16), sub // 4)]

    def w_y(u, r):
        at = (u, r - 1)
        return remote(piece(u, f, x, True), piece(u, f, x), y_s.at[at], y_r.at[at], peer("fsdp", 2 * r))

    def w_x(u, r, t):
        at = (u, r - 1, t - 1)
        here = piece(u, f ^ (2 * r), x)
        return remote(here, here, x_s.at[at], x_r.at[at], peer("dp", t))

    def w_fy(u, r):
        at = (u, r - 1)
        here = piece(u, f ^ (2 * r), x)
        return remote(here, here, fy_s.at[at], fy_r.at[at], core)

    def w_fx(u, r, t):
        at = (u, r - 1, t - 1)
        here = piece(u, f ^ (2 * r), x ^ t)
        return remote(here, here, fx_s.at[at], fx_r.at[at], core)

    def issue(u):
        if u < len(units):
            for r in range(1, ys):
                w_y(u, r).start()

    def came_y(u):
        for r in range(1, ys):
            w_y(u, r).wait_recv()
        issue(u + 3)
        for r in range(1, ys):
            for t in range(1, dp):
                w_x(u, r, t).start()
            w_fy(u, r).start()

    def came_x(u):
        for r in range(1, ys):
            for t in range(1, dp):
                w_x(u, r, t).wait_recv()
                w_fx(u, r, t).start()

    def normalise_rows(src, at, count):
        def body(i, carry):
            here = pl.ds(pl.multiple_of(i * 128, 128), 128)
            there = pl.ds(pl.multiple_of(at + i * 128, 128), 128)
            hat, _ = normalise(src[here, :].astype(F32))
            value = (hat * gain + bias).astype(BF16)
            normed[there, :] = value
            n_t[:, there] = value.T
            return carry

        lax.fori_loop(count[0], count[1], body, 0)

    def project(at, c):
        here = pl.ds(pl.multiple_of(at, 128), local)
        (q, k, v)[c][here, :] = nn(normed[here, :], w[:, c * half : (c + 1) * half]).astype(BF16)

    for i in range(3):
        hold(i).start()
    load.wait()
    normalise_rows(mine, parity * local, (0, local // 128))
    for c in range(3):
        q_local(c).wait()
        q_core(c).wait_recv()
        for r in range(1, ys):
            q_y(c, r).wait_recv()
            q_far(c, r).start()
        if c == 0:
            for i in range(3):
                hold(i).wait()
            issue(0)
            for i in range(3):
                s_local(i).start()
                s_core(i).start()
        elif c == 1:
            issue(1)
        else:
            issue(2)
        for r in range(1, ys):
            q_far(c, r).wait_recv()
        if c == 0:
            token(0).wait_recv()
            index = lax.broadcasted_iota(jnp.int32, (BLK, 1), 0)
            made[...] = jnp.where(
                index < starts[0, 0], theirs[0:BLK, :].astype(F32), mine[local - BLK : local, :].astype(F32)
            ).astype(BF16)

            @pl.when(s < 2)
            def _():
                pads[...] = made[...]

        project(parity * local, c)
        if c == 0:

            @pl.when(s == 1)
            def _():
                remote(made, pads, pad_s.at[0], pad_r.at[0], peer("seq", 3)).start()

    w_store = pltpu.make_async_copy(w, w_out, out_l.at[0])
    w_store.start()
    forward_pads = remote(pads, pads, pad_s.at[1], pad_r.at[1], mate)

    @pl.when(s == 2)
    def _():
        remote(made, pads, pad_s.at[0], pad_r.at[0], peer("seq", 3)).wait_recv()
        forward_pads.start()

    away = (1 - parity) * local
    normalise_rows(theirs, away, (0, BLK // 128))
    came_y(0)
    token(1).wait_recv()
    normalise_rows(theirs, away, (BLK // 128, local // 128))
    for c in range(3):
        project(away, c)
    stores = [
        pltpu.make_async_copy(a, b, out_l.at[1 + i])
        for i, (a, b) in enumerate(((q, q_out), (k, k_out), (v, v_out), (n_t, n_out), (theirs, tok_out)))
    ]
    for copy in stores:
        copy.start()
    came_y(1)
    came_x(0)

    @pl.when(s == 3)
    def _():
        forward_pads.wait_recv()

    hat, _ = normalise(pads[...].astype(F32))
    value = (hat * gain + bias).astype(BF16)
    np_t[...] = value.T
    kp[...] = nn(value, w[:, half : 2 * half]).astype(BF16)
    vp[...] = nn(value, w[:, 2 * half :]).astype(BF16)
    late = [
        pltpu.make_async_copy(a, b, out_l.at[6 + i])
        for i, (a, b) in enumerate(((np_t, np_out), (kp, kp_out), (vp, vp_out), (pads, pad_out)))
    ]
    for copy in late:
        copy.start()
    came_y(2)
    came_x(1)

    def give(i):
        lanes = pl.ds(pl.multiple_of(i * 2 * HD, 128), 2 * HD)
        return remote(
            mixed.at[pl.ds(pl.multiple_of(away, 16), local), lanes], other.at[:, lanes], o_s.at[i], o_r.at[i], mate
        )

    pairs = half // (2 * HD)
    done_y, done_x = 3, 2
    for i in range(pairs):
        lanes = slice(i * 2 * HD, (i + 1) * 2 * HD)

        def put(at, value):
            mixed[at, lanes] = value

        def put_lse(h, at, value):
            lse[i, h : h + 1, at] = value

        attend_pair(
            bounds,
            lambda at: q[at, lanes],
            lambda at: k[at, lanes],
            lambda at: v[at, lanes],
            lambda at: kp[at, lanes],
            lambda at: vp[at, lanes],
            put,
            put_lse,
        )
        give(i).start()
        came_y(done_y)
        came_x(done_x)
        done_y, done_x = done_y + 1, done_x + 1
    last = [
        pltpu.make_async_copy(mixed, mix_out, out_l.at[10]),
        pltpu.make_async_copy(lse, lse_out, out_l.at[11]),
        pltpu.make_async_copy(
            mixed.at[pl.ds(pl.multiple_of(parity * local, 16), local)], own_out, out_l.at[12]
        ),
    ]
    for copy in last:
        copy.start()
    for u in range(done_y, len(units)):
        came_y(u)
        came_x(u - 1)
    came_x(len(units) - 1)

    for i in range(pairs):
        give(i).wait()
    for i in range(3):
        s_local(i).wait()
        s_core(i).wait()
    for u in range(len(units)):
        for r in range(1, ys):
            w_y(u, r).wait_send()
            w_fy(u, r).wait()
            for t in range(1, dp):
                w_x(u, r, t).wait_send()
                w_fx(u, r, t).wait()
    for c in range(3):
        q_core(c).wait_send()
        for r in range(1, ys):
            q_y(c, r).wait_send()
            q_far(c, r).wait_send()
    token(0).wait_send()
    token(1).wait_send()

    @pl.when(s == 1)
    def _():
        remote(made, pads, pad_s.at[0], pad_r.at[0], peer("seq", 3)).wait_send()

    @pl.when(s == 2)
    def _():
        forward_pads.wait_send()

    for copy in [w_store] + stores + late + last:
        copy.wait()


def front(caps, starts, tokens, wqkv, wo, wu, wd, gain, bias, fsdp, dp):
    local, d = tokens.shape
    half, ff = d // 2, wu.shape[1]
    pairs = half // (2 * HD)
    y, px, n = max(fsdp // 2 - 1, 1), max(dp - 1, 1), 9
    dma = pltpu.SemaphoreType.DMA
    outs = [((2 * local, half), BF16)] * 3 + [
        ((d, 2 * local), BF16),
        ((d, BLK), BF16),
        ((BLK, half), BF16),
        ((BLK, half), BF16),
        ((d, 3 * half), BF16),
        ((2 * local, half), BF16),
        ((local, half), BF16),
        ((pairs, 2, 2 * local), F32),
        ((local, half), BF16),
        ((local, d), BF16),
        ((BLK, d), BF16),
        ((d, d), BF16),
        ((d, ff), BF16),
        ((ff, d), BF16),
    ]
    buffers = [
        (local, d), (local, d), (BLK, d), (BLK, d), (d, 3 * half), (2 * local, d), (d, 2 * local), (d, BLK),
        (2 * local, half), (2 * local, half), (2 * local, half), (BLK, half), (BLK, half), (2 * local, half),
        wo.shape, wu.shape, wd.shape,
    ]
    sems = [(1,), (2,), (2,), (2,), (2,), (3,), (3,), (3,), (3, y), (3, y), (3, y), (3, y)]
    sems += [(3,)] * 4 + [(n, y)] * 2 + [(n, y, px)] * 2 + [(n, y)] * 2 + [(n, y, px)] * 2 + [(pairs,)] * 2 + [(13,)]
    return pl.pallas_call(
        functools.partial(front_body, fsdp=fsdp, dp=dp),
        in_specs=[pl.BlockSpec(memory_space=pltpu.SMEM)] * 2 + [hbm()] * 5 + [pl.BlockSpec(memory_space=pltpu.VMEM)] * 2,
        out_specs=[hbm()] * len(outs),
        out_shape=[shape(*o) for o in outs],
        scratch_shapes=[pltpu.VMEM(b, BF16) for b in buffers]
        + [pltpu.VMEM((pairs, 2, 2 * local), F32)]
        + [dma(s) for s in sems],
        compiler_params=pltpu.CompilerParams(vmem_limit_bytes=VMEM_LIMIT, collective_id=1, has_side_effects=True),
        cost_estimate=pl.CostEstimate(flops=10**10, bytes_accessed=10**8, transcendentals=0),
    )(caps, starts, tokens, wqkv, wo, wu, wd, gain, bias)


def forward_body(
    own, other, x, up, gains, biases, wo, wu, wd, out, g_feed, act_t, slope, n_t, branch, middle, edges, normed, feed
):
    parity = lax.axis_index("seq") % 2
    step, last = pl.program_id(0), pl.num_programs(0) - 1
    half = own.shape[1]
    blocks = x.shape[0] // 128

    @pl.when(step == 0)
    def _():
        w_own = wo[pl.ds(pl.multiple_of(parity * half, 128), half), :]
        w_other = wo[pl.ds(pl.multiple_of((1 - parity) * half, 128), half), :]
        branch[...] = nn(own[...], w_own) + nn(other[...], w_other)

        def rows(i, carry):
            at = pl.ds(pl.multiple_of(i * 128, 128), 128)
            hat, _ = normalise(branch[at, :])
            mid = x[at, :].astype(F32) + hat * gains[1:2, :] + biases[1:2, :]
            middle[at, :] = mid
            hat, _ = normalise(mid)
            two = (hat * gains[2:3, :] + biases[2:3, :]).astype(BF16)
            normed[at, :] = two
            n_t[:, at] = two.T
            return carry

        lax.fori_loop(0, blocks, rows, 0)
        feed[...] = jnp.zeros_like(feed)

    u = nn(normed[...], wu[...])
    th = jnp.tanh(0.7978845608 * (u + 0.044715 * (u * u * u)))
    act = (0.5 * u * (1.0 + th)).astype(BF16)
    slope[...] = (
        0.5 * (1.0 + th) + 0.5 * u * (1.0 - th * th) * (0.7978845608 + (3 * 0.044715 * 0.7978845608) * (u * u))
    ).astype(BF16)
    act_t[...] = act.T
    feed[...] += nn(act, wd[...])

    @pl.when(step == last)
    def _():
        def rows(i, carry):
            at = pl.ds(pl.multiple_of(i * 128, 128), 128)
            g = up[at, :].astype(F32)
            hat, rstd = normalise(feed[at, :])
            gain = gains[3:4, :]
            out[at, :] = (middle[at, :] + hat * gain + biases[3:4, :]).astype(BF16)
            g_feed[at, :] = norm_back(g, hat, rstd, gain).astype(BF16)
            return (
                carry[0] + jnp.sum(g * hat, axis=0, keepdims=True),
                carry[1] + jnp.sum(g, axis=0, keepdims=True),
            )

        zero = jnp.zeros((1, x.shape[1]), F32)
        a, b = lax.fori_loop(0, blocks, rows, (zero, zero))
        edges[0:1, :] = a
        edges[1:2, :] = b


def forward(mixed, other, x, up, gains, biases, wo, wu, wd):
    local, d = x.shape
    half, ff = mixed.shape[1], wu.shape[1]
    tile = 1024
    once = lambda s: pl.BlockSpec(s, lambda *_: (0,) * len(s), pipeline_mode=pl.Buffered(1))
    return call(
        forward_body,
        (ff // tile,),
        0,
        [
            once(mixed.shape),
            once(other.shape),
            once(x.shape),
            once(up.shape),
            once(gains.shape),
            once(biases.shape),
            once(wo.shape),
            pl.BlockSpec((d, tile), lambda i: (0, i)),
            pl.BlockSpec((tile, d), lambda i: (i, 0)),
        ],
        [
            full((local, d)),
            full((local, d)),
            pl.BlockSpec((tile, local), lambda i: (i, 0)),
            pl.BlockSpec((local, tile), lambda i: (0, i)),
            full((d, local)),
            full((local, d)),
            full((local, d)),
            full((2, d)),
        ],
        [
            shape((local, d), BF16),
            shape((local, d), BF16),
            shape((ff, local), BF16),
            shape((local, ff), BF16),
            shape((d, local), BF16),
            shape((local, d), F32),
            shape((local, d), F32),
            shape((2, d), F32),
        ],
        [pltpu.VMEM((local, d), BF16), pltpu.VMEM((local, d), F32)],
        flops=2 * local * d * (d + 2 * ff),
        moved=40e6,
    )(mixed, other, x, up, gains, biases, wo, wu, wd)


class Lane:
    @staticmethod
    def scratch(count, rows, cols, fsdp, dp, masks):
        y, x, z = max(fsdp // 2 - 1, 1), max(dp - 1, 1), len(masks)
        dma = pltpu.SemaphoreType.DMA
        sems = [(count,)] * 2 + [(count, y)] * 2 + [(count, x)] * 2 + [(count, z)] * 4 + [(count, x)] * 2 + [(count,)] * 3
        return (
            [
                pltpu.VMEM((count, fsdp // 2, rows, cols), BF16),
                pltpu.VMEM((count, y, rows, cols), BF16),
                pltpu.VMEM((count, x, rows // dp, cols), BF16),
            ]
            + [pltpu.VMEM((count, rows // dp, cols >> (i + 1)), BF16) for i in range(z)]
            + [dma(s) for s in sems]
        )

    @staticmethod
    def size(masks):
        return 3 + len(masks) + 15

    def __init__(self, refs, final, fsdp, dp, masks, both=None):
        z = len(masks)
        self.acc, self.y_in, self.x_in = refs[:3]
        self.z_in = refs[3 : 3 + z]
        names = ("core_s", "core_r", "y_s", "y_r", "x_s", "x_r", "z_s", "z_r", "zz_s", "zz_r", "xx_s", "xx_r", "own")
        names += ("pair_s", "pair_r")
        self.both = both
        self.sems = dict(zip(names, refs[3 + z :]))
        self.final = final
        self.ys, self.dp, self.masks = fsdp // 2, dp, masks
        self.count, _, self.rows, self.cols = self.acc.shape
        self.x = lax.axis_index("dp")
        s = lax.axis_index("seq")
        self.bits = [s // m % 2 for m in masks]
        self.stages = [self.from_y, self.from_x]
        self.stages += [functools.partial(self.from_z, i) for i in range(z)]
        self.stages += [functools.partial(self.back_from_z, i) for i in reversed(range(z))]
        self.stages += [self.from_pair] if both is not None else []
        self.stages += [self.back_from_x]

    def place(self, level, away=False):
        at = 0
        for i in range(level):
            bit = self.bits[i]
            if away and i == level - 1:
                bit = 1 - bit
            at = at + bit * (self.cols >> (i + 1))
        if level == 0:
            return pl.ds(0, self.cols)
        return pl.ds(pl.multiple_of(at, 128), self.cols >> level)

    def band(self, mask=0):
        n = self.rows // self.dp
        return pl.ds(pl.multiple_of((self.x ^ mask) * n, 16), n)

    def core(self, u, src):
        return remote(src, self.acc.at[u], self.sems["core_s"].at[u], self.sems["core_r"].at[u], peer("fsdp", 1))

    def over_y(self, u, ry):
        s = self.sems
        return remote(
            self.acc.at[u, ry], self.y_in.at[u, ry - 1], s["y_s"].at[u, ry - 1], s["y_r"].at[u, ry - 1], peer("fsdp", 2 * ry)
        )

    def over_x(self, u, rx):
        s = self.sems
        return remote(
            self.acc.at[u, 0, self.band(rx)],
            self.x_in.at[u, rx - 1],
            s["x_s"].at[u, rx - 1],
            s["x_r"].at[u, rx - 1],
            peer("dp", rx),
        )

    def over_z(self, u, i):
        s = self.sems
        return remote(
            self.acc.at[u, 0, self.band(), self.place(i + 1, True)],
            self.z_in[i].at[u],
            s["z_s"].at[u, i],
            s["z_r"].at[u, i],
            peer("seq", self.masks[i]),
        )

    def back_z(self, u, i):
        s = self.sems
        at = self.final.at[u, self.band(), self.place(i + 1)]
        last = i == len(self.masks) - 1
        src = self.acc.at[u, 0, self.band(), self.place(i + 1)] if last else at
        return remote(src, at, s["zz_s"].at[u, i], s["zz_r"].at[u, i], peer("seq", self.masks[i]))

    def back_x(self, u, rx):
        s = self.sems
        at = self.final.at[u, self.band()] if self.both is None else self.both.at[:, u, self.band()]
        return remote(at, at, s["xx_s"].at[u, rx - 1], s["xx_r"].at[u, rx - 1], peer("dp", rx))

    def keep(self, u):
        at = self.place(len(self.masks))
        return pltpu.make_async_copy(
            self.acc.at[u, 0, self.band(), at], self.final.at[u, self.band(), at], self.sems["own"].at[u]
        )

    def add(self, target, sources):
        rows = target.shape[0]
        step = 64 if rows % 64 == 0 else 16

        def body(i, carry):
            at = pl.ds(pl.multiple_of(i * step, 16), step)
            total = target[at, :].astype(F32)
            for src in sources:
                total = total + src[at, :].astype(F32)
            target[at, :] = total.astype(BF16)
            return carry

        lax.fori_loop(0, rows // step, body, 0)

    def start_y(self, u):
        for ry in range(1, self.ys):
            self.over_y(u, ry).start()

    def from_y(self, u):
        for ry in range(1, self.ys):
            self.over_y(u, ry).wait_recv()
        self.add(self.acc.at[u, 0], [self.y_in.at[u, ry - 1] for ry in range(1, self.ys)])
        for rx in range(1, self.dp):
            self.over_x(u, rx).start()

    def from_x(self, u):
        for rx in range(1, self.dp):
            self.over_x(u, rx).wait_recv()
        self.add(self.acc.at[u, 0, self.band()], [self.x_in.at[u, rx - 1] for rx in range(1, self.dp)])
        self.over_z(u, 0).start()

    def from_z(self, i, u):
        self.over_z(u, i).wait_recv()
        self.add(self.acc.at[u, 0, self.band(), self.place(i + 1)], [self.z_in[i].at[u]])
        if i + 1 < len(self.masks):
            self.over_z(u, i + 1).start()
        else:
            self.keep(u).start()
            self.back_z(u, i).start()

    def back_from_z(self, i, u):
        if i == len(self.masks) - 1:
            self.keep(u).wait()
        self.back_z(u, i).wait_recv()
        if i:
            self.back_z(u, i - 1).start()
        elif self.both is not None:
            self.pair(u).start()
        else:
            for rx in range(1, self.dp):
                self.back_x(u, rx).start()

    def pair(self, u):
        at = self.final.at[u, self.band()]
        return remote(at, at, self.sems["pair_s"].at[u], self.sems["pair_r"].at[u], peer("seq", 1))

    def from_pair(self, u):
        self.pair(u).wait_recv()
        for rx in range(1, self.dp):
            self.back_x(u, rx).start()

    def back_from_x(self, u):
        for rx in range(1, self.dp):
            self.back_x(u, rx).wait_recv()

    def drain(self, u):
        for ry in range(1, self.ys):
            self.over_y(u, ry).wait_send()
        for rx in range(1, self.dp):
            self.over_x(u, rx).wait_send()
            self.back_x(u, rx).wait_send()
        for i in range(len(self.masks)):
            self.over_z(u, i).wait_send()
            self.back_z(u, i).wait_send()
        if self.both is not None:
            self.pair(u).wait_send()


def partners(fsdp, dp):
    return (
        [peer("fsdp", 1)]
        + [peer("fsdp", 2 * ry) for ry in range(1, fsdp // 2)]
        + [peer("dp", rx) for rx in range(1, dp)]
        + [peer("seq", m) for m in (1, 2, 3)]
    )


def doublings(fsdp, dp, seq):
    steps = []
    for axis, size in (("fsdp", fsdp), ("dp", dp), ("seq", seq)):
        m = 1
        while m < size:
            steps.append((axis, m))
            m *= 2
    return steps


def rear_body(
    caps, starts, act_t, g_feed, two_t, slope, wd, wu, wo, middle, branch, upstream, mixed_own, other,
    q, k, v, mixed, kp, vp, lse, w, n_t, np_t, tokens, theirs, padx, gains, edges3,
    final_a, final_b, grad_in, sums, g_mid,
    *rest, fsdp, dp, seq
):
    size_a, size_b = Lane.size((1, 2)), Lane.size((2,))
    a = Lane(rest[:size_a], final_a, fsdp, dp, (1, 2))
    rest = rest[size_a:]
    parity = lax.axis_index("seq") % 2
    b = Lane(rest[:size_b], final_b.at[parity], fsdp, dp, (2,), final_b)
    (
        ring, ring_b, do, dq, dk, dv, dkp, dvp, dk_sum, dv_sum, edges0,
        g_out, g_in, gp_out, gp_in, run, got, d_send, edges12,
        load, tiles_l, blocks_l, mid_s, d_s, d_r, gs_s, gs_r, gp_s, gp_r, e_s, e_r,
    ) = rest[size_b:]
    f, s = lax.axis_index("fsdp"), lax.axis_index("seq")
    local, d = tokens.shape
    half = d // 2
    ys = fsdp // 2
    rows = a.rows
    mate = peer("seq", 1)
    bounds = slot_bounds(caps, starts)
    greet(partners(fsdp, dp))

    my_rows = pl.ds(pl.multiple_of(parity * local, 128), local)
    give = remote(d_send, do.at[my_rows], d_s.at[0], d_r.at[0], mate)

    def shard(r):
        return r ^ f

    def band(r):
        return pl.ds(pl.multiple_of(shard(r) * rows, 16), rows)

    def give_and_take(c, first, make):
        @pl.when(c < PIECES)
        def _():
            u = first + c
            slot = ring.at[u % 4]
            if first:
                a.core(u - 4, slot).wait_send()
            for ry in range(ys):
                slot[ry] = make(c, 2 * ry + 1).astype(BF16)
            a.core(u, slot).start()

        @pl.when(c >= 1)
        def _():
            u = first + c - 1
            a.core(u, ring.at[u % 4]).wait_recv()
            for ry in range(ys):
                a.acc[u, ry] = (make(c - 1, 2 * ry) + a.acc[u, ry].astype(F32)).astype(BF16)

    def feed_phase(g_v, two_v, hid_v, gbr_v):
        common = [
            pltpu.make_async_copy(g_feed, g_v, load.at[0]),
            pltpu.make_async_copy(two_t, two_v, load.at[1]),
        ]

        def down_phase(act_v):
            def fetch(c):
                return pltpu.make_async_copy(act_t.at[:, c], act_v.at[c], load.at[2 + c])

            for copy in (common[0], fetch(0), fetch(1), common[1], fetch(2), fetch(3)):
                copy.start()
            common[0].wait()

            def step(c, carry):
                @pl.when(c < PIECES)
                def _():
                    fetch(c).wait()

                give_and_take(c, 0, lambda c, r: nn(act_v[c, shard(r)], g_v[...]))

                @pl.when((c >= 1) & (c <= 2))
                def _():
                    a.start_y(c - 1)

                return carry

            lax.fori_loop(0, PIECES + 1, step, 0)
            common[1].wait()

        def back_phase(g_two):
            count = 2 * fsdp
            wide = wd.shape[0] // count
            piece = wide // 2

            def tile_phase(wd_v, wu_v, slope_v):
                def fetch(j, slot):
                    at = pl.ds(pl.multiple_of(j * wide, 128), wide)
                    return [
                        pltpu.make_async_copy(wd.at[at], wd_v.at[slot], tiles_l.at[0, slot]),
                        pltpu.make_async_copy(slope.at[:, at], slope_v.at[slot], tiles_l.at[1, slot]),
                        pltpu.make_async_copy(wu.at[:, at], wu_v.at[slot], tiles_l.at[2, slot]),
                    ]

                for copy in fetch(0, 0):
                    copy.start()

                def step(j, carry):
                    slot = j % 2

                    @pl.when(j + 1 < count)
                    def _():
                        for copy in fetch(j + 1, 1 - slot):
                            copy.start()

                    for copy in fetch(j, slot):
                        copy.wait()
                    h = (nt(g_v[...], wd_v[slot]) * slope_v[slot].astype(F32)).astype(BF16)
                    at = pl.ds(pl.multiple_of(j // 2 * piece, 128), piece)
                    for i in range(2):
                        hid_v[j % 2 * 2 + i, :, at] = h[:, i * piece : (i + 1) * piece]
                    part = nt(h, wu_v[slot])

                    @pl.when(j == 0)
                    def _():
                        g_two[...] = part

                    @pl.when(j != 0)
                    def _():
                        g_two[...] += part

                    @pl.when(j == count // 2)
                    def _():
                        tick(0)

                    return carry

                lax.fori_loop(0, count, step, 0)

            pl.run_scoped(tile_phase, dt((2, wide, d)), dt((2, d, wide)), dt((2, local, wide)))

            def middle_phase(mid_v, br_v, up_v, gm_v, wo_v):
                load_wo = pltpu.make_async_copy(wo, wo_v, load.at[6])
                load_wo.start()

                def fetch(i, slot):
                    at = pl.ds(pl.multiple_of(i * 128, 128), 128)
                    return [
                        pltpu.make_async_copy(middle.at[at], mid_v.at[slot], blocks_l.at[0, slot]),
                        pltpu.make_async_copy(branch.at[at], br_v.at[slot], blocks_l.at[1, slot]),
                        pltpu.make_async_copy(upstream.at[at], up_v.at[slot], blocks_l.at[2, slot]),
                    ]

                def leave(i, slot):
                    at = pl.ds(pl.multiple_of(i * 128, 128), 128)
                    return pltpu.make_async_copy(gm_v.at[slot], g_mid.at[at], mid_s.at[slot])

                count = local // 128
                for copy in fetch(0, 0):
                    copy.start()
                edges12[...] = jnp.zeros_like(edges12)
                tick(1)

                def step(i, carry):
                    slot = i % 2

                    @pl.when(i + 1 < count)
                    def _():
                        for copy in fetch(i + 1, 1 - slot):
                            copy.start()

                    for copy in fetch(i, slot):
                        copy.wait()
                    at = pl.ds(pl.multiple_of(i * 128, 128), 128)
                    g = g_two[at, :]
                    hat, rstd = normalise(mid_v[slot])
                    edges12[2:3, :] += jnp.sum(g * hat, axis=0, keepdims=True)
                    edges12[3:4, :] += jnp.sum(g, axis=0, keepdims=True)
                    gm = up_v[slot].astype(F32) + norm_back(g, hat, rstd, gains[2:3, :])

                    @pl.when(i >= 2)
                    def _():
                        leave(i - 2, slot).wait()

                    gm_v[slot] = gm
                    leave(i, slot).start()
                    hat, rstd = normalise(br_v[slot])
                    edges12[0:1, :] += jnp.sum(gm * hat, axis=0, keepdims=True)
                    edges12[1:2, :] += jnp.sum(gm, axis=0, keepdims=True)
                    gbr_v[at, :] = norm_back(gm, hat, rstd, gains[1:2, :]).astype(BF16)
                    return carry

                lax.fori_loop(0, count, step, 0)
                load_wo.wait()
                grad = gbr_v[...]
                d_send[...] = nt(grad, wo_v[pl.ds(pl.multiple_of((1 - parity) * half, 128), half), :]).astype(BF16)
                give.start()
                do[my_rows, :] = nt(grad, wo_v[pl.ds(pl.multiple_of(parity * half, 128), half), :]).astype(BF16)
                for i in (count - 2, count - 1):
                    leave(i, i % 2).wait()

            pl.run_scoped(
                middle_phase,
                dt((2, 128, d), F32), dt((2, 128, d), F32), dt((2, 128, d)), dt((2, 128, d), F32), dt((d, d)),
            )

        def up_phase(att):
            attn = [
                pltpu.make_async_copy(
                    mixed_own, att.at[:, pl.ds(pl.multiple_of(parity * half, 128), half)], load.at[7]
                ),
                pltpu.make_async_copy(
                    other, att.at[:, pl.ds(pl.multiple_of((1 - parity) * half, 128), half)], load.at[8]
                ),
            ]
            for copy in attn:
                copy.start()

            def step(c, carry):
                give_and_take(c, PIECES, lambda c, r: nn(two_v[band(r), :], hid_v[c]))

                @pl.when(c == 1)
                def _():
                    tick(2)

                return carry

            lax.fori_loop(0, PIECES + 1, step, 0)
            u = 2 * PIECES
            slot = ring.at[u % 4]
            a.core(u - 4, slot).wait_send()
            for copy in attn:
                copy.wait()
            for ry in range(ys):
                slot[ry] = tn(att[:, band(2 * ry + 1)], gbr_v[...]).astype(BF16)
            a.core(u, slot).start()
            for ry in range(ys):
                held = tn(att[:, band(2 * ry)], gbr_v[...])
                if ry == 0:
                    a.core(u, slot).wait_recv()
                a.acc[u, ry] = (held + a.acc[u, ry].astype(F32)).astype(BF16)

        pl.run_scoped(down_phase, dt((PIECES, fsdp, rows, local)))
        pl.run_scoped(back_phase, dt((local, d), F32))
        pl.run_scoped(up_phase, dt((local, d)))

    def starts_of(lane, t):
        if lane is b:
            return (2,) if t == a.count - 1 else ()
        if t < 0 or t + 3 >= a.count:
            return ()
        return (t + 2,) if t < 3 else (t + 2, t + 3) if t == 3 else (t + 3,)

    def tick(t):
        for lane, first in ((a, 0), (b, a.count)):
            for k, stage in enumerate(lane.stages):
                u = t - k - first
                if isinstance(t, int):
                    if 0 <= u < lane.count:
                        stage(u)
                    if k == 0:
                        for other in starts_of(lane, t):
                            lane.start_y(other)
                elif lane is a:

                    @pl.when(u >= 0)
                    def _():
                        stage(u)

                    if k == 0:

                        @pl.when(u + 3 < lane.count)
                        def _():
                            lane.start_y(u + 3)

    first = remote(gp_out, gp_in, gp_s.at[0], gp_r.at[0], mate)
    second = remote(gp_out, gp_in, gp_s.at[0], gp_r.at[0], peer("seq", 3))
    third = remote(gp_in, gp_in, gp_s.at[0], gp_r.at[0], mate)

    def count_edges(g, x):
        hat, _ = normalise(x.astype(F32))
        return jnp.sum(g * hat, axis=0, keepdims=True), jnp.sum(g, axis=0, keepdims=True)

    def attention_phase(q_v, k_v, v_v, o_v, kp_v, vp_v, lse_v, wkv_v, px_v, dq_pad):
        pairs = ((q, q_v), (mixed, o_v), (kp, kp_v), (vp, vp_v), (lse, lse_v), (w.at[:, pl.ds(half, 2 * half)], wkv_v))
        pairs += ((padx, px_v), (k, k_v), (v, v_v))
        copies = [pltpu.make_async_copy(x, y, load.at[9 + i]) for i, (x, y) in enumerate(pairs)]
        for copy in copies:
            copy.start()
        tick(3)
        for copy in copies:
            copy.wait()
        give.wait_recv()

        def views(i):
            lanes = pl.ds(pl.multiple_of(i * 2 * HD, 128), 2 * HD)
            return (
                lanes,
                lambda at: q_v[at, lanes],
                lambda at: o_v[at, lanes],
                lambda h, at: lse_v[i, h : h + 1, at],
                lambda at: do[at, lanes],
            )

        def pad_step(i, carry):
            lanes, q_of, o_of, lse_of, do_of = views(i)

            def put_pad(n, value):
                dq_pad[n, :, lanes] = value

            gk, gv = attend_back_pads(bounds, q_of, kp_v[:, lanes], vp_v[:, lanes], o_of, lse_of, do_of, put_pad)
            dkp[:, lanes] = (gk * 0.125).astype(BF16)
            dvp[:, lanes] = gv.astype(BF16)
            return carry

        lax.fori_loop(0, half // (2 * HD), pad_step, 0)
        g = nt(dkp[...], wkv_v[:, 0:half]) + nt(dvp[...], wkv_v[:, half:])
        gp_out[...] = g.astype(BF16)

        @pl.when(s == 3)
        def _():
            first.start()

        one, two = count_edges(g, px_v[...])
        edges0[0:1, :] = one
        edges0[1:2, :] = two

        def step(i, carry):
            lanes, q_of, o_of, lse_of, do_of = views(i)

            def put(at, value):
                dq[at, lanes] = value

            attend_back_pair(
                bounds,
                q_of,
                lambda at: k_v[at, lanes],
                lambda at: v_v[at, lanes],
                o_of,
                lse_of,
                do_of,
                lambda n: dq_pad[n, :, lanes],
                put,
                dk_sum,
                dv_sum,
            )
            dk[:, lanes] = (dk_sum[...] * 0.125).astype(BF16)
            dv[:, lanes] = dv_sum[...].astype(BF16)
            tick(i + 4)

            @pl.when((s == 2) & (i == 1))
            def _():
                first.wait_recv()
                gp_out[...] = (gp_out[...].astype(F32) + gp_in[...].astype(F32)).astype(BF16)
                second.start()

            @pl.when((s == 1) & (i == 3))
            def _():
                second.wait_recv()
                third.start()

            return carry

        lax.fori_loop(0, half // (2 * HD), step, 0)

    steps = doublings(fsdp, dp, seq)

    def double(i):
        axis, m = steps[i]
        return remote(run.at[i], got.at[i], e_s.at[i], e_r.at[i], peer(axis, m))

    def double_start(i):
        double(i).start()

    def double_end(i):
        double(i).wait_recv()
        run[i + 1] = run[i] + got[i]

    def project_phase(w_v, nt_v, npt_v, x_v, y_v, mid_v, own, out_v):
        pairs = ((w, w_v), (theirs, y_v), (n_t, nt_v), (np_t, npt_v), (tokens, x_v), (g_mid, mid_v))
        copies = [pltpu.make_async_copy(x, y, load.at[18 + i]) for i, (x, y) in enumerate(pairs)]
        for copy in copies:
            copy.start()
        gain = gains[0:1, :]
        back_rows = (dq, dk, dv)
        back_pads = (None, dkp, dvp)

        def grad(c, r):
            total = nn(nt_v[band(r), :], back_rows[c][...])
            if c:
                total = total + nn(npt_v[band(r), :], back_pads[c][...])
            return total

        def weight(c):
            return w_v[:, c * half : (c + 1) * half]

        def through(first_row, source, store, edge):
            def body(i, carry):
                at = pl.ds(pl.multiple_of(first_row + i * 128, 128), 128)
                here = pl.ds(pl.multiple_of(i * 128, 128), 128)
                g = nt(dq[at, :], weight(0)) + nt(dk[at, :], weight(1)) + nt(dv[at, :], weight(2))
                store(i, here, g)
                one, two = count_edges(g, source[here, :])
                return carry[0] + one, carry[1] + two

            return lax.fori_loop(0, local // 128, body, edge)

        def pass_rows(i):
            at = pl.ds(pl.multiple_of(i * 128, 128), 128)
            return remote(g_out.at[at], g_in.at[at], gs_s.at[i], gs_r.at[i], mate)

        def store_out(i, at, value):
            g_out[at, :] = value.astype(BF16)

        def store_own(i, at, value):
            own[at, :] = value

        for copy in copies[:2]:
            copy.wait()
        edge = through((1 - parity) * local, y_v, store_out, (edges0[0:1, :], edges0[1:2, :]))
        for copy in copies[2:]:
            copy.wait()
        for c in range(3):
            for ry in range(ys):
                ring_b[c, ry] = grad(c, 2 * ry + 1).astype(BF16)
            b.core(c, ring_b.at[c]).start()
        for c in range(3):
            for ry in range(ys):
                held = grad(c, 2 * ry)
                if ry == 0:
                    b.core(c, ring_b.at[c]).wait_recv()
                b.acc[c, ry] = (held + b.acc[c, ry].astype(F32)).astype(BF16)
        b.start_y(0)
        b.start_y(1)
        tick(8)
        pass_rows(0).start()
        edge = through(parity * local, x_v, store_own, edge)
        order = (edge[0], edges12[0:1, :], edges12[2:3, :], edges3[0:1, :])
        order += (edge[1], edges12[1:2, :], edges12[3:4, :], edges3[1:2, :])
        for i, value in enumerate(order):
            run[0, i : i + 1, :] = value
        leave = pltpu.make_async_copy(out_v, grad_in, load.at[25])

        def finish_rows():
            for i in range(local // 128):
                pass_rows(i).wait_recv()

            @pl.when(s == 1)
            def _():
                third.wait_send()

            @pl.when(s == 0)
            def _():
                third.wait_recv()

            @pl.when(s == 2)
            def _():
                second.wait_send()

            @pl.when(s == 3)
            def _():
                first.wait_send()

            @pl.when(s < 2)
            def _():
                row = lax.broadcasted_iota(jnp.int32, (BLK, 1), 0)
                mine = ((s == 0) & (row < starts[0, 0])) | ((s == 1) & (row >= starts[0, 0] + caps[0, 0]))
                extra = jnp.where(mine, gp_in[...].astype(F32), 0.0)
                at = pl.ds(pl.multiple_of(jnp.where(s == 0, 0, local - BLK), 128), BLK)
                own[at, :] += extra

            def finish(i, carry):
                at = pl.ds(pl.multiple_of(i * 128, 128), 128)
                hat, rstd = normalise(x_v[at, :].astype(F32))
                g = own[at, :] + g_in[at, :].astype(F32)
                out_v[at, :] = (mid_v[at, :] + norm_back(g, hat, rstd, gain)).astype(BF16)
                return carry

            lax.fori_loop(0, local // 128, finish, 0)
            leave.start()

        double_start(0)
        end = max(a.count + len(a.stages), a.count + b.count + len(b.stages))
        pending = 0
        for t in range(9, end):
            tick(t)
            if t - 8 < local // 128:
                pass_rows(t - 8).start()
            if pending < len(steps):
                double_end(pending)
                pending += 1
                if pending < len(steps):
                    double_start(pending)
            if t == 15:
                finish_rows()
        for i in range(pending, len(steps)):
            double_end(i)
            if i + 1 < len(steps):
                double_start(i + 1)
        last = pltpu.make_async_copy(run.at[len(steps)], sums, load.at[24])
        last.start()

        for i in range(local // 128):
            pass_rows(i).wait_send()
        last.wait()
        leave.wait()

    dt = lambda s, t=BF16: pltpu.VMEM(s, t)
    pl.run_scoped(
        feed_phase,
        dt((local, d)),
        dt((d, local)),
        dt((PIECES, local, d)),
        dt((local, d)),
    )
    pl.run_scoped(
        attention_phase,
        dt(q.shape), dt(k.shape), dt(v.shape), dt(mixed.shape), dt(kp.shape), dt(vp.shape), dt(lse.shape, F32),
        dt((d, 2 * half)), dt(padx.shape), dt((2, BLK, half), F32),
    )
    pl.run_scoped(
        project_phase,
        dt(w.shape), dt(n_t.shape), dt(np_t.shape), dt(tokens.shape), dt(theirs.shape),
        dt(g_mid.shape, F32), dt((local, d), F32), dt((local, d)),
    )
    give.wait_send()
    for u in range(2 * PIECES - 3, 2 * PIECES + 1):
        a.core(u, ring.at[u % 4]).wait_send()
    for u in range(b.count):
        b.core(u, ring_b.at[u]).wait_send()
    for lane in (a, b):
        for u in range(lane.count):
            lane.drain(u)
    for i in range(len(steps)):
        double(i).wait_send()


def rear(caps, starts, arrays, small, sizes):
    fsdp, dp, seq = sizes
    local, d = arrays[1].shape
    half = d // 2
    rows, y = d // fsdp, fsdp // 2
    n = 2 * PIECES + 1
    steps = len(doublings(fsdp, dp, seq))
    dma = pltpu.SemaphoreType.DMA
    vm = pltpu.VMEM
    return pl.pallas_call(
        functools.partial(rear_body, fsdp=fsdp, dp=dp, seq=seq),
        in_specs=[pl.BlockSpec(memory_space=pltpu.SMEM)] * 2
        + [hbm()] * len(arrays)
        + [pl.BlockSpec(memory_space=pltpu.VMEM)] * len(small),
        out_specs=[hbm()] * 5,
        out_shape=[
            shape((n, rows, d), BF16),
            shape((2, 3, rows, half), BF16),
            shape((local, d), BF16),
            shape((8, d), F32),
            shape((local, d), F32),
        ],
        scratch_shapes=Lane.scratch(n, rows, d, fsdp, dp, (1, 2))
        + Lane.scratch(3, rows, half, fsdp, dp, (2,))
        + [vm((4, y, rows, d), BF16), vm((3, y, rows, half), BF16)]
        + [vm((2 * local, half), BF16)] * 4
        + [vm((BLK, half), BF16)] * 2
        + [vm((2 * local, 2 * HD), F32)] * 2
        + [vm((2, d), F32)]
        + [vm((local, d), BF16)] * 2
        + [vm((BLK, d), BF16)] * 2
        + [vm((steps + 1, 8, d), F32), vm((steps, 8, d), F32), vm((local, half), BF16), vm((4, d), F32)]
        + [dma((26,)), dma((3, 2)), dma((3, 2)), dma((2,)), dma((1,)), dma((1,))]
        + [dma((local // 128,))] * 2
        + [dma((1,))] * 2
        + [dma((steps,)), dma((steps,))],
        compiler_params=pltpu.CompilerParams(vmem_limit_bytes=VMEM_LIMIT, collective_id=0, has_side_effects=True),
        cost_estimate=pl.CostEstimate(flops=10**10, bytes_accessed=10**8, transcendentals=0),
    )(caps, starts, *arrays, *small)


def deliver_body(done, done_q, grad_in, sums, qkv, proj, up, down, out, gain, bias, a, b, c_in, s_in, wide, q_wide, load, sem):
    rows, d = a.shape[1:]
    half = b.shape[3]
    loads = [pltpu.make_async_copy(done.at[i], a.at[i], load.at[i]) for i in range(a.shape[0])]
    loads += [
        pltpu.make_async_copy(done_q, b, load.at[9]),
        pltpu.make_async_copy(grad_in, c_in, load.at[10]),
        pltpu.make_async_copy(sums, s_in, load.at[11]),
    ]
    for copy in loads:
        copy.start()
    stores = []

    def store(src, dst):
        copy = pltpu.make_async_copy(src, dst, sem.at[len(stores)])
        copy.start()
        stores.append(copy)

    shards = d // rows
    for i in range(a.shape[0]):
        loads[i].wait()
        wide[i] = a[i].astype(F32)
        if i == 2 * PIECES:
            store(wide.at[i], proj)
        elif i < PIECES:
            store(wide.at[i], down.at[pl.ds(i * rows, rows)])
        else:
            for h in range(shards):
                at = (h * PIECES + i - PIECES) * rows
                store(wide.at[i, :, pl.ds(h * rows, rows)], up.at[:, pl.ds(at, rows)])
    for copy in loads[a.shape[0] :]:
        copy.wait()
    for h in range(2):
        for i in range(3):
            q_wide[h, i] = b[h, i].astype(F32)
            store(q_wide.at[h, i], qkv.at[:, pl.ds((2 * i + h) * half, half)])
    store(c_in, out)
    gain[...] = s_in[0:4, :]
    bias[...] = s_in[4:8, :]
    for copy in stores:
        copy.wait()


def deliver(done, done_q, grad_in, sums, ff):
    n, rows, d = done.shape
    half = done_q.shape[3]
    count = PIECES + PIECES * (d // rows) + 1 + 6 + 1
    vm, dma = pltpu.VMEM, pltpu.SemaphoreType.DMA
    small = pl.BlockSpec(memory_space=pltpu.VMEM)
    return pl.pallas_call(
        deliver_body,
        in_specs=[hbm()] * 4,
        out_specs=[hbm()] * 5 + [small, small],
        out_shape=[
            shape((rows, 6 * half), F32),
            shape((rows, d), F32),
            shape((rows, ff), F32),
            shape((PIECES * rows, d), F32),
            shape(grad_in.shape, BF16),
            shape((4, d), F32),
            shape((4, d), F32),
        ],
        scratch_shapes=[
            vm(done.shape, BF16),
            vm(done_q.shape, BF16),
            vm(grad_in.shape, BF16),
            vm(sums.shape, F32),
            vm(done.shape, F32),
            vm(done_q.shape, F32),
            dma((12,)),
            dma((count,)),
        ],
        compiler_params=pltpu.CompilerParams(vmem_limit_bytes=VMEM_LIMIT),
        cost_estimate=pl.CostEstimate(flops=10**7, bytes_accessed=2 * 10**7, transcendentals=0),
    )(done, done_q, grad_in, sums)


def local(
    tokens, qkv_weight, out_weight, up_weight, down_weight, norm_gain, norm_bias, caption_len, item_start, grad_out
):
    x_tok, up = tokens[0], grad_out[0]
    local_rows, d = x_tok.shape
    fsdp, dp, seq = (lax.axis_size(axis) for axis in ("fsdp", "dp", "seq"))
    ff = up_weight.shape[1]
    (q, k, v, n_t, np_t, kp, vp, w_qkv, mixed, mixed_own, lse, other, theirs, pads, wo, wu, wd) = front(
        caption_len, item_start, x_tok, qkv_weight, out_weight, up_weight, down_weight, norm_gain, norm_bias, fsdp, dp
    )
    (out, g_feed, act_t, slope, two_t, branch, middle, edges3) = forward(
        mixed_own, other, x_tok, up, norm_gain, norm_bias, wo, wu, wd
    )
    done, done_q, grad_in, sums, _ = rear(
        caption_len,
        item_start,
        (
            act_t.reshape(fsdp, PIECES, d // fsdp, local_rows), g_feed, two_t, slope, wd, wu, wo,
            middle, branch, up, mixed_own, other, q, k, v, mixed, kp, vp, lse, w_qkv, n_t, np_t, x_tok, theirs, pads,
        ),
        (norm_gain, edges3),
        (fsdp, dp, seq),
    )
    grad_qkv, grad_proj, grad_up, grad_down, grad_in, grad_gain, grad_bias = deliver(done, done_q, grad_in, sums, ff)
    return (out[None], grad_in[None], grad_qkv, grad_proj, grad_up, grad_down, grad_gain, grad_bias)


def solution(mesh):
    rows = P(("fsdp", "dp"), "seq", None)
    shard = P("fsdp", None)
    items = P(("fsdp", "dp"), None)
    return jax.shard_map(
        local,
        mesh=mesh,
        in_specs=(rows, shard, shard, shard, shard, P(), P(), items, items, rows),
        out_specs=(rows, rows, shard, shard, shard, shard, P(), P()),
        check_vma=False,
    )
```
